32 devices in a mesh: parts: 2 (over y), mp: 4 (over z), shot: 4 (over x, core).
Axes of the slice: x: 2, y: 2, z: 4, core: 2. Of those that a mesh axis runs over, the one named last changes fastest.
Arguments:
- courant: float32 [192, 256, 128], P(('parts', 'mp')), parts along dimension 0, may hold values from 0.04 to 0.2
- forward_old: float32 [8, 96, 256, 128], P(('parts', 'shot'), 'mp'), parts along dimension 0, may hold values from -5 to 5
- forward_now: float32 [8, 96, 256, 128], P(('parts', 'shot'), 'mp'), parts along dimension 0, may hold values from -5 to 5
- adjoint_late: float32 [8, 96, 256, 128], P(('parts', 'shot'), 'mp'), parts along dimension 0, may hold values from -5 to 5
- adjoint_now: float32 [8, 96, 256, 128], P(('parts', 'shot'), 'mp'), parts along dimension 0, may hold values from -5 to 5
- src_cell: int32 [8, 64], P(('parts', 'shot')), parts along dimension 0, may hold values from 0 to 3145727
- src_sign: int32 [8, 64], P(('parts', 'shot')), parts along dimension 0, may hold values from 0 to 1
- wavelet: float32 [8, 2, 64], P(('parts', 'shot')), parts along dimension 0, may hold values from -16 to 16
- rec_cell: int32 [4096], P('parts'), parts along dimension 0, may hold values from 0 to 3145727
- rec_data: float32 [8, 2, 2048], P(('parts', 'shot')), parts along dimension 0, may hold values from -16 to 16
Outputs:
- raw_gradient: float32 [192, 256, 128], P(('parts', 'mp'), 'shot'), parts along dimension 0
- smooth_gradient: float32 [192, 256, 128], P(('parts', 'shot'), None, 'mp'), parts along dimension 0
The draws below stay inside these ranges and needn't reach their ends.
There are 2 independent parts, one for each index of `parts`. The reference program is written for one: setup_inputs(seed, part) draws one part's arguments, and reference() takes and returns one part's arrays. A program takes and returns all parts, laid end to end along the dimension named above; each array names one. Nothing has to cross between parts.
All inputs are finite; a program needn't handle non-finite values.
Results may differ from the reference program's by a relative error of at most 0.00025.
Values sent between devices are 32-bit elements; how exact they have to be, the bound alone decides.
No kernel may reach another device: no remote copies, remote signals or barrier semaphores. Data moves between devices by JAX's collectives and lax.ppermute only.
A program may use at most 128 MiB of HBM per device.

```python
import math
import jax
import jax.numpy as jnp
from jax import lax

NY = 256
NZ = 128
NSRC = 64
NREC = 2048
SMOOTH_X = 32
SMOOTH_YZ = 4
NX = 96
SHOTS = 4


def set_ends(array, own_key, low, top_value):
    place = [jax.random.randint(jax.random.fold_in(own_key, axis), (), 0, length) for axis, length in enumerate(array.shape)]
    widest = array.shape.index(max(array.shape))
    next_to = place[:widest] + [(place[widest] + 1) % array.shape[widest]] + place[widest + 1:]
    return array.at[tuple(place)].set(low).at[tuple(next_to)].set(top_value)


def steps_of(rng, shape, split, low, high):
    level, own = 1.0, jax.random.fold_in(rng, 6)
    for dim, blocks in split:
        steps = jnp.exp(jax.random.uniform(jax.random.fold_in(own, dim), (blocks,), jnp.float32, low / len(split), high / len(split)))
        level = level * jnp.repeat(steps, shape[dim] // blocks).reshape([-1 if axis == dim else 1 for axis in range(len(shape))])
    return level


def normal_values(own_key, dims, spread, most, shards=(), held_as=jnp.bfloat16):
    entries = jax.random.normal(own_key, dims, jnp.float32) * spread
    if len(shards) > 0:
        entries = steps_of(own_key, dims, shards, -0.22, 0.18) * entries
    return jnp.clip(entries, min=-most, max=most).astype(held_as)


def setup_inputs(seed: int = 0, part: int = 0) -> dict:
    seeds = jax.random.split(jax.random.key(seed), 11)
    own_keys = jax.random.split(jax.random.fold_in(seeds[10], part), 11)
    return {
        "courant": jnp.clip(jnp.exp(math.log(0.2) - 1.609438 * jax.random.uniform(own_keys[0], (NX, NY, NZ), jnp.float32) ** steps_of(own_keys[0], (NX, NY, NZ), ((0, 4),), -0.2, 0.2)), 0.04, 0.2),
        "forward_old": normal_values(own_keys[1], (SHOTS, NX, NY, NZ), 0.7, 5.0, ((0, 4), (1, 4)), jnp.float32),
        "forward_now": normal_values(own_keys[2], (SHOTS, NX, NY, NZ), 0.7, 5.0, ((0, 4), (1, 4)), jnp.float32),
        "adjoint_late": normal_values(own_keys[3], (SHOTS, NX, NY, NZ), 0.7, 5.0, ((0, 4), (1, 4)), jnp.float32),
        "adjoint_now": normal_values(own_keys[4], (SHOTS, NX, NY, NZ), 0.7, 5.0, ((0, 4), (1, 4)), jnp.float32),
        "src_cell": set_ends(jax.random.randint(own_keys[5], (SHOTS, NSRC), 0, NX * NY * NZ), jax.random.fold_in(own_keys[5], 1), 0, (NX * NY * NZ) - 1).astype(jnp.int32),
        "src_sign": set_ends(jax.random.randint(own_keys[6], (SHOTS, NSRC), 0, 2), jax.random.fold_in(own_keys[6], 1), 0, 1).astype(jnp.int32),
        "wavelet": normal_values(own_keys[7], (SHOTS, 2, NSRC), 4.0, 16.0, ((0, 4),), jnp.float32),
        "rec_cell": set_ends(jax.random.randint(own_keys[8], (NREC,), 0, NX * NY * NZ), jax.random.fold_in(own_keys[8], 1), 0, (NX * NY * NZ) - 1).astype(jnp.int32),
        "rec_data": normal_values(own_keys[9], (SHOTS, 2, NREC), 4.0, 16.0, ((0, 4),), jnp.float32),
    }


COEFS = (8.0 / 5.0, -1.0 / 5.0, 8.0 / 315.0, -1.0 / 560.0)
CENTER = -205.0 / 72.0

def laplace(padded):
    row_count = padded.shape[-3] - 8
    center_rows = padded[..., 4:4 + row_count, :, :]
    leading = ((0, 0),) * (padded.ndim - 3)
    padded_yz = jnp.pad(center_rows, leading + ((0, 0), (4, 4), (4, 4)))
    width_y = center_rows.shape[-2]
    width_z = center_rows.shape[-1]
    accum_sum = 3.0 * CENTER * center_rows
    for offset, weight in enumerate(COEFS):
        reach = offset + 1
        along_x = padded[..., 4 + reach:4 + reach + row_count, :, :] + padded[..., 4 - reach:4 - reach + row_count, :, :]
        along_y = padded_yz[..., :, 4 + reach:4 + reach + width_y, 4:4 + width_z] + padded_yz[..., :, 4 - reach:4 - reach + width_y, 4:4 + width_z]
        along_z = padded_yz[..., :, 4:4 + width_y, 4 + reach:4 + reach + width_z] + padded_yz[..., :, 4:4 + width_y, 4 - reach:4 - reach + width_z]
        accum_sum = accum_sum + weight * (along_x + along_y + along_z)
    return accum_sum

def inject(field, cells, values, first_row):
    plane_size = field.shape[-2] * field.shape[-1]
    local_cell = cells - first_row * plane_size
    valid = (local_cell >= 0) & (local_cell < field.size)
    target = jnp.where(valid, local_cell, field.size)
    return field.reshape(-1).at[target].add(values, mode='drop').reshape(field.shape)

def sine_table(length):
    counter = jnp.arange(length, dtype=jnp.int32) + 1
    product = counter[:, None] * counter[None, :] % (2 * (length + 1))
    return jnp.sin(jnp.pi * product.astype(jnp.float32) / (length + 1))

def response(length, strength):
    counter = jnp.arange(length, dtype=jnp.int32) + 1
    half_sine = jnp.sin(jnp.pi * counter.astype(jnp.float32) / (2 * (length + 1)))
    return 1.0 / (1.0 + strength * 4.0 * half_sine * half_sine)

def spread_scale(fx_resp, fy_resp, fz_resp):
    return 1.0 / jnp.sqrt(jnp.mean(fx_resp * fx_resp)) * (1.0 / jnp.sqrt(jnp.mean(fy_resp * fy_resp))) * (1.0 / jnp.sqrt(jnp.mean(fz_resp * fz_resp)))

def pad_rows(field):
    return jnp.pad(field, ((4, 4), (0, 0), (0, 0)))

def reference(courant, forward_old, forward_now, adjoint_late, adjoint_now, src_cell, src_sign, wavelet, rec_cell, rec_data):
    total_sum = jnp.zeros(courant.shape, jnp.float32)
    for group in range(SHOTS):
        signed = (2 * src_sign[group] - 1).astype(jnp.float32)
        now_fwd = forward_now[group]
        now_adj = adjoint_now[group]
        accel_first = inject(courant * laplace(pad_rows(now_fwd)), src_cell[group], signed * wavelet[group, 0], 0)
        next_fwd = 2.0 * now_fwd - forward_old[group] + accel_first
        accel_second = inject(courant * laplace(pad_rows(next_fwd)), src_cell[group], signed * wavelet[group, 1], 0)
        mid_adj = 2.0 * now_adj - adjoint_late[group] + inject(courant * laplace(pad_rows(now_adj)), rec_cell, rec_data[group, 0], 0)
        first_adj = 2.0 * mid_adj - now_adj + inject(courant * laplace(pad_rows(mid_adj)), rec_cell, rec_data[group, 1], 0)
        total_sum = total_sum + (first_adj * accel_first + mid_adj * accel_second)
    raw_gradient = total_sum / SHOTS
    highest = lax.Precision.HIGHEST
    table_x = sine_table(NX)
    table_y = sine_table(NY)
    table_z = sine_table(NZ)
    fx_resp = response(NX, float(SMOOTH_X * SMOOTH_X))
    fy_resp = response(NY, float(SMOOTH_YZ * SMOOTH_YZ))
    fz_resp = response(NZ, float(SMOOTH_YZ * SMOOTH_YZ))
    spectrum = jnp.einsum('ia,abc->ibc', table_x, raw_gradient, precision=highest)
    spectrum = jnp.einsum('jb,ibc->ijc', table_y, spectrum, precision=highest)
    spectrum = jnp.einsum('kc,ijc->ijk', table_z, spectrum, precision=highest)
    spectrum = spectrum * (fx_resp[:, None, None] * fy_resp[None, :, None] * fz_resp[None, None, :])
    spectrum = jnp.einsum('ia,abc->ibc', table_x, spectrum, precision=highest)
    spectrum = jnp.einsum('jb,ibc->ijc', table_y, spectrum, precision=highest)
    spectrum = jnp.einsum('kc,ijc->ijk', table_z, spectrum, precision=highest)
    factor = 2.0 / (NX + 1) * (2.0 / (NY + 1)) * (2.0 / (NZ + 1))
    smooth_gradient = spectrum * (factor * spread_scale(fx_resp, fy_resp, fz_resp))
    return (raw_gradient, smooth_gradient)
```

```python
import functools
import math

import jax
import jax.numpy as jnp
import ml_dtypes
import numpy as np
from jax import lax
from jax.experimental import pallas as pl
from jax.experimental.pallas import tpu as pltpu
from jax.sharding import PartitionSpec as P

SMOOTH_X = 32
SMOOTH_YZ = 4

COEFS = (8.0 / 5.0, -1.0 / 5.0, 8.0 / 315.0, -1.0 / 560.0)
CENTER = -205.0 / 72.0
REACH = len(COEFS)
SCALE = 5040.0
WHOLE = tuple(float(round(SCALE * a)) for a in COEFS)

LANES = 128
BF16 = jnp.bfloat16
F32 = jnp.float32
ANY = pl.BlockSpec(memory_space=pl.ANY)
VMEM = pl.BlockSpec(memory_space=pltpu.VMEM)
SMEM = pl.BlockSpec(memory_space=pltpu.SMEM)
PARAMS = pltpu.CompilerParams(vmem_limit_bytes=56 * 1024 * 1024)


def band(length):
    table = np.zeros((length, length), np.float32)
    for k, weight in enumerate(WHOLE, 1):
        near = np.arange(length - k)
        table[near, near + k] = weight
        table[near + k, near] = weight
    return table


def response(length, strength):
    counter = np.arange(1, length + 1, dtype=np.float64)
    half_sine = np.sin(np.pi * counter / (2 * (length + 1)))
    return 1.0 / (1.0 + strength * 4.0 * half_sine * half_sine)


def filter_matrix(length, strength):
    counter = np.arange(1, length + 1, dtype=np.float64)
    table = np.sin(np.pi * counter[:, None] * counter[None, :] / (length + 1))
    return 2.0 / (length + 1) * (table * response(length, strength)[None, :]) @ table


def scan_tables(length, strength, block):
    rate = math.acosh(1.0 + 0.5 / strength)
    index = np.arange(1, length + 1, dtype=np.float64)
    rise = np.sinh(rate * index)
    fall = np.sinh(rate * (length + 1 - index))
    whole = strength * math.sinh(rate) * math.sinh(rate * (length + 1))
    diag = rise * fall / whole
    left = np.concatenate([[0.0], rise[:-1] / rise[1:]])
    right = np.concatenate([fall[1:] / fall[:-1], [0.0]])
    first = (np.arange(length) // block) * block
    last = first + block - 1
    from_left = np.where(first > 0, rise[np.maximum(first - 1, 0)], 0.0) / rise
    from_right = np.where(last + 1 < length, fall[np.minimum(last + 1, length - 1)], 0.0) / fall
    rows = np.stack([diag, left, right, diag * from_left, diag * from_right])
    blocks = length // block
    carry = np.zeros((blocks, blocks))
    for here in range(blocks):
        for there in range(blocks):
            if there < here:
                carry[here, there] = rise[there * block + block - 1] / rise[here * block - 1]
            elif there > here:
                carry[here, there] = fall[there * block] / fall[here * block + block]
    return rows.astype(np.float32), carry.astype(np.float32)


def split_table(table):
    high = table.astype(np.float32).astype(ml_dtypes.bfloat16)
    low = (table - high.astype(np.float64)).astype(np.float32).astype(ml_dtypes.bfloat16)
    return jnp.asarray(high), jnp.asarray(low)


def split(value):
    high = value.astype(BF16)
    low = (value - high.astype(F32)).astype(BF16)
    return high, low


def dot(a, b):
    return jnp.dot(a, b, preferred_element_type=F32)


def dot_t(a, b):
    return lax.dot_general(a, b, (((1,), (1,)), ((), ())), preferred_element_type=F32)


def laplace_plane(pad, p, band_y, band_z):
    here = pad[p + REACH]
    width = here.shape[1]
    both = jnp.concatenate(split(here), axis=1)
    along_y = dot(band_y[...], both)
    along_z = dot(both, band_z[...])
    total = (3.0 * SCALE * CENTER) * here
    for k, weight in enumerate(WHOLE, 1):
        total += weight * (pad[p + REACH + k] + pad[p + REACH - k])
    return total + (along_y[:, :width] + along_y[:, width:]) + along_z


def divmod_fixed(value, size):
    if size & (size - 1) == 0:
        return lax.shift_right_logical(value, size.bit_length() - 1), value & (size - 1)
    return lax.div(value, size), lax.rem(value, size)


def step_one_kernel(
    first_ref, src_cell, src_sign, wavelet, rec_cell, rec_data,
    courant, f_old, f_now, a_late, a_now, band_y, band_z,
    accel_out, next_out, mid_out, src_out, rec_out,
    f_pad, a_pad, c_buf, f_buf, a_buf, acc_buf, s_first, r_first, s_second, r_second,
    found, place, sems, out_sems,
):
    rows, ny, nz = courant.shape
    inside = pl.ds(REACH, rows)
    loads = [
        pltpu.make_async_copy(f_now, f_pad.at[inside], sems.at[0]),
        pltpu.make_async_copy(courant, c_buf, sems.at[1]),
        pltpu.make_async_copy(f_old, f_buf, sems.at[2]),
        pltpu.make_async_copy(a_now, a_pad.at[inside], sems.at[3]),
        pltpu.make_async_copy(a_late, a_buf, sems.at[4]),
    ]
    for load in loads:
        load.start()
    edge = jnp.zeros((REACH, ny, nz), F32)
    for pad in (f_pad, a_pad):
        pad[:REACH] = edge
        pad[REACH + rows :] = edge

    tiles = rows * ny // 8
    group = ny // 8

    def clear(p, _):
        blank = jnp.zeros((group, 8, nz), F32)
        for ref in (s_first, r_first, s_second, r_second):
            ref[pl.ds(p * group, group)] = blank
        return 0

    lax.fori_loop(0, rows, clear, 0)

    start = first_ref[0]
    size = rows * ny * nz
    flat = lax.broadcasted_iota(jnp.int32, (8, nz), 0) * nz + lax.broadcasted_iota(jnp.int32, (8, nz), 1)

    def put(refs, local, values):
        tile, within = divmod_fixed(local, 8 * nz)
        spot = flat == within
        for ref, value in zip(refs, values, strict=True):
            ref[tile] = ref[tile] + jnp.where(spot, value, 0.0)

    nsrc = src_cell.shape[1]

    def one_source(i, _):
        local = src_cell[0, i] - start
        mine = (local >= 0) & (local < size)
        local = jnp.where(mine, local, 0)
        sign = jnp.where(mine, (2 * src_sign[0, i] - 1).astype(F32), 0.0)
        put((s_first, s_second), local, (sign * wavelet[0, 0, i], sign * wavelet[0, 1, i]))
        return 0

    lax.fori_loop(0, nsrc, one_source, 0, unroll=8 if nsrc % 8 == 0 else 1)

    nrec = rec_cell.shape[0]

    def look(j, count):
        local = rec_cell[j] - start
        mine = (local >= 0) & (local < size)
        found[count] = j
        place[count] = local
        return count + mine.astype(jnp.int32)

    count = lax.fori_loop(0, nrec, look, 0, unroll=16 if nrec % 16 == 0 else 1)

    def some_receivers(g, _):
        for e in range(8):
            i = g * 8 + e
            mine = i < count
            j = jnp.where(mine, found[i], 0)
            local = jnp.where(mine, place[i], 0)
            first = jnp.where(mine, rec_data[0, 0, j], 0.0)
            second = jnp.where(mine, rec_data[0, 1, j], 0.0)
            put((r_first, r_second), local, (first, second))
        return 0

    lax.fori_loop(0, (count + 7) // 8, some_receivers, 0)
    stores = [
        pltpu.make_async_copy(s_second, src_out, out_sems.at[0]),
        pltpu.make_async_copy(r_second, rec_out, out_sems.at[1]),
    ]
    for store in stores:
        store.start()

    for load in loads[:3]:
        load.wait()

    def forward(p, _):
        courant_here = c_buf[p] * (1.0 / SCALE)
        c_buf[p] = courant_here
        spike = s_first[pl.ds(p * group, group)].reshape(ny, nz)
        accel = courant_here * laplace_plane(f_pad, p, band_y, band_z) + spike
        acc_buf[p] = accel
        f_buf[p] = (2.0 * f_pad[p + REACH] - f_buf[p]) + accel
        return 0

    lax.fori_loop(0, rows, forward, 0)
    more = [
        pltpu.make_async_copy(acc_buf, accel_out, out_sems.at[2]),
        pltpu.make_async_copy(f_buf, next_out, out_sems.at[3]),
    ]
    for store in more:
        store.start()
    stores += more
    for load in loads[3:]:
        load.wait()

    def adjoint(p, _):
        spike = r_first[pl.ds(p * group, group)].reshape(ny, nz)
        change = c_buf[p] * laplace_plane(a_pad, p, band_y, band_z) + spike
        a_buf[p] = (2.0 * a_pad[p + REACH] - a_buf[p]) + change
        return 0

    lax.fori_loop(0, rows, adjoint, 0)
    last = pltpu.make_async_copy(a_buf, mid_out, out_sems.at[4])
    last.start()
    stores.append(last)
    for store in stores:
        store.wait()


def step_one(first, src_cell, src_sign, wavelet, rec_cell, rec_data, courant, f_old, f_now, a_late, a_now, bands):
    rows, ny, nz = courant.shape
    field = jax.ShapeDtypeStruct((rows, ny, nz), F32)
    spikes = jax.ShapeDtypeStruct((rows * ny // 8, 8, nz), F32)
    whole = pltpu.VMEM((rows, ny, nz), F32)
    padded = pltpu.VMEM((rows + 2 * REACH, ny, nz), F32)
    sparse = pltpu.VMEM((rows * ny // 8, 8, nz), F32)
    nrec = rec_cell.shape[0]
    return pl.pallas_call(
        step_one_kernel,
        out_shape=(field, field, field, spikes, spikes),
        in_specs=[SMEM] * 6 + [ANY] * 5 + [VMEM] * 2,
        out_specs=(ANY,) * 5,
        scratch_shapes=[
            padded, padded, whole, whole, whole, whole, sparse, sparse, sparse, sparse,
            pltpu.SMEM((nrec + 8,), jnp.int32),
            pltpu.SMEM((nrec + 8,), jnp.int32),
            pltpu.SemaphoreType.DMA((5,)),
            pltpu.SemaphoreType.DMA((5,)),
        ],
        compiler_params=PARAMS,
        cost_estimate=pl.CostEstimate(flops=10**10, bytes_accessed=40 * 2**20, transcendentals=0),
        name="step_one",
    )(first, src_cell, src_sign, wavelet, rec_cell, rec_data, courant, f_old, f_now, a_late, a_now, *bands)


def sides(first_ref, rows):
    even = first_ref[1] == 0
    high = rows - REACH
    return (jnp.where(even, high, 0), even), (jnp.where(even, 0, high), jnp.logical_not(even))


def halo_sum(halo, q, upper):
    total = None
    for k, weight in enumerate(COEFS, 1):
        if q + k >= REACH:
            h = q + k - REACH
            term = weight * halo[jnp.where(upper, h, REACH - 1 - h)]
            total = term if total is None else total + term
    return total


def correct_kernel(count, first_ref, *refs):
    courant, parts, halos = refs[0], refs[1 : 1 + count], refs[1 + count : 3 + count]
    outs = refs[3 + count : 3 + 3 * count]
    c_buf, bufs, sems, out_sems = refs[3 + 3 * count], refs[4 + 3 * count], refs[5 + 3 * count], refs[6 + 3 * count]
    rows = courant.shape[0]
    slots = sides(first_ref, rows)
    loads, stores = [], []
    for s, (base, _) in enumerate(slots):
        for i, ref in enumerate((courant, *parts)):
            target = c_buf.at[s] if i == 0 else bufs.at[i - 1, s]
            loads.append(pltpu.make_async_copy(ref.at[pl.ds(base, REACH)], target, sems.at[s, i]))
            loads[-1].start()
    for s, (_, upper) in enumerate(slots):
        for load in loads[s * (1 + count) : (s + 1) * (1 + count)]:
            load.wait()
        for q in range(REACH):
            here = jnp.where(upper, q, REACH - 1 - q)
            change = c_buf[s, here] * halo_sum(halos[s], q, upper)
            for i in range(count):
                bufs[i, s, here] = bufs[i, s, here] + change
        for i in range(count):
            stores.append(pltpu.make_async_copy(bufs.at[i, s], outs[2 * i + s], out_sems.at[i, s]))
            stores[-1].start()
    for store in stores:
        store.wait()


def correct(first, courant, parts, halos):
    _, ny, nz = courant.shape
    slot = jax.ShapeDtypeStruct((REACH, ny, nz), F32)
    count = len(parts)
    return pl.pallas_call(
        functools.partial(correct_kernel, count),
        out_shape=(slot,) * (2 * count),
        in_specs=[SMEM] + [ANY] * (1 + count) + [VMEM] * 2,
        out_specs=(ANY,) * (2 * count),
        scratch_shapes=[
            pltpu.VMEM((2, REACH, ny, nz), F32),
            pltpu.VMEM((count, 2, REACH, ny, nz), F32),
            pltpu.SemaphoreType.DMA((2, 1 + count)),
            pltpu.SemaphoreType.DMA((count, 2)),
        ],
        compiler_params=PARAMS,
        cost_estimate=pl.CostEstimate(flops=10**7, bytes_accessed=6 * 2**20, transcendentals=0),
        name="correct",
    )(first, courant, *parts, *halos)


def step_two_kernel(
    first_ref, courant, a_now, accel_in, next_in, mid_in, src_in, rec_in, f0, f1, c0, c1, m0, m1, band_y, band_z,
    send_out, keep_out, edge_out, by_f_out, by_a_out,
    f_pad, a_pad, c_buf, now_buf, acc_buf, s_buf, r_buf, gt_buf, edge_buf, by_f, by_a, sems, out_sems,
):
    rows, ny, nz = courant.shape
    slots = sides(first_ref, rows)
    bit = first_ref[2]
    middle = pl.ds(REACH, rows - 2 * REACH)
    group = ny // 8
    blocks = gt_buf.shape[1]
    loads = []

    def fetch(source, target):
        loads.append(pltpu.make_async_copy(source, target, sems.at[len(loads)]))
        loads[-1].start()

    for source, edges, target, offset in (
        (next_in, (f0, f1), f_pad, REACH),
        (mid_in, (m0, m1), a_pad, REACH),
        (accel_in, (c0, c1), acc_buf, 0),
    ):
        fetch(source.at[middle], target.at[pl.ds(REACH + offset, rows - 2 * REACH)])
        for (base, _), edge in zip(slots, edges, strict=True):
            fetch(edge, target.at[pl.ds(base + offset, REACH)])
    for source, target in ((courant, c_buf), (a_now, now_buf), (src_in, s_buf), (rec_in, r_buf)):
        fetch(source, target)
    blank = jnp.zeros((REACH, ny, nz), F32)
    for pad in (f_pad, a_pad):
        pad[:REACH] = blank
        pad[REACH + rows :] = blank
    for load in loads:
        load.wait()

    def plane(p, _):
        c = c_buf[p] * (1.0 / SCALE)
        spike_s = s_buf[pl.ds(p * group, group)].reshape(ny, nz)
        spike_r = r_buf[pl.ds(p * group, group)].reshape(ny, nz)
        mid = a_pad[p + REACH]
        accel = c * laplace_plane(f_pad, p, band_y, band_z) + spike_s
        first = (2.0 * mid - now_buf[p]) + (c * laplace_plane(a_pad, p, band_y, band_z) + spike_r)
        gt_buf[p] = (first * acc_buf[p] + mid * accel).reshape(blocks, ny // blocks, nz)
        return 0

    lax.fori_loop(0, rows, plane, 0)
    stores = []

    def put(source, target):
        stores.append(pltpu.make_async_copy(source, target, out_sems.at[len(stores)]))
        stores[-1].start()

    for j in range(blocks // 2):
        put(gt_buf.at[middle, 2 * j + 1 - bit], send_out.at[:, j])
        put(gt_buf.at[middle, 2 * j + bit], keep_out.at[:, j])
    for s, (base, _) in enumerate(slots):
        for q in range(REACH):
            c = c_buf[base + q]
            by_f[s, q] = c * a_pad[base + q + REACH]
            by_a[s, q] = c * acc_buf[base + q]
            edge_buf[s, q] = gt_buf[base + q].reshape(ny, nz)
    put(edge_buf, edge_out)
    put(by_f, by_f_out)
    put(by_a, by_a_out)
    for store in stores:
        store.wait()


def step_two(first, courant, a_now, accel, nxt, mid, src, rec, edges, bands, blocks):
    rows, ny, nz = courant.shape
    inner = rows - 2 * REACH
    half = jax.ShapeDtypeStruct((inner, blocks // 2, ny // blocks, nz), F32)
    edge = jax.ShapeDtypeStruct((2, REACH, ny, nz), F32)
    whole = pltpu.VMEM((rows, ny, nz), F32)
    padded = pltpu.VMEM((rows + 2 * REACH, ny, nz), F32)
    sparse = pltpu.VMEM((rows * ny // 8, 8, nz), F32)
    slot = pltpu.VMEM((2, REACH, ny, nz), F32)
    return pl.pallas_call(
        step_two_kernel,
        out_shape=(half, half, edge, edge, edge),
        in_specs=[SMEM] + [ANY] * 13 + [VMEM] * 2,
        out_specs=(ANY,) * 5,
        scratch_shapes=[
            padded, padded, whole, whole, whole, sparse, sparse,
            pltpu.VMEM((rows, blocks, ny // blocks, nz), F32),
            slot, slot, slot,
            pltpu.SemaphoreType.DMA((13,)),
            pltpu.SemaphoreType.DMA((blocks + 3,)),
        ],
        compiler_params=PARAMS,
        cost_estimate=pl.CostEstimate(flops=10**10, bytes_accessed=40 * 2**20, transcendentals=0),
        name="step_two",
    )(first, courant, a_now, accel, nxt, mid, src, rec, *edges, *bands)


def finish_kernel(first_ref, edge, by_f, by_a, f0, f1, a0, a1, send_out, keep_out, buf, out_sems):
    blocks = buf.shape[1]
    _, reach, ny, nz = edge.shape
    bit = first_ref[2]
    rows = first_ref[3]
    for s, (_, upper) in enumerate(sides(first_ref, rows)):
        f_halo, a_halo = (f0, f1)[s], (a0, a1)[s]
        for q in range(reach):
            here = jnp.where(upper, q, reach - 1 - q)
            total = edge[s, here] + by_f[s, here] * halo_sum(f_halo, q, upper)
            total += by_a[s, here] * halo_sum(a_halo, q, upper)
            buf[s * reach + here] = total.reshape(blocks, ny // blocks, nz)
    stores = []
    for j in range(blocks // 2):
        stores.append(pltpu.make_async_copy(buf.at[:, 2 * j + 1 - bit], send_out.at[:, j], out_sems.at[2 * j]))
        stores.append(pltpu.make_async_copy(buf.at[:, 2 * j + bit], keep_out.at[:, j], out_sems.at[2 * j + 1]))
    for store in stores:
        store.start()
    for store in stores:
        store.wait()


def finish(first, edge, by_f, by_a, f_halos, a_halos, blocks):
    _, reach, ny, nz = edge.shape
    half = jax.ShapeDtypeStruct((2 * reach, blocks // 2, ny // blocks, nz), F32)
    return pl.pallas_call(
        finish_kernel,
        out_shape=(half, half),
        in_specs=[SMEM] + [VMEM] * 7,
        out_specs=(ANY,) * 2,
        scratch_shapes=[
            pltpu.VMEM((2 * reach, blocks, ny // blocks, nz), F32),
            pltpu.SemaphoreType.DMA((blocks,)),
        ],
        compiler_params=PARAMS,
        cost_estimate=pl.CostEstimate(flops=10**7, bytes_accessed=7 * 2**20, transcendentals=0),
        name="finish",
    )(first, edge, by_f, by_a, *f_halos, *a_halos)


def depth_kernel(edge_chunk, pieces, ratio, first_ref, keep, got, z_high, z_low, *refs):
    if edge_chunk:
        refs = refs[1:]
    raw_out, outs, (raw_buf, spectrum, sem) = refs[0], refs[1 : 1 + pieces], refs[1 + pieces :]
    planes, yb, nz = raw_buf.shape
    shots = first_ref[4].astype(F32)
    raw_buf[...] = (keep[...] + got[...]).reshape(planes, yb, nz) / shots
    rows = raw_out.shape[0]
    stores = []
    if edge_chunk:
        for s, (base, _) in enumerate(sides(first_ref, rows)):
            stores.append(
                pltpu.make_async_copy(raw_buf.at[pl.ds(s * REACH, REACH)], raw_out.at[pl.ds(base, REACH)], sem.at[s])
            )
    else:
        stores.append(pltpu.make_async_copy(raw_buf, raw_out.at[pl.ds(REACH, planes)], sem.at[0]))
    for store in stores:
        store.start()
    lanes = LANES // yb
    count = planes // lanes
    zb = nz // pieces
    for p in range(count):
        rows_here = jnp.concatenate([raw_buf[h * count + p] for h in range(lanes)], axis=0)
        high, low = split(rows_here)
        table = z_high[...]
        spectrum[p] = (dot_t(table, high) + dot_t(table, low) + dot_t(z_low[...], high)).reshape(pieces, zb, LANES)
    offset = first_ref[5]
    for k, out in enumerate(outs):
        out[...] = spectrum[:, lax.rem(offset + k, pieces)]
    for store in stores:
        store.wait()


def depth(first, keep, got, tables, raw_shape, pieces, previous=None):
    planes, _, yb, nz = keep.shape
    lanes = LANES // yb
    count = planes // lanes
    piece = jax.ShapeDtypeStruct((count, nz // pieces, LANES), F32)
    edge_chunk = previous is not None
    return pl.pallas_call(
        functools.partial(depth_kernel, edge_chunk, pieces, None),
        out_shape=(jax.ShapeDtypeStruct(raw_shape, F32),) + (piece,) * pieces,
        in_specs=[SMEM] + [VMEM] * 4 + ([ANY] if edge_chunk else []),
        out_specs=(ANY,) + (VMEM,) * pieces,
        scratch_shapes=[
            pltpu.VMEM((planes, yb, nz), F32),
            pltpu.VMEM((count, pieces, nz // pieces, LANES), F32),
            pltpu.SemaphoreType.DMA((2,)),
        ],
        input_output_aliases={5: 0} if edge_chunk else {},
        compiler_params=PARAMS,
        cost_estimate=pl.CostEstimate(flops=10**8, bytes_accessed=2 * 2**20, transcendentals=0),
        name="depth",
    )(first, keep, got, *tables, *([previous] if edge_chunk else []))


def rows_kernel(pieces, ratio, shots, rows, first_ref, scan, *refs):
    mains, edges = refs[:pieces], refs[pieces : 2 * pieces]
    y_high, y_low = refs[2 * pieces : 2 * pieces + 2]
    out, sends = refs[2 * pieces + 2], refs[2 * pieces + 3 : 2 * pieces + 2 + shots]
    main_buf, edge_buf, field, ends, sems = refs[2 * pieces + 2 + shots :]
    shot, mp = first_ref[6], first_ref[7]
    total, zb, ny = field.shape
    yb = ny // shots
    lanes = LANES // yb
    loads = []
    for k in range(pieces):
        q = lax.rem(mp - k + pieces, pieces)
        source, sub = lax.div(q, ratio), lax.rem(q, ratio)
        loads.append(pltpu.make_async_copy(mains[k], main_buf.at[sub, source], sems.at[0, k]))
        loads.append(pltpu.make_async_copy(edges[k], edge_buf.at[sub, source], sems.at[1, k]))
    for load in loads:
        load.start()
    for load in loads:
        load.wait()
    lane = lax.broadcasted_iota(jnp.int32, (zb, LANES), 1)
    slot_of = lane // yb
    main_count, edge_count = mains[0].shape[0], edges[0].shape[0]
    for sub in range(ratio):
        even = lax.rem(shot * ratio + sub, 2) == 0
        base = (jnp.where(even, rows - REACH, 0), jnp.where(even, 0, rows - REACH))
        for buf, count in ((main_buf, main_count), (edge_buf, edge_count)):
            for p in range(count):
                for h in range(lanes):
                    chunk_plane = h * count + p
                    if buf is main_buf:
                        x = sub * rows + REACH + chunk_plane
                    else:
                        x = sub * rows + base[chunk_plane // REACH] + chunk_plane % REACH
                    for t in range(shots // lanes):
                        value = None
                        for e in range(lanes):
                            piece = buf[sub, t * lanes + e, p]
                            if e != h:
                                piece = pltpu.roll(piece, (e - h) * yb % LANES, 1)
                            value = piece if value is None else jnp.where(slot_of == e, piece, value)
                        field[x, :, pl.ds(t * LANES, LANES)] = value
    first_x = shot * total

    def up(x, carry):
        carry = field[x] + scan[1, first_x + x] * carry
        out[x] = carry
        return carry

    ends[0] = lax.fori_loop(0, total, up, jnp.zeros((zb, ny), F32))

    def down(i, carry):
        x = total - 1 - i
        both = (out[x] + carry) * scan[0, first_x + x]
        before = field[x] + carry
        out[x] = both
        return scan[2, jnp.maximum(first_x + x - 1, 0)] * before

    def down_all():
        carry = jnp.zeros((zb, ny), F32)
        carry = lax.fori_loop(0, total - 1, down, carry)
        out[0] = (out[0] + carry) * scan[0, first_x]
        return field[0] + carry

    ends[1] = down_all()
    high_t, low_t = y_high[...], y_low[...]

    step = max(1, 256 // zb)
    while total % step:
        step -= 1

    def across(i, _):
        block = out[pl.ds(i * step, step)].reshape(step * zb, ny)
        high, low = split(block)
        result = dot_t(high, high_t) + dot_t(low, high_t) + dot_t(high, low_t)
        out[pl.ds(i * step, step)] = result.reshape(step, zb, ny)
        return 0

    lax.fori_loop(0, total // step, across, 0)
    for j, send in enumerate(sends, 1):
        send[...] = jnp.where((shot ^ j) > shot, ends[0], ends[1])


def rows_filter(first, scan, mains, edges, tables, ratio, shots, rows):
    pieces = len(mains)
    main_count, zb, _ = mains[0].shape
    edge_count = edges[0].shape[0]
    ny = tables[0].shape[0]
    total = ratio * rows
    end = jax.ShapeDtypeStruct((zb, ny), F32)
    return pl.pallas_call(
        functools.partial(rows_kernel, pieces, ratio, shots, rows),
        out_shape=(jax.ShapeDtypeStruct((total, zb, ny), F32),) + (end,) * (shots - 1),
        in_specs=[SMEM] * 2 + [ANY] * (2 * pieces) + [VMEM] * 2,
        out_specs=(VMEM,) * shots,
        scratch_shapes=[
            pltpu.VMEM((ratio, shots, main_count, zb, LANES), F32),
            pltpu.VMEM((ratio, shots, edge_count, zb, LANES), F32),
            pltpu.VMEM((total, zb, ny), F32),
            pltpu.VMEM((2, zb, ny), F32),
            pltpu.SemaphoreType.DMA((2, pieces)),
        ],
        compiler_params=PARAMS,
        cost_estimate=pl.CostEstimate(flops=10**8, bytes_accessed=2 * 2**20, transcendentals=0),
        name="rows",
    )(first, scan, *mains, *edges, *tables)


def join_kernel(shots, first_ref, scan, carry, part, *refs):
    ends, (y_high, y_low, out) = refs[: shots - 1], refs[shots - 1 :]
    total, zb, ny = part.shape
    shot = first_ref[6]
    first_x = shot * total
    below = jnp.zeros((zb, ny), F32)
    above = jnp.zeros((zb, ny), F32)
    for j, end in enumerate(ends, 1):
        other = shot ^ j
        term = carry[shot, other] * end[...]
        below += jnp.where(other < shot, term, 0.0)
        above += jnp.where(other > shot, term, 0.0)
    high, low = split(jnp.concatenate([below, above], axis=0))
    both = dot_t(high, y_high[...]) + dot_t(low, y_high[...]) + dot_t(high, y_low[...])
    below, above = both[:zb], both[zb:]
    for x in range(total):
        value = part[x] + scan[3, first_x + x] * below + scan[4, first_x + x] * above
        out[x] = value.T


def join(first, scan, carry, part, ends, tables):
    total, zb, ny = part.shape
    shots = len(ends) + 1
    return pl.pallas_call(
        functools.partial(join_kernel, shots),
        out_shape=jax.ShapeDtypeStruct((total, ny, zb), F32),
        in_specs=[SMEM] * 3 + [VMEM] * (shots + 2),
        out_specs=VMEM,
        compiler_params=PARAMS,
        cost_estimate=pl.CostEstimate(flops=10**8, bytes_accessed=2 * 2**20, transcendentals=0),
        name="join",
    )(first, scan, carry, part, *ends, *tables)


def neighbours(count, start):
    low = range(start, count - 1, 2)
    return [(i, i + 1) for i in low] + [(i + 1, i) for i in low]


def swap(values):
    count = lax.axis_size("mp")
    return tuple(lax.ppermute(v, "mp", neighbours(count, start)) for start, v in enumerate(values))


def boundary(field, even):
    high = field.shape[0] - REACH
    return tuple(
        lax.dynamic_slice_in_dim(field, jnp.where(even == (slot == 0), high, 0), REACH, axis=0) for slot in (0, 1)
    )


def flip(value, bit):
    count = lax.axis_size("shot")
    return lax.ppermute(value, "shot", [(i, i ^ bit) for i in range(count)])


def sum_groups(send, keep, shot):
    got = flip(send, 1)
    bit = 2
    while keep.shape[1] > 1:
        planes, blocks, yb, nz = keep.shape
        mine = (shot // bit) % 2
        shape = (planes, blocks // 2, 2, yb, nz)
        keep, got = keep.reshape(shape), got.reshape(shape)

        def part(which):
            return tuple(lax.dynamic_index_in_dim(v, which, 2, keepdims=False) for v in (keep, got))

        to_send = sum(part(1 - mine))
        keep = sum(part(mine))
        got = flip(to_send, bit)
        bit *= 2
    return keep, got


def spread(pieces, ratio):
    mp, shots = lax.axis_size("mp"), lax.axis_size("shot")
    out = []
    for k, piece in enumerate(pieces):
        pairs = []
        for m in range(mp):
            for s in range(shots):
                target = (s * ratio + m % ratio + k) % mp
                pairs.append((m * shots + s, target * shots + m // ratio))
        out.append(lax.ppermute(piece, ("mp", "shot"), pairs))
    return out


def per_device(
    courant, forward_old, forward_now, adjoint_late, adjoint_now,
    src_cell, src_sign, wavelet, rec_cell, rec_data,
):
    mp_count, shots = lax.axis_size("mp"), lax.axis_size("shot")
    mp, shot = lax.axis_index("mp"), lax.axis_index("shot")
    rows, ny, nz = courant.shape
    ratio = mp_count // shots
    full_x = rows * mp_count
    even = mp % 2 == 0
    first = jnp.stack(
        [
            mp * (rows * ny * nz), mp % 2, shot % 2, jnp.int32(rows), jnp.int32(shots),
            shot * ratio + mp % ratio, shot, mp,
        ]
    ).astype(jnp.int32)
    band_y, band_z = band(ny), band(nz)
    bands = (jnp.asarray(band_y, BF16), jnp.asarray(np.concatenate([band_z, band_z]), BF16))
    strength = float(SMOOTH_YZ * SMOOTH_YZ)
    strength_x = float(SMOOTH_X * SMOOTH_X)
    scan, carry = scan_tables(full_x, strength_x, rows * ratio)
    kappa = 1.0
    for length, e in ((full_x, strength_x), (ny, strength), (nz, strength)):
        resp = response(length, e)
        kappa /= math.sqrt(np.mean(resp * resp))
    z_tables = split_table(filter_matrix(nz, strength))
    y_tables = split_table(kappa * filter_matrix(ny, strength))

    f_old, f_now, a_late, a_now = forward_old[0], forward_now[0], adjoint_late[0], adjoint_now[0]
    f_halo = swap(boundary(f_now, even))
    a_halo = swap(boundary(a_now, even))
    accel, nxt, mid, src, rec = step_one(
        first, src_cell, src_sign, wavelet, rec_cell, rec_data, courant, f_old, f_now, a_late, a_now, bands
    )
    c0, c1, f0, f1 = correct(first, courant, (accel, nxt), f_halo)
    f_halo = swap((f0, f1))
    m0, m1 = correct(first, courant, (mid,), a_halo)
    a_halo = swap((m0, m1))
    send, keep, edge, by_f, by_a = step_two(
        first, courant, a_now, accel, nxt, mid, src, rec, (f0, f1, c0, c1, m0, m1), bands, shots
    )
    raw_shape = (rows, ny // shots, nz)
    keep, got = sum_groups(send, keep, shot)
    raw, *mains = depth(first, keep, got, z_tables, raw_shape, mp_count)
    mains = spread(mains, ratio)
    send, keep = finish(first, edge, by_f, by_a, f_halo, a_halo, shots)
    keep, got = sum_groups(send, keep, shot)
    raw, *edges = depth(first, keep, got, z_tables, raw_shape, mp_count, raw)
    edges = spread(edges, ratio)
    part, *ends = rows_filter(first, jnp.asarray(scan), mains, edges, y_tables, ratio, shots, rows)
    ends = [flip(end, j) for j, end in enumerate(ends, 1)]
    smooth = join(first, jnp.asarray(scan), jnp.asarray(carry), part, ends, y_tables)
    return raw, smooth


def solution(mesh):
    return jax.shard_map(
        per_device,
        mesh=mesh,
        in_specs=(
            P(("parts", "mp"), None, None),
            P(("parts", "shot"), "mp", None, None),
            P(("parts", "shot"), "mp", None, None),
            P(("parts", "shot"), "mp", None, None),
            P(("parts", "shot"), "mp", None, None),
            P(("parts", "shot"), None),
            P(("parts", "shot"), None),
            P(("parts", "shot"), None, None),
            P("parts"),
            P(("parts", "shot"), None, None),
        ),
        out_specs=(P(("parts", "mp"), "shot", None), P(("parts", "shot"), None, "mp")),
        check_vma=False,
    )
```

```python
import functools
import math

import jax
import jax.numpy as jnp
import ml_dtypes
import numpy as np
from jax import lax
from jax.experimental import pallas as pl
from jax.experimental.pallas import tpu as pltpu
from jax.sharding import PartitionSpec as P

SMOOTH_X = 32
SMOOTH_YZ = 4

COEFS = (8.0 / 5.0, -1.0 / 5.0, 8.0 / 315.0, -1.0 / 560.0)
CENTER = -205.0 / 72.0
REACH = len(COEFS)
SCALE = 5040.0
WHOLE = tuple(float(round(SCALE * a)) for a in COEFS)

LANES = 128
BF16 = jnp.bfloat16
F32 = jnp.float32
ANY = pl.BlockSpec(memory_space=pl.ANY)
VMEM = pl.BlockSpec(memory_space=pltpu.VMEM)
SMEM = pl.BlockSpec(memory_space=pltpu.SMEM)


def band(length):
    table = np.zeros((length, length), np.float32)
    for k, weight in enumerate(WHOLE, 1):
        near = np.arange(length - k)
        table[near, near + k] = weight
        table[near + k, near] = weight
    return table


def response(length, strength):
    counter = np.arange(1, length + 1, dtype=np.float64)
    half_sine = np.sin(np.pi * counter / (2 * (length + 1)))
    return 1.0 / (1.0 + strength * 4.0 * half_sine * half_sine)


def filter_matrix(length, strength):
    counter = np.arange(1, length + 1, dtype=np.float64)
    table = np.sin(np.pi * counter[:, None] * counter[None, :] / (length + 1))
    return 2.0 / (length + 1) * (table * response(length, strength)[None, :]) @ table


def scan_tables(length, strength, block):
    rate = math.acosh(1.0 + 0.5 / strength)
    index = np.arange(1, length + 1, dtype=np.float64)
    rise = np.sinh(rate * index)
    fall = np.sinh(rate * (length + 1 - index))
    whole = strength * math.sinh(rate) * math.sinh(rate * (length + 1))
    diag = rise * fall / whole
    left = np.concatenate([[0.0], rise[:-1] / rise[1:]])
    right = np.concatenate([fall[1:] / fall[:-1], [0.0]])
    first = (np.arange(length) // block) * block
    last = first + block - 1
    from_left = np.where(first > 0, rise[np.maximum(first - 1, 0)], 0.0) / rise
    from_right = np.where(last + 1 < length, fall[np.minimum(last + 1, length - 1)], 0.0) / fall
    rows = np.stack([diag, left, right, diag * from_left, diag * from_right])
    blocks = length // block
    carry = np.zeros((blocks, blocks))
    for here in range(blocks):
        for there in range(blocks):
            if there < here:
                carry[here, there] = rise[there * block + block - 1] / rise[here * block - 1]
            elif there > here:
                carry[here, there] = fall[there * block] / fall[here * block + block]
    return rows.astype(np.float32), carry.astype(np.float32)


def split_table(table):
    high = table.astype(np.float32).astype(ml_dtypes.bfloat16)
    low = (table - high.astype(np.float64)).astype(np.float32).astype(ml_dtypes.bfloat16)
    return jnp.asarray(high), jnp.asarray(low)


def split(value):
    high = value.astype(BF16)
    low = (value - high.astype(F32)).astype(BF16)
    return high, low


def dot(a, b):
    return jnp.dot(a, b, preferred_element_type=F32)


def dot_t(a, b):
    return lax.dot_general(a, b, (((1,), (1,)), ((), ())), preferred_element_type=F32)


def laplace_plane(field, p, band_y, band_z):
    here = field[p]
    width = here.shape[1]
    both = jnp.concatenate(split(here), axis=1)
    along_y = dot(band_y[...], both)
    along_z = dot(both, band_z[...])
    total = (3.0 * SCALE * CENTER) * here
    for k, weight in enumerate(WHOLE, 1):
        total += weight * (field[p + k] + field[p - k])
    return total + (along_y[:, :width] + along_y[:, width:]) + along_z


def divmod_fixed(value, size):
    if size & (size - 1) == 0:
        return lax.shift_right_logical(value, size.bit_length() - 1), value & (size - 1)
    return lax.div(value, size), lax.rem(value, size)


class Copies:
    def __init__(self, sems):
        self.sems, self.used = sems, 0

    def start(self, source, target):
        copy = pltpu.make_async_copy(source, target, self.sems.at[self.used])
        self.used += 1
        copy.start()
        return copy


def wait_all(copies):
    for copy in copies:
        copy.wait()


def chunk_bounds(rows):
    step = max(2 * REACH, -(-rows // 3))
    return [(low, min(low + step, rows)) for low in range(0, rows, step)]


def put_blocks(copies, buf, planes, shot, outs):
    return [copies.start(buf.at[planes, shot ^ j], out) for j, out in enumerate(outs)]


def step_one_kernel(
    first_ref, src_cell, src_sign, wavelet, rec_tile, rec_cell, rec_data,
    courant, f_old, f_now, a_late, a_now, band_y, band_z,
    c_buf, acc_buf, f_next, a_mid, a_base, s_second, near_out, keep_out,
    f_pad, a_pad, s_first, r_first, r_second, gt_buf, slot_buf, slots, found, slot_sem, sems,
):
    rows, ny, nz = courant.shape
    copies = Copies(sems)
    bounds = chunk_bounds(rows)

    def chunks(source, target, offset=0):
        return [
            copies.start(source.at[pl.ds(low, high - low)], target.at[pl.ds(low + offset, high - low)])
            for low, high in bounds
        ]

    loads = [chunks(f_now, f_pad, REACH), chunks(courant, c_buf), chunks(f_old, f_next, REACH)]
    late_loads = [chunks(a_now, a_pad, REACH), chunks(a_late, a_mid, REACH)]
    edge = jnp.zeros((REACH, ny, nz), F32)
    for pad in (f_pad, a_pad, f_next, a_mid):
        pad[:REACH] = edge
        pad[REACH + rows :] = edge

    group = ny // 8

    def clear(p, _):
        blank = jnp.zeros((group, 8, nz), F32)
        for ref in (s_first, r_first, s_second, r_second):
            ref[pl.ds(p * group, group)] = blank
        return 0

    lax.fori_loop(0, rows, clear, 0)

    start = first_ref[0]
    size = rows * ny * nz
    flat = lax.broadcasted_iota(jnp.int32, (8, nz), 0) * nz + lax.broadcasted_iota(jnp.int32, (8, nz), 1)

    def put(refs, local, values):
        tile, within = divmod_fixed(local, 8 * nz)
        spot = flat == within
        for ref, value in zip(refs, values, strict=True):
            ref[tile] = ref[tile] + jnp.where(spot, value, 0.0)

    nsrc = src_cell.shape[1]

    def one_source(i, _):
        local = src_cell[0, i] - start
        mine = (local >= 0) & (local < size)
        local = jnp.where(mine, local, 0)
        sign = jnp.where(mine, (2 * src_sign[0, i] - 1).astype(F32), 0.0)
        put((s_first, s_second), local, (sign * wavelet[0, 0, i], sign * wavelet[0, 1, i]))
        return 0

    lax.fori_loop(0, nsrc, one_source, 0, unroll=8 if nsrc % 8 == 0 else 1)

    nrec = rec_cell.shape[0]

    tiles = rec_tile.shape[0]
    local = rec_tile[...] - start
    inside = (local >= 0) & (local < size)
    marks = jnp.where(inside, 1.0, 0.0).astype(BF16)
    row, col = (lax.broadcasted_iota(jnp.int32, (LANES, LANES), d) for d in (0, 1))
    before = dot(marks, jnp.where(row < col, 1.0, 0.0).astype(BF16))
    sums = dot(marks, jnp.ones((LANES, LANES), BF16))
    row, col = (lax.broadcasted_iota(jnp.int32, (tiles, tiles), d) for d in (0, 1))
    above = dot(jnp.where(col < row, 1.0, 0.0).astype(BF16), sums.astype(BF16))
    count = jnp.sum(jnp.where(inside, 1.0, 0.0)).astype(jnp.int32)
    slot_buf[...] = jnp.where(inside, (before + above).astype(jnp.int32), nrec)
    fetch = pltpu.make_async_copy(slot_buf, slots, slot_sem)
    fetch.start()
    fetch.wait()
    batch = 32

    def look(g, _):
        tile = lax.div(g * batch, LANES)
        at = g * batch - tile * LANES
        places = [slots[tile, at + e] for e in range(batch)]
        for e, place in enumerate(places):
            found[place] = g * batch + e
        return 0

    lax.fori_loop(0, nrec // batch, look, 0)

    def receivers(g, valid):
        items = []
        for e in range(8):
            j = found[g * 8 + e]
            if valid is not None:
                j = jnp.where(e < valid, j, 0)
            items.append((rec_cell[j], rec_data[0, 0, j], rec_data[0, 1, j]))
        for e, (cell, first, second) in enumerate(items):
            place = cell - start
            if valid is not None:
                place = jnp.where(e < valid, place, 0)
                first = jnp.where(e < valid, first, 0.0)
                second = jnp.where(e < valid, second, 0.0)
            put((r_first, r_second), place, (first, second))
        return 0

    groups = lax.div(count, 8)
    lax.fori_loop(0, groups, lambda g, _: receivers(g, None), 0)
    receivers(groups, count - groups * 8)

    def forward(p, _):
        courant_here = c_buf[p] * (1.0 / SCALE)
        c_buf[p] = courant_here
        spike = s_first[pl.ds(p * group, group)].reshape(ny, nz)
        accel = courant_here * laplace_plane(f_pad, p + REACH, band_y, band_z) + spike
        acc_buf[p] = accel
        f_next[p + REACH] = (2.0 * f_pad[p + REACH] - f_next[p + REACH]) + accel
        return 0

    loads[0][0].wait()
    for i, (low, high) in enumerate(bounds):
        if i + 1 < len(bounds):
            loads[0][i + 1].wait()
        loads[1][i].wait()
        loads[2][i].wait()
        lax.fori_loop(low, high, forward, 0)

    def adjoint(p, _):
        spike = r_first[pl.ds(p * group, group)].reshape(ny, nz)
        change = c_buf[p] * laplace_plane(a_pad, p + REACH, band_y, band_z) + spike
        mid = (2.0 * a_pad[p + REACH] - a_mid[p + REACH]) + change
        a_mid[p + REACH] = mid
        later = r_second[pl.ds(p * group, group)].reshape(ny, nz)
        a_base[p] = (2.0 * mid - a_pad[p + REACH]) + later
        return 0

    late_loads[0][0].wait()
    for i, (low, high) in enumerate(bounds):
        if i + 1 < len(bounds):
            late_loads[0][i + 1].wait()
        late_loads[1][i].wait()
        lax.fori_loop(low, high, adjoint, 0)

    blocks = gt_buf.shape[1]

    def inner(i, _):
        p = i + 2 * REACH
        c = c_buf[p]
        here = pl.ds(p * group, group)
        mid = a_mid[p + REACH]
        accel = c * laplace_plane(f_next, p + REACH, band_y, band_z) + s_second[here].reshape(ny, nz)
        first = a_base[p] + c * laplace_plane(a_mid, p + REACH, band_y, band_z)
        gt_buf[i] = (first * acc_buf[p] + mid * accel).reshape(blocks, ny // blocks, nz)
        return 0

    lax.fori_loop(0, rows - 4 * REACH, inner, 0)
    bit = first_ref[2]
    stores = []
    for j in range(blocks // 2):
        stores.append(copies.start(gt_buf.at[:, 2 * j + 1 - bit], near_out.at[:, j]))
        stores.append(copies.start(gt_buf.at[:, 2 * j + bit], keep_out.at[:, j]))
    wait_all(stores)


def cheap(megabytes):
    return pltpu.CompilerParams(vmem_limit_bytes=megabytes * 2**20)


COST = pl.CostEstimate(flops=1000, bytes_accessed=1000, transcendentals=0)
LONG = pl.CostEstimate(flops=10**12, bytes_accessed=1000, transcendentals=0)


def held(*shape):
    return pltpu.VMEM(shape, F32)


def in_hbm(arrays):
    return [pltpu.with_memory_space_constraint(array, pltpu.HBM) for array in arrays]


def keep_held(arrays):
    return [pltpu.with_memory_space_constraint(array, pltpu.VMEM) for array in arrays]


def step_one(first, src_cell, src_sign, wavelet, rec_cell, rec_data, courant, f_old, f_now, a_late, a_now, bands, shots):
    rows, ny, nz = courant.shape
    half = jax.ShapeDtypeStruct((rows - 4 * REACH, shots // 2, ny // shots, nz), F32)
    whole, padded, sparse = (rows, ny, nz), (rows + 2 * REACH, ny, nz), (rows * ny // 8, 8, nz)
    nrec = rec_cell.shape[0]
    return pl.pallas_call(
        step_one_kernel,
        out_shape=tuple(held(*shape) for shape in (whole, whole, padded, padded, whole, sparse)) + (half, half),
        in_specs=[SMEM] * 4 + [VMEM] + [SMEM] * 2 + [ANY] * 5 + [VMEM] * 2,
        out_specs=(VMEM,) * 6 + (ANY,) * 2,
        scratch_shapes=[
            held(*padded), held(*padded), held(*sparse), held(*sparse), held(*sparse),
            held(rows - 4 * REACH, shots, ny // shots, nz),
            pltpu.VMEM((nrec // LANES, LANES), jnp.int32),
            pltpu.SMEM((nrec // LANES, LANES), jnp.int32),
            pltpu.SMEM((nrec + 16,), jnp.int32),
            pltpu.SemaphoreType.DMA,
            pltpu.SemaphoreType.DMA((5 * len(chunk_bounds(rows)) + shots,)),
        ],
        compiler_params=cheap(22),
        cost_estimate=LONG,
        name="step_one",
    )(
        first, src_cell, src_sign, wavelet, rec_cell.reshape(-1, LANES), rec_cell, rec_data,
        *in_hbm((courant, f_old, f_now, a_late, a_now)), *bands,
    )


def sides(first_ref, rows):
    even = first_ref[1] == 0
    high = rows - REACH
    return (jnp.where(even, high, 0), even), (jnp.where(even, 0, high), jnp.logical_not(even))


def halo_sum(halo, q, upper):
    total = None
    for k, weight in enumerate(WHOLE, 1):
        if q + k >= REACH:
            h = q + k - REACH
            term = weight * halo[jnp.where(upper, h, REACH - 1 - h)]
            total = term if total is None else total + term
    return total


def pick_kernel(first_ref, f_now, a_now, *refs):
    outs, sems = refs[:2], refs[2]
    copies = Copies(sems)
    wait_all([
        copies.start(field.at[pl.ds(base, REACH)], outs[s].at[i])
        for s, (base, _) in enumerate(sides(first_ref, f_now.shape[0]))
        for i, field in enumerate((f_now, a_now))
    ])


def pick(first, f_now, a_now):
    _, ny, nz = f_now.shape
    both = jax.ShapeDtypeStruct((2, REACH, ny, nz), F32)
    return pl.pallas_call(
        pick_kernel,
        out_shape=(both, both),
        in_specs=[SMEM] + [ANY] * 2,
        out_specs=(VMEM,) * 2,
        scratch_shapes=[pltpu.SemaphoreType.DMA((4,))],
        compiler_params=cheap(8),
        cost_estimate=COST,
        name="pick",
    )(first, *in_hbm((f_now, a_now)))


def correct_kernel(
    first_ref, c_buf, acc_in, next_in, mid_in, base_in, halo0, halo1, keep, near, acc_buf, f_next, a_mid, a_base, *refs
):
    edges, terms, sems = refs[:2], refs[2:-1], refs[-1]
    rows = c_buf.shape[0]
    copies = Copies(sems)
    shot = first_ref[6]
    stores = []
    for s, (base, upper) in enumerate(sides(first_ref, rows)):
        halo = (halo0, halo1)[s]
        for q in range(REACH):
            here = base + jnp.where(upper, q, REACH - 1 - q)
            c = c_buf[here]
            change = c * halo_sum(halo.at[0], q, upper)
            acc_buf[here] = acc_in[here] + change
            f_next[here + REACH] = next_in[here + REACH] + change
            change = c * halo_sum(halo.at[1], q, upper)
            a_mid[here + REACH] = mid_in[here + REACH] + change
            a_base[here] = base_in[here] + 2.0 * change
        inside = pl.ds(base + REACH, REACH)
        stores.append(copies.start(f_next.at[inside], edges[s].at[0]))
        stores.append(copies.start(a_mid.at[inside], edges[s].at[1]))
    for i, term in enumerate(terms):
        block = lax.div(shot ^ (2 * i), 2)
        term[...] = keep[:, block] + near[:, block]
    wait_all(stores)


def correct(first, c, accel, nxt, mid, a_base, halos, keep, near):
    rows, ny, nz = c.shape
    both = jax.ShapeDtypeStruct((2, REACH, ny, nz), F32)
    planes, blocks, yb, _ = keep.shape
    term = jax.ShapeDtypeStruct((planes, yb, nz), F32)
    return pl.pallas_call(
        correct_kernel,
        out_shape=tuple(held(*array.shape) for array in (accel, nxt, mid, a_base)) + (both, both) + (term,) * blocks,
        in_specs=[SMEM] + [VMEM] * 9,
        out_specs=(VMEM,) * 4 + (ANY,) * 2 + (VMEM,) * blocks,
        scratch_shapes=[pltpu.SemaphoreType.DMA((4,))],
        input_output_aliases={2: 0, 3: 1, 4: 2, 5: 3},
        compiler_params=cheap(8),
        cost_estimate=COST,
        name="correct",
    )(first, *keep_held((c, accel, nxt, mid, a_base)), *halos, keep, near)


def step_two_kernel(waits, first_ref, c_buf, acc_buf, f_next, a_mid, a_base, s_buf, band_y, band_z, *refs):
    edge_out, by_f, by_a, *terms_out = refs[waits:-2]
    gt_buf, sems = refs[-2:]
    rows, ny, nz = c_buf.shape
    copies = Copies(sems)
    group = ny // 8
    blocks = gt_buf.shape[1]

    def plane(p, _):
        c = c_buf[p]
        here = pl.ds(p * group, group)
        mid = a_mid[p + REACH]
        accel = c * laplace_plane(f_next, p + REACH, band_y, band_z) + s_buf[here].reshape(ny, nz)
        first = a_base[p] + c * laplace_plane(a_mid, p + REACH, band_y, band_z)
        gt_buf[p] = (first * acc_buf[p] + mid * accel).reshape(blocks, ny // blocks, nz)
        return 0

    stores = []
    shot = first_ref[6]
    for i, low in enumerate((REACH, rows - 2 * REACH)):
        lax.fori_loop(low, low + REACH, plane, 0)
        outs = [out.at[pl.ds(i * REACH, REACH)] for out in terms_out]
        stores += put_blocks(copies, gt_buf, pl.ds(low, REACH), shot, outs)
    for low in (0, rows - REACH):
        lax.fori_loop(low, low + REACH, plane, 0)
    for s, (base, _) in enumerate(sides(first_ref, rows)):
        for q in range(REACH):
            c = c_buf[base + q]
            by_f[s, q] = c * a_mid[base + q + REACH]
            by_a[s, q] = c * acc_buf[base + q]
            edge_out[s, q] = gt_buf[base + q].reshape(ny, nz)
    wait_all(stores)


def step_two(first, arrays, bands, after, shots):
    rows, ny, nz = arrays[0].shape
    edge = jax.ShapeDtypeStruct((2, REACH, ny, nz), F32)
    term = jax.ShapeDtypeStruct((2 * REACH, ny // shots, nz), F32)
    return pl.pallas_call(
        functools.partial(step_two_kernel, len(after)),
        out_shape=(edge, edge, edge) + (term,) * shots,
        in_specs=[SMEM] + [VMEM] * 8 + [ANY] * len(after),
        out_specs=(VMEM,) * 3 + (ANY,) * shots,
        scratch_shapes=[held(rows, shots, ny // shots, nz), pltpu.SemaphoreType.DMA((2 * shots,))],
        compiler_params=cheap(12),
        cost_estimate=LONG,
        name="step_two",
    )(first, *keep_held(arrays), *bands, *after)


def finish_kernel(first_ref, edge, by_f, by_a, halo0, halo1, *refs):
    outs, buf = refs[:-1], refs[-1]
    blocks = buf.shape[1]
    _, reach, ny, nz = edge.shape
    for s, (_, upper) in enumerate(sides(first_ref, first_ref[3])):
        halo = (halo0, halo1)[s]
        for q in range(reach):
            here = jnp.where(upper, q, reach - 1 - q)
            total = edge[s, here] + by_f[s, here] * halo_sum(halo.at[0], q, upper)
            total += by_a[s, here] * halo_sum(halo.at[1], q, upper)
            buf[s * reach + here] = total.reshape(blocks, ny // blocks, nz)
    for j, out in enumerate(outs):
        out[...] = buf[:, first_ref[6] ^ j]


def finish(first, edge, by_f, by_a, halos, shots):
    _, reach, ny, nz = edge.shape
    term = jax.ShapeDtypeStruct((2 * reach, ny // shots, nz), F32)
    return pl.pallas_call(
        finish_kernel,
        out_shape=(term,) * shots,
        in_specs=[SMEM] + [VMEM] * 5,
        out_specs=(VMEM,) * shots,
        scratch_shapes=[pltpu.VMEM((2 * reach, shots, ny // shots, nz), F32)],
        compiler_params=cheap(16),
        cost_estimate=LONG,
        name="finish",
    )(first, edge, by_f, by_a, *halos)


def depth_kernel(layout, parts, pieces, first_ref, *refs):
    used = sum(len(offsets) for offsets in parts)
    terms, refs = refs[:used], refs[used:]
    z_high, z_low = refs[:2]
    raw_out, outs, (raw_buf, spectrum, sems) = refs[-pieces - 4], refs[-pieces - 3 : -3], refs[-3:]
    planes, yb, nz = raw_buf.shape
    shots = first_ref[4].astype(F32)
    copies = Copies(sems)
    low, at = 0, 0
    for chunk, offsets in zip(layout, parts, strict=True):
        size = sum(count for _, count in chunk)
        total = None
        for offset in offsets:
            term = terms[at][offset : offset + size]
            total = term if total is None else total + term
            at += 1
        raw_buf[low : low + size] = total / shots
        low += size
    stores, done = [], 0
    rows = raw_out.shape[0]
    for chunk in layout:
        for where, count in chunk:
            base = sides(first_ref, rows)[where][0] if isinstance(where, bool) else where
            stores.append(copies.start(raw_buf.at[pl.ds(done, count)], raw_out.at[pl.ds(base, count)]))
            done += count
    lanes = LANES // yb
    count = planes // lanes
    zb = nz // pieces
    for p in range(count):
        rows_here = jnp.concatenate([raw_buf[h * count + p] for h in range(lanes)], axis=0)
        high, low_part = split(rows_here)
        table = z_high[...]
        spectrum[p] = (dot_t(table, high) + dot_t(table, low_part) + dot_t(z_low[...], high)).reshape(pieces, zb, LANES)
    offset = first_ref[5]
    for k, out in enumerate(outs):
        out[...] = spectrum[:, lax.rem(offset + k, pieces)]
    wait_all(stores)


def depth(first, layout, terms, tables, raw_shape, pieces, after=(), previous=None):
    planes = sum(count for chunk in layout for _, count in chunk)
    _, yb, nz = raw_shape
    lanes = LANES // yb
    count = planes // lanes
    piece = jax.ShapeDtypeStruct((count, nz // pieces, LANES), F32)
    extra = (*after, *(() if previous is None else (previous,)))
    flat = [term for chunk in terms for term, _ in chunk]
    offsets = [[offset for _, offset in chunk] for chunk in terms]
    last = 1 + len(flat) + 2 + len(extra) - 1
    return pl.pallas_call(
        functools.partial(depth_kernel, layout, offsets, pieces),
        out_shape=(jax.ShapeDtypeStruct(raw_shape, F32),) + (piece,) * pieces,
        in_specs=[SMEM] + [VMEM] * (len(flat) + 2) + [ANY] * len(extra),
        out_specs=(ANY,) + (VMEM,) * pieces,
        scratch_shapes=[
            pltpu.VMEM((planes, yb, nz), F32),
            pltpu.VMEM((count, pieces, nz // pieces, LANES), F32),
            pltpu.SemaphoreType.DMA((sum(len(chunk) for chunk in layout),)),
        ],
        input_output_aliases={} if previous is None else {last: 0},
        compiler_params=cheap(16),
        cost_estimate=LONG,
        name="depth",
    )(first, *flat, *tables, *extra)


def gather_kernel(pieces, ratio, shots, count, plane_of, first_ref, *refs):
    parts, (y_high, y_low, out, buf, field, sems) = refs[:pieces], refs[pieces:]
    mp, shot = first_ref[7], first_ref[6]
    copies = Copies(sems)
    loads = []
    for k in range(pieces):
        q = lax.rem(mp - k + pieces, pieces)
        loads.append(copies.start(parts[k], buf.at[lax.rem(q, ratio), lax.div(q, ratio)]))
    wait_all(loads)
    _, zb, ny = field.shape
    yb = ny // shots
    lanes = LANES // yb
    slot_of = lax.broadcasted_iota(jnp.int32, (zb, LANES), 1) // yb
    for sub in range(ratio):
        for p in range(count):
            for h in range(lanes):
                x = sub * count * lanes + h * count + p
                for t in range(shots // lanes):
                    value = None
                    for e in range(lanes):
                        piece = buf[sub, t * lanes + e, p]
                        if e != h:
                            piece = pltpu.roll(piece, (e - h) * yb % LANES, 1)
                        value = piece if value is None else jnp.where(slot_of == e, piece, value)
                    field[x, :, pl.ds(t * LANES, LANES)] = value
    filter_second(field, out, y_high[...], y_low[...])


def filter_second(field, out, high_t, low_t):
    total, zb, ny = field.shape
    step = max(1, 256 // zb)
    while total % step:
        step -= 1
    for i in range(0, total, step):
        high, low = split(field[i : i + step].reshape(step * zb, ny))
        result = dot_t(high, high_t) + dot_t(low, high_t) + dot_t(high, low_t)
        out[i : i + step] = result.reshape(step, zb, ny)


def gather(first, parts, tables, ratio, shots):
    pieces = len(parts)
    count, zb, _ = parts[0].shape
    ny = tables[0].shape[0]
    total = ratio * count * (LANES * shots // ny)
    return pl.pallas_call(
        functools.partial(gather_kernel, pieces, ratio, shots, count, None),
        out_shape=jax.ShapeDtypeStruct((total, zb, ny), F32),
        in_specs=[SMEM] + [ANY] * pieces + [VMEM] * 2,
        out_specs=VMEM,
        scratch_shapes=[
            pltpu.VMEM((ratio, shots, count, zb, LANES), F32),
            pltpu.VMEM((total, zb, ny), F32),
            pltpu.SemaphoreType.DMA((pieces,)),
        ],
        compiler_params=cheap(16),
        cost_estimate=LONG,
        name="gather",
    )(first, *parts, *tables)


def scan_kernel(planes, rows, shots, first_ref, scan, mains, edges, out, *refs):
    sends, (field, ends) = refs[: shots - 1], refs[shots - 1 :]
    shot = first_ref[6]
    total, zb, ny = field.shape
    ratio = total // rows
    per_slab = len(planes)
    for sub in range(ratio):
        for i, x in enumerate(planes):
            field[sub * rows + x] = mains[sub * per_slab + i]
        even = lax.rem(shot * ratio + sub, 2) == 0
        for s, base in enumerate((jnp.where(even, rows - REACH, 0), jnp.where(even, 0, rows - REACH))):
            for q in range(REACH):
                field[sub * rows + base + q] = edges[sub * 2 * REACH + s * REACH + q]
    first_x = shot * total

    def up(x, carry):
        carry = field[x] + scan[1, first_x + x] * carry
        out[x] = carry
        return carry

    ends[0] = lax.fori_loop(0, total, up, jnp.zeros((zb, ny), F32))

    def down(i, carry):
        x = total - 1 - i
        out[x] = (out[x] + carry) * scan[0, first_x + x]
        return scan[2, first_x + x - 1] * (field[x] + carry)

    carry = lax.fori_loop(0, total - 1, down, jnp.zeros((zb, ny), F32))
    out[0] = (out[0] + carry) * scan[0, first_x]
    ends[1] = field[0] + carry
    for j, send in enumerate(sends, 1):
        send[...] = jnp.where((shot ^ j) > shot, ends[0], ends[1])


def scan_first(first, scan, mains, edges, planes, rows, shots):
    per_slab = len(planes)
    ratio = mains.shape[0] // per_slab
    _, zb, ny = mains.shape
    end = jax.ShapeDtypeStruct((zb, ny), F32)
    total = rows * ratio
    return pl.pallas_call(
        functools.partial(scan_kernel, planes, rows, shots),
        out_shape=(jax.ShapeDtypeStruct((total, zb, ny), F32),) + (end,) * (shots - 1),
        in_specs=[SMEM] * 2 + [VMEM] * 2,
        out_specs=(VMEM,) * shots,
        scratch_shapes=[pltpu.VMEM((total, zb, ny), F32), pltpu.VMEM((2, zb, ny), F32)],
        compiler_params=cheap(16),
        cost_estimate=COST,
        name="scan",
    )(first, scan, mains, edges)


def join_kernel(shots, first_ref, scan, carry, part, *refs):
    ends, out = refs[: shots - 1], refs[shots - 1]
    total, zb, ny = part.shape
    shot = first_ref[6]
    first_x = shot * total
    below = jnp.zeros((zb, ny), F32)
    above = jnp.zeros((zb, ny), F32)
    for j, end in enumerate(ends, 1):
        other = shot ^ j
        term = carry[shot, other] * end[...]
        below += jnp.where(other < shot, term, 0.0)
        above += jnp.where(other > shot, term, 0.0)
    for x in range(total):
        out[x] = part[x] + scan[3, first_x + x] * below + scan[4, first_x + x] * above


def join(first, scan, carry, part, ends):
    total, zb, ny = part.shape
    shots = len(ends) + 1
    return pl.pallas_call(
        functools.partial(join_kernel, shots),
        out_shape=jax.ShapeDtypeStruct((total, zb, ny), F32),
        in_specs=[SMEM] * 3 + [VMEM] * shots,
        out_specs=VMEM,
        compiler_params=cheap(16),
        cost_estimate=COST,
        name="join",
    )(first, scan, carry, part, *ends)


def neighbours(count, start):
    low = range(start, count - 1, 2)
    return [(i, i + 1) for i in low] + [(i + 1, i) for i in low]


def swap(values):
    count = lax.axis_size("mp")
    return tuple(lax.ppermute(v, "mp", neighbours(count, start)) for start, v in enumerate(values))


def flip(value, bit):
    count = lax.axis_size("shot")
    return lax.ppermute(value, "shot", [(i, i ^ bit) for i in range(count)])


def share(terms):
    return [terms[0]] + [flip(term, j) for j, term in enumerate(terms[1:], 1)]


def spread(pieces, ratio):
    mp, shots = lax.axis_size("mp"), lax.axis_size("shot")
    out = []
    for k, piece in enumerate(pieces):
        pairs = []
        for m in range(mp):
            for s in range(shots):
                target = (s * ratio + m % ratio + k) % mp
                pairs.append((m * shots + s, target * shots + m // ratio))
        out.append(lax.ppermute(piece, ("mp", "shot"), pairs))
    return out


def per_device(
    courant, forward_old, forward_now, adjoint_late, adjoint_now,
    src_cell, src_sign, wavelet, rec_cell, rec_data,
):
    mp_count, shots = lax.axis_size("mp"), lax.axis_size("shot")
    mp, shot = lax.axis_index("mp"), lax.axis_index("shot")
    rows, ny, nz = courant.shape
    ratio = mp_count // shots
    full_x = rows * mp_count
    first = jnp.stack(
        [
            mp * (rows * ny * nz), mp % 2, shot % 2, jnp.int32(rows), jnp.int32(shots),
            shot * ratio + mp % ratio, shot, mp,
        ]
    ).astype(jnp.int32)
    band_y, band_z = band(ny), band(nz)
    bands = (jnp.asarray(band_y, BF16), jnp.asarray(np.concatenate([band_z, band_z]), BF16))
    strength = float(SMOOTH_YZ * SMOOTH_YZ)
    strength_x = float(SMOOTH_X * SMOOTH_X)
    scan, carry = scan_tables(full_x, strength_x, rows * ratio)
    kappa = 1.0
    for length, e in ((full_x, strength_x), (ny, strength), (nz, strength)):
        resp = response(length, e)
        kappa /= math.sqrt(np.mean(resp * resp))
    z_tables = split_table(filter_matrix(nz, strength))
    y_tables = split_table(kappa * filter_matrix(ny, strength))

    f_old, f_now, a_late, a_now = forward_old[0], forward_now[0], adjoint_late[0], adjoint_now[0]
    halos = swap(pick(first, f_now, a_now))
    c, accel, nxt, mid, a_base, src, near, keep = step_one(
        first, src_cell, src_sign, wavelet, rec_cell, rec_data, courant, f_old, f_now, a_late, a_now, bands, shots
    )
    accel, nxt, mid, a_base, edge0, edge1, *inner = correct(
        first, c, accel, nxt, mid, a_base, halos, keep, flip(near, 1)
    )
    halos = swap((edge0, edge1))
    inner = [inner[0]] + [flip(term, 2 * i) for i, term in enumerate(inner[1:], 1)]
    edge, by_f, by_a, *outer = step_two(first, (c, accel, nxt, mid, a_base, src), bands, inner[1:], shots)
    outer = share(outer)
    last = share(finish(first, edge, by_f, by_a, halos, shots))
    raw_shape = (rows, ny // shots, nz)
    layout = [[(2 * REACH, rows - 4 * REACH)], [(REACH, REACH), (rows - 2 * REACH, REACH)]]
    terms = [[(term, 0) for term in inner], [(term, 0) for term in outer]]
    raw, *mains = depth(first, layout, terms, z_tables, raw_shape, mp_count)
    mains = gather(first, spread(mains, ratio), y_tables, ratio, shots)
    layout_edge = [[(False, REACH), (True, REACH)]]
    terms = [[(term, 0) for term in last]]
    raw, *edges = depth(first, layout_edge, terms, z_tables, raw_shape, mp_count, (), raw)
    edges = gather(first, spread(edges, ratio), y_tables, ratio, shots)
    planes = [low + i for chunk in layout for low, count in chunk for i in range(count)]
    part, *ends = scan_first(first, jnp.asarray(scan), mains, edges, planes, rows, shots)
    ends = [flip(end, j) for j, end in enumerate(ends, 1)]
    smooth = join(first, jnp.asarray(scan), jnp.asarray(carry), part, ends)
    smooth = jnp.transpose(smooth, (0, 2, 1))
    return raw, smooth


def solution(mesh):
    return jax.shard_map(
        per_device,
        mesh=mesh,
        in_specs=(
            P(("parts", "mp"), None, None),
            P(("parts", "shot"), "mp", None, None),
            P(("parts", "shot"), "mp", None, None),
            P(("parts", "shot"), "mp", None, None),
            P(("parts", "shot"), "mp", None, None),
            P(("parts", "shot"), None),
            P(("parts", "shot"), None),
            P(("parts", "shot"), None, None),
            P("parts"),
            P(("parts", "shot"), None, None),
        ),
        out_specs=(P(("parts", "mp"), "shot", None), P(("parts", "shot"), None, "mp")),
        check_vma=False,
    )
```

```python
import functools
import math

import jax
import jax.numpy as jnp
import ml_dtypes
import numpy as np
from jax import lax
from jax.experimental import pallas as pl
from jax.experimental.pallas import tpu as pltpu
from jax.sharding import PartitionSpec as P

SMOOTH_X = 32
SMOOTH_YZ = 4

COEFS = (8.0 / 5.0, -1.0 / 5.0, 8.0 / 315.0, -1.0 / 560.0)
CENTER = -205.0 / 72.0
REACH = len(COEFS)
SCALE = 5040.0
WHOLE = tuple(float(round(SCALE * a)) for a in COEFS)

LANES = 128
BF16 = jnp.bfloat16
F32 = jnp.float32
ANY = pl.BlockSpec(memory_space=pl.ANY)
VMEM = pl.BlockSpec(memory_space=pltpu.VMEM)
SMEM = pl.BlockSpec(memory_space=pltpu.SMEM)


def band(length):
    table = np.zeros((length, length), np.float32)
    for k, weight in enumerate(WHOLE, 1):
        near = np.arange(length - k)
        table[near, near + k] = weight
        table[near + k, near] = weight
    return table


def response(length, strength):
    counter = np.arange(1, length + 1, dtype=np.float64)
    half_sine = np.sin(np.pi * counter / (2 * (length + 1)))
    return 1.0 / (1.0 + strength * 4.0 * half_sine * half_sine)


def filter_matrix(length, strength):
    counter = np.arange(1, length + 1, dtype=np.float64)
    table = np.sin(np.pi * counter[:, None] * counter[None, :] / (length + 1))
    return 2.0 / (length + 1) * (table * response(length, strength)[None, :]) @ table


def scan_tables(length, strength, block):
    rate = math.acosh(1.0 + 0.5 / strength)
    index = np.arange(1, length + 1, dtype=np.float64)
    rise = np.sinh(rate * index)
    fall = np.sinh(rate * (length + 1 - index))
    whole = strength * math.sinh(rate) * math.sinh(rate * (length + 1))
    diag = rise * fall / whole
    left = np.concatenate([[0.0], rise[:-1] / rise[1:]])
    right = np.concatenate([fall[1:] / fall[:-1], [0.0]])
    first = (np.arange(length) // block) * block
    last = first + block - 1
    from_left = np.where(first > 0, rise[np.maximum(first - 1, 0)], 0.0) / rise
    from_right = np.where(last + 1 < length, fall[np.minimum(last + 1, length - 1)], 0.0) / fall
    rows = np.stack([diag, left, right, diag * from_left, diag * from_right])
    blocks = length // block
    carry = np.zeros((blocks, blocks))
    for here in range(blocks):
        for there in range(blocks):
            if there < here:
                carry[here, there] = rise[there * block + block - 1] / rise[here * block - 1]
            elif there > here:
                carry[here, there] = fall[there * block] / fall[here * block + block]
    return rows.astype(np.float32), carry.astype(np.float32)


def split_table(table):
    high = table.astype(np.float32).astype(ml_dtypes.bfloat16)
    low = (table - high.astype(np.float64)).astype(np.float32).astype(ml_dtypes.bfloat16)
    return jnp.asarray(high), jnp.asarray(low)


def split(value):
    high = value.astype(BF16)
    low = (value - high.astype(F32)).astype(BF16)
    return high, low


def dot(a, b):
    return jnp.dot(a, b, preferred_element_type=F32)


def dot_t(a, b):
    return lax.dot_general(a, b, (((1,), (1,)), ((), ())), preferred_element_type=F32)


def laplace_plane(field, p, band_y, band_z):
    here = field[p]
    width = here.shape[1]
    both = jnp.concatenate(split(here), axis=1)
    along_y = dot(band_y[...], both)
    along_z = dot(both, band_z[...])
    total = (3.0 * SCALE * CENTER) * here
    for k, weight in enumerate(WHOLE, 1):
        total += weight * (field[p + k] + field[p - k])
    return total + (along_y[:, :width] + along_y[:, width:]) + along_z


def divmod_fixed(value, size):
    if size & (size - 1) == 0:
        return lax.shift_right_logical(value, size.bit_length() - 1), value & (size - 1)
    return lax.div(value, size), lax.rem(value, size)


class Copies:
    def __init__(self, sems):
        self.sems, self.used = sems, 0

    def start(self, source, target):
        copy = pltpu.make_async_copy(source, target, self.sems.at[self.used])
        self.used += 1
        copy.start()
        return copy


def wait_all(copies):
    for copy in copies:
        copy.wait()


def chunk_bounds(rows):
    step = max(2 * REACH, -(-rows // 3))
    return [(low, min(low + step, rows)) for low in range(0, rows, step)]


def put_blocks(copies, buf, planes, shot, outs):
    return [copies.start(buf.at[planes, shot ^ j], out) for j, out in enumerate(outs)]


def step_one_kernel(
    src_cell, src_sign, wavelet, rec_tile, data_tile,
    courant, f_old, f_now, a_late, a_now, band_y, band_z,
    c_buf, acc_buf, f_next, a_mid, a_base, s_second,
    *refs,
):
    terms_out = refs[:-15]
    (
        f_pad, a_pad, s_first, r_first, r_second, gt_buf,
        place_buf, value_buf, count_buf, places, values, counts, list_sems, term_sems, sems,
    ) = refs[-15:]
    rows, ny, nz = courant.shape
    copies = Copies(sems)
    bounds = chunk_bounds(rows)

    def chunks(source, target, offset=0):
        return [
            copies.start(source.at[pl.ds(low, high - low)], target.at[pl.ds(low + offset, high - low)])
            for low, high in bounds
        ]

    loads = [chunks(f_now, f_pad, REACH), chunks(courant, c_buf), chunks(f_old, f_next, REACH)]
    late_loads = [chunks(a_now, a_pad, REACH), chunks(a_late, a_mid, REACH)]
    edge = jnp.zeros((REACH, ny, nz), F32)
    for pad in (f_pad, a_pad, f_next, a_mid):
        pad[:REACH] = edge
        pad[REACH + rows :] = edge

    group = ny // 8

    def clear(p, _):
        blank = jnp.zeros((group, 8, nz), F32)
        for ref in (s_first, r_first, s_second, r_second):
            ref[pl.ds(p * group, group)] = blank
        return 0

    lax.fori_loop(0, rows, clear, 0)

    size = rows * ny * nz
    start = lax.axis_index("mp") * size
    flat = lax.broadcasted_iota(jnp.int32, (8, nz), 0) * nz + lax.broadcasted_iota(jnp.int32, (8, nz), 1)

    def put(refs, local, values):
        tile, within = divmod_fixed(local, 8 * nz)
        spot = flat == within
        for ref, value in zip(refs, values, strict=True):
            ref[tile] = ref[tile] + jnp.where(spot, value, 0.0)

    nsrc = src_cell.shape[1]

    def one_source(i, _):
        local = src_cell[0, i] - start
        mine = (local >= 0) & (local < size)
        local = jnp.where(mine, local, 0)
        sign = jnp.where(mine, (2 * src_sign[0, i] - 1).astype(F32), 0.0)
        put((s_first, s_second), local, (sign * wavelet[0, 0, i], sign * wavelet[0, 1, i]))
        return 0

    lax.fori_loop(0, nsrc, one_source, 0, unroll=8 if nsrc % 8 == 0 else 1)


    tiles = rec_tile.shape[0]
    local = rec_tile[...] - start
    inside = (local >= 0) & (local < size)
    marks = jnp.where(inside, 1.0, 0.0).astype(BF16)
    row, col = (lax.broadcasted_iota(jnp.int32, (LANES, LANES), d) for d in (0, 1))
    before = jnp.where(inside, dot(marks, jnp.where(row < col, 1.0, 0.0).astype(BF16)).astype(jnp.int32), -1)
    thirds = []
    for value in (jnp.where(inside, local, 0).astype(F32), data_tile[0], data_tile[1]):
        for _ in range(3):
            part = value.astype(BF16)
            value = value - part.astype(F32)
            thirds.append(part)
    for t in range(tiles):
        moves = jnp.where(row == before[t : t + 1], 1.0, 0.0).astype(BF16)
        stacked = jnp.concatenate([part[t : t + 1] for part in thirds] + [thirds[0][:7]], axis=0)
        moved = dot_t(stacked, moves)
        place_buf[t : t + 1] = (moved[0:1] + moved[1:2] + moved[2:3]).astype(jnp.int32)
        value_buf[0, t : t + 1] = moved[3:4] + moved[4:5] + moved[5:6]
        value_buf[1, t : t + 1] = moved[6:7] + moved[7:8] + moved[8:9]
    count_buf[...] = dot(marks, jnp.ones((LANES, LANES), BF16)).astype(jnp.int32)
    fetches = [
        pltpu.make_async_copy(source, target, list_sems.at[i])
        for i, (source, target) in enumerate(((place_buf, places), (value_buf, values), (count_buf, counts)))
    ]
    for fetch in fetches:
        fetch.start()
    wait_all(fetches)

    def receivers(t, _):
        def some(g, _):
            items = []
            for e in range(8):
                i = g * 8 + e
                items.append((places[t, i], values[0, t, i], values[1, t, i]))
            for place, first, second in items:
                put((r_first, r_second), place, (first, second))
            return 0

        return lax.fori_loop(0, lax.div(counts[t, 0] + 7, 8), some, 0)

    lax.fori_loop(0, tiles, receivers, 0)

    def forward(p, _):
        courant_here = c_buf[p] * (1.0 / SCALE)
        c_buf[p] = courant_here
        spike = s_first[pl.ds(p * group, group)].reshape(ny, nz)
        accel = courant_here * laplace_plane(f_pad, p + REACH, band_y, band_z) + spike
        acc_buf[p] = accel
        f_next[p + REACH] = (2.0 * f_pad[p + REACH] - f_next[p + REACH]) + accel
        return 0

    for group_loads in loads:
        wait_all(group_loads)
    lax.fori_loop(0, rows, forward, 0, unroll=2)

    def adjoint(p, _):
        spike = r_first[pl.ds(p * group, group)].reshape(ny, nz)
        change = c_buf[p] * laplace_plane(a_pad, p + REACH, band_y, band_z) + spike
        mid = (2.0 * a_pad[p + REACH] - a_mid[p + REACH]) + change
        a_mid[p + REACH] = mid
        later = r_second[pl.ds(p * group, group)].reshape(ny, nz)
        a_base[p] = (2.0 * mid - a_pad[p + REACH]) + later
        return 0

    for group_loads in late_loads:
        wait_all(group_loads)
    lax.fori_loop(0, rows, adjoint, 0, unroll=2)

    blocks = gt_buf.shape[1]

    def inner(i, _):
        p = i + 2 * REACH
        c = c_buf[p]
        here = pl.ds(p * group, group)
        accel = c * laplace_plane(f_next, p + REACH, band_y, band_z) + s_second[here].reshape(ny, nz)
        first = a_base[p] + c * laplace_plane(a_mid, p + REACH, band_y, band_z)
        gt_buf[i] = (first * acc_buf[p] + a_mid[p + REACH] * accel).reshape(blocks, ny // blocks, nz)
        return 0

    lax.fori_loop(0, rows - 4 * REACH, inner, 0)
    wait_all(put_blocks(Copies(term_sems), gt_buf, slice(None), lax.axis_index("shot"), terms_out))


def cheap(megabytes):
    return pltpu.CompilerParams(vmem_limit_bytes=megabytes * 2**20)


COST = pl.CostEstimate(flops=1000, bytes_accessed=1000, transcendentals=0)
LONG = pl.CostEstimate(flops=10**12, bytes_accessed=1000, transcendentals=0)


def held(*shape):
    return pltpu.VMEM(shape, F32)


def in_hbm(arrays):
    return [pltpu.with_memory_space_constraint(array, pltpu.HBM) for array in arrays]


def keep_held(arrays):
    return [pltpu.with_memory_space_constraint(array, pltpu.VMEM) for array in arrays]


def step_one(src_cell, src_sign, wavelet, rec_cell, rec_data, courant, f_old, f_now, a_late, a_now, bands, shots):
    rows, ny, nz = courant.shape
    term = held(rows - 4 * REACH, ny // shots, nz)
    whole, padded, sparse = (rows, ny, nz), (rows + 2 * REACH, ny, nz), (rows * ny // 8, 8, nz)
    tiles = rec_cell.shape[0] // LANES
    return pl.pallas_call(
        step_one_kernel,
        out_shape=tuple(held(*shape) for shape in (whole, whole, padded, padded, whole, sparse)) + (term,) * shots,
        in_specs=[SMEM] * 3 + [VMEM] * 2 + [ANY] * 5 + [VMEM] * 2,
        out_specs=(VMEM,) * (6 + shots),
        scratch_shapes=[
            held(*padded), held(*padded), held(*sparse), held(*sparse), held(*sparse),
            held(rows - 4 * REACH, shots, ny // shots, nz),
            pltpu.VMEM((tiles, LANES), jnp.int32),
            pltpu.VMEM((2, tiles, LANES), F32),
            pltpu.VMEM((tiles, LANES), jnp.int32),
            pltpu.SMEM((tiles, LANES), jnp.int32),
            pltpu.SMEM((2, tiles, LANES), F32),
            pltpu.SMEM((tiles, LANES), jnp.int32),
            pltpu.SemaphoreType.DMA((3,)),
            pltpu.SemaphoreType.DMA((shots,)),
            pltpu.SemaphoreType.DMA((5 * len(chunk_bounds(rows)),)),
        ],
        compiler_params=cheap(24),
        cost_estimate=LONG,
        name="step_one",
    )(
        src_cell, src_sign, wavelet, rec_cell.reshape(-1, LANES), rec_data.reshape(2, -1, LANES),
        *in_hbm((courant, f_old, f_now, a_late, a_now)), *bands,
    )


def sides(rows):
    even = lax.rem(lax.axis_index("mp"), 2) == 0
    high = rows - REACH
    return (jnp.where(even, high, 0), even), (jnp.where(even, 0, high), jnp.logical_not(even))


STRIP = 32


def halo_sums(halo, upper):
    planes = [halo(jnp.where(upper, h, REACH - 1 - h)) for h in range(REACH)]
    return [sum(WHOLE[h + REACH - q - 1] * planes[h] for h in range(q + 1)) for q in range(REACH)]


def strips(count, body):
    def step(i, _):
        body(pl.ds(pl.multiple_of(i * STRIP, STRIP), STRIP))
        return 0

    lax.fori_loop(0, count // STRIP, step, 0)


def pick_kernel(f_now, a_now, *refs):
    outs, sems = refs[:2], refs[2]
    copies = Copies(sems)
    wait_all([
        copies.start(field.at[pl.ds(base, REACH)], outs[s].at[i])
        for s, (base, _) in enumerate(sides(f_now.shape[0]))
        for i, field in enumerate((f_now, a_now))
    ])


def pick(f_now, a_now):
    _, ny, nz = f_now.shape
    both = held(2, REACH, ny, nz)
    return pl.pallas_call(
        pick_kernel,
        out_shape=(both, both),
        in_specs=[ANY] * 2,
        out_specs=(VMEM,) * 2,
        scratch_shapes=[pltpu.SemaphoreType.DMA((4,))],
        compiler_params=cheap(8),
        cost_estimate=COST,
        name="pick",
    )(*in_hbm((f_now, a_now)))


def correct_kernel(
    c_buf, acc_in, next_in, mid_in, base_in, halo0, halo1, acc_buf, f_next, a_mid, a_base, edge0, edge1
):
    edges = (edge0, edge1)
    rows, ny, _ = c_buf.shape

    def strip(part):
        for s, (base, upper) in enumerate(sides(rows)):
            halo = (halo0, halo1)[s]
            forward = halo_sums(lambda h, halo=halo: halo[0, h, part], upper)
            adjoint = halo_sums(lambda h, halo=halo: halo[1, h, part], upper)
            for q in range(REACH):
                place = jnp.where(upper, q, REACH - 1 - q)
                here = base + place
                c = c_buf[here, part]
                change = c * forward[q]
                acc_buf[here, part] = acc_in[here, part] + change
                value = next_in[here + REACH, part] + change
                f_next[here + REACH, part] = value
                edges[s][0, place, part] = value
                change = c * adjoint[q]
                value = mid_in[here + REACH, part] + change
                a_mid[here + REACH, part] = value
                edges[s][1, place, part] = value
                a_base[here, part] = base_in[here, part] + 2.0 * change

    strips(ny, strip)


def correct(c, accel, nxt, mid, a_base, halos):
    rows, ny, nz = c.shape
    both = held(2, REACH, ny, nz)
    return pl.pallas_call(
        correct_kernel,
        out_shape=tuple(held(*array.shape) for array in (accel, nxt, mid, a_base)) + (both, both),
        in_specs=[VMEM] * 7,
        out_specs=(VMEM,) * 6,
        input_output_aliases={1: 0, 2: 1, 3: 2, 4: 3},
        compiler_params=cheap(8),
        cost_estimate=COST,
        name="correct",
    )(*keep_held((c, accel, nxt, mid, a_base)), *halos)


def step_two_kernel(waits, c_buf, acc_buf, f_next, a_mid, a_base, s_buf, band_y, band_z, *refs):
    edge_out, by_f, by_a, *terms_out, gt_buf, sems = refs[waits:]
    rows, ny, nz = c_buf.shape
    copies = Copies(sems)
    group = ny // 8
    blocks = gt_buf.shape[1]

    def plane(p, _):
        c = c_buf[p]
        here = pl.ds(p * group, group)
        mid = a_mid[p + REACH]
        accel = c * laplace_plane(f_next, p + REACH, band_y, band_z) + s_buf[here].reshape(ny, nz)
        first = a_base[p] + c * laplace_plane(a_mid, p + REACH, band_y, band_z)
        gt_buf[p] = (first * acc_buf[p] + mid * accel).reshape(blocks, ny // blocks, nz)
        return 0

    def inner(i, _):
        return plane(jnp.where(i < REACH, i + REACH, i + rows - 3 * REACH), 0)

    lax.fori_loop(0, 2 * REACH, inner, 0)
    stores = []
    for i, low in enumerate((REACH, rows - 2 * REACH)):
        outs = [out.at[pl.ds(i * REACH, REACH)] for out in terms_out]
        stores += put_blocks(copies, gt_buf, pl.ds(low, REACH), lax.axis_index("shot"), outs)

    bases = [base for base, _ in sides(rows)]

    def outer(i, _):
        s, q = lax.div(i, REACH), lax.rem(i, REACH)
        p = jnp.where(s == 0, bases[0], bases[1]) + q
        plane(p, 0)
        c = c_buf[p]
        by_f[s, q] = c * a_mid[p + REACH]
        by_a[s, q] = c * acc_buf[p]
        edge_out[s, q] = gt_buf[p].reshape(ny, nz)
        return 0

    lax.fori_loop(0, 2 * REACH, outer, 0)
    wait_all(stores)


def step_two(arrays, bands, after, shots):
    rows, ny, nz = arrays[0].shape
    edge = held(2, REACH, ny, nz)
    term = held(2 * REACH, ny // shots, nz)
    return pl.pallas_call(
        functools.partial(step_two_kernel, len(after)),
        out_shape=(edge, edge, edge) + (term,) * shots,
        in_specs=[VMEM] * (8 + len(after)),
        out_specs=(VMEM,) * (3 + shots),
        scratch_shapes=[held(rows, shots, ny // shots, nz), pltpu.SemaphoreType.DMA((2 * shots,))],
        compiler_params=cheap(12),
        cost_estimate=LONG,
        name="step_two",
    )(*keep_held(arrays), *bands, *after)


def add_up_kernel(shots, *refs):
    terms, out = refs[:shots], refs[2 * shots]
    total = terms[0][...]
    for term in terms[1:]:
        total += term[...]
    out[...] = total


def add_up(terms, passed):
    shots = len(terms)
    outs = pl.pallas_call(
        functools.partial(add_up_kernel, shots),
        out_shape=tuple(held(*array.shape) for array in (terms[0], *passed)),
        in_specs=[VMEM] * shots + [ANY] * shots,
        out_specs=(VMEM,) + (ANY,) * shots,
        input_output_aliases={shots + i: 1 + i for i in range(shots)},
        compiler_params=cheap(8),
        cost_estimate=COST,
        name="add_up",
    )(*keep_held((*terms, *passed)))
    return outs[0], outs[1:]


def finish_kernel(edge, by_f, by_a, halo0, halo1, near_out, keep_out):
    _, blocks, yb, _ = near_out.shape
    bit = lax.rem(lax.axis_index("shot"), 2)
    width = math.gcd(yb, STRIP)

    def strip(i, _):
        for out, mine in ((near_out, 1 - bit), (keep_out, bit)):
            for j in range(blocks):
                inside = pl.ds(pl.multiple_of(i * width, width), width)
                part = pl.ds(pl.multiple_of((2 * j + mine) * yb + i * width, width), width)
                for s, (_, upper) in enumerate(sides(2 * REACH)):
                    halo = (halo0, halo1)[s]
                    forward = halo_sums(lambda h, halo=halo: halo[0, h, part], upper)
                    adjoint = halo_sums(lambda h, halo=halo: halo[1, h, part], upper)
                    for q in range(REACH):
                        place = jnp.where(upper, q, REACH - 1 - q)
                        total = edge[s, place, part] + by_f[s, place, part] * forward[q]
                        out[s * REACH + place, j, inside] = total + by_a[s, place, part] * adjoint[q]
        return 0

    lax.fori_loop(0, yb // width, strip, 0)


def finish(edge, by_f, by_a, halos, shots):
    _, reach, ny, nz = edge.shape
    half = held(2 * reach, shots // 2, ny // shots, nz)
    return pl.pallas_call(
        finish_kernel,
        out_shape=(half, half),
        in_specs=[VMEM] * 5,
        out_specs=(VMEM,) * 2,
        compiler_params=cheap(16),
        cost_estimate=LONG,
        name="finish",
    )(edge, by_f, by_a, *halos)


def depth_kernel(layout, parts, pieces, *refs):
    used = sum(len(offsets) for offsets in parts)
    terms, refs = refs[:used], refs[used:]
    z_high, z_low = refs[:2]
    raw_out, outs, (raw_buf, spectrum, sems) = refs[-pieces - 4], refs[-pieces - 3 : -3], refs[-3:]
    planes, yb, nz = raw_buf.shape
    shots = lax.axis_size("shot")
    copies = Copies(sems)
    low, at = 0, 0
    for chunk, offsets in zip(layout, parts, strict=True):
        size = sum(count for _, count in chunk)
        total = None
        for offset in offsets:
            term = terms[at][offset : offset + size]
            total = term if total is None else total + term
            at += 1
        raw_buf[low : low + size] = total / shots
        low += size
    stores, done = [], 0
    rows = raw_out.shape[0]
    for chunk in layout:
        for where, count in chunk:
            base = sides(rows)[where][0] if isinstance(where, bool) else where
            stores.append(copies.start(raw_buf.at[pl.ds(done, count)], raw_out.at[pl.ds(base, count)]))
            done += count
    lanes = LANES // yb
    count = planes // lanes
    zb = nz // pieces

    def turn(p, _):
        rows_here = jnp.concatenate([raw_buf[h * count + p] for h in range(lanes)], axis=0)
        high, low_part = split(rows_here)
        table = z_high[...]
        spectrum[p] = (dot_t(table, high) + dot_t(table, low_part) + dot_t(z_low[...], high)).reshape(pieces, zb, LANES)
        return 0

    lax.fori_loop(0, count, turn, 0, unroll=2)
    offset = piece_offset()
    for k, out in enumerate(outs):
        out[...] = spectrum[:, lax.rem(offset + k, pieces)]
    wait_all(stores)


def depth(layout, terms, tables, raw_shape, pieces, after=(), previous=None):
    planes = sum(count for chunk in layout for _, count in chunk)
    _, yb, nz = raw_shape
    lanes = LANES // yb
    count = planes // lanes
    piece = held(count, nz // pieces, LANES)
    extra = (*after, *(() if previous is None else (previous,)))
    flat = [term for chunk in terms for term, _ in chunk]
    offsets = [[offset for _, offset in chunk] for chunk in terms]
    last = len(flat) + 2 + len(extra) - 1
    return pl.pallas_call(
        functools.partial(depth_kernel, layout, offsets, pieces),
        out_shape=(jax.ShapeDtypeStruct(raw_shape, F32),) + (piece,) * pieces,
        in_specs=[VMEM] * (len(flat) + 2) + [ANY] * len(extra),
        out_specs=(ANY,) + (VMEM,) * pieces,
        scratch_shapes=[
            pltpu.VMEM((planes, yb, nz), F32),
            pltpu.VMEM((count, pieces, nz // pieces, LANES), F32),
            pltpu.SemaphoreType.DMA((sum(len(chunk) for chunk in layout),)),
        ],
        input_output_aliases={} if previous is None else {last: 0},
        compiler_params=cheap(16),
        cost_estimate=LONG,
        name="depth",
    )(*flat, *tables, *extra)


def piece_offset():
    ratio = lax.axis_size("mp") // lax.axis_size("shot")
    return lax.axis_index("shot") * ratio + lax.rem(lax.axis_index("mp"), ratio)


def depth_edge_kernel(pieces, keep, near, z_high, z_low, own, *refs):
    far, outs, (total, spectrum) = refs[: -pieces - 2], refs[-pieces - 2 : -2], refs[-2:]
    planes, blocks, yb, nz = keep.shape
    total[...] = (keep[...] + near[...]) / lax.axis_size("shot")
    for i, term in enumerate((own, *far)):
        term[...] = total[:, lax.div(lax.axis_index("shot") ^ (2 * i), 2)]

    def turn(p, _):
        high, low = split(total[p].reshape(blocks * yb, nz))
        table = z_high[...]
        both = dot_t(table, high) + dot_t(table, low) + dot_t(z_low[...], high)
        spectrum[p] = both.reshape(pieces, nz // pieces, blocks * yb)
        return 0

    lax.fori_loop(0, planes, turn, 0, unroll=2)
    for k, out in enumerate(outs):
        out[...] = spectrum[:, lax.rem(piece_offset() + k, pieces)]


def depth_edge(keep, near, tables, pieces):
    planes, blocks, yb, nz = keep.shape
    term = held(planes, yb, nz)
    piece = held(planes, nz // pieces, blocks * yb)
    outs = pl.pallas_call(
        functools.partial(depth_edge_kernel, pieces),
        out_shape=(term,) * blocks + (piece,) * pieces,
        in_specs=[VMEM] * 4,
        out_specs=(VMEM,) * (blocks + pieces),
        scratch_shapes=[
            pltpu.VMEM(keep.shape, F32),
            pltpu.VMEM((planes, pieces, nz // pieces, blocks * yb), F32),
        ],
        compiler_params=cheap(12),
        cost_estimate=LONG,
        name="depth_edge",
    )(keep, near, *tables)
    return outs[:blocks], outs[blocks:]


def raw_edge_kernel(*refs):
    terms, (raw_out, buf, sems) = refs[:-4], refs[-3:]
    total = terms[0][...]
    for term in terms[1:]:
        total += term[...]
    buf[...] = total
    copies = Copies(sems)
    wait_all([
        copies.start(buf.at[pl.ds(s * REACH, REACH)], raw_out.at[pl.ds(base, REACH)])
        for s, (base, _) in enumerate(sides(raw_out.shape[0]))
    ])


def raw_edge(terms, raw):
    return pl.pallas_call(
        raw_edge_kernel,
        out_shape=jax.ShapeDtypeStruct(raw.shape, F32),
        in_specs=[VMEM] * len(terms) + [ANY],
        out_specs=ANY,
        scratch_shapes=[pltpu.VMEM(terms[0].shape, F32), pltpu.SemaphoreType.DMA((2,))],
        input_output_aliases={len(terms): 0},
        compiler_params=cheap(8),
        cost_estimate=COST,
        name="raw_edge",
    )(*terms, raw)


def gather_planes(ratio, shots, parts, buf, field, sems):
    pieces = len(parts)
    mp = lax.axis_index("mp")
    copies = Copies(sems)
    loads = []
    for k, part in enumerate(parts):
        q = lax.rem(mp - k + pieces, pieces)
        loads.append(copies.start(part, buf.at[lax.rem(q, ratio), lax.div(q, ratio)]))
    wait_all(loads)
    count = buf.shape[2]
    _, zb, ny = field.shape
    yb = ny // shots
    lanes = LANES // yb
    slot_of = lax.broadcasted_iota(jnp.int32, (zb, LANES), 1) // yb
    for sub in range(ratio):
        for p in range(count):
            for h in range(lanes):
                x = sub * count * lanes + h * count + p
                for t in range(shots // lanes):
                    value = None
                    for e in range(lanes):
                        piece = buf[sub, t * lanes + e, p]
                        if e != h:
                            piece = pltpu.roll(piece, (e - h) * yb % LANES, 1)
                        value = piece if value is None else jnp.where(slot_of == e, piece, value)
                    field[x, :, pl.ds(t * LANES, LANES)] = value


def gather_halves(ratio, shots, parts, buf, field, sems):
    pieces = len(parts)
    copies = Copies(sems)
    loads = []
    for k, part in enumerate(parts):
        q = lax.rem(lax.axis_index("mp") - k + pieces, pieces)
        loads.append(copies.start(part, buf.at[lax.rem(q, ratio), lax.div(q, ratio)]))
    wait_all(loads)
    _, _, count, zb, half = buf.shape
    ny = field.shape[2]
    yb = ny // shots
    lanes = LANES // yb
    slot_of = lax.broadcasted_iota(jnp.int32, (zb, LANES), 1) // yb
    for sub in range(ratio):
        for p in range(count):
            cores = [sum(buf[sub, s, p] for s in range(core, shots, 2)) for core in (0, 1)]
            for t in range(ny // LANES):
                value = None
                for e in range(lanes):
                    core, place = (t * lanes + e) % 2, (t * lanes + e) // 2
                    low = place // lanes * LANES
                    piece = cores[core][:, low : low + LANES]
                    if e != place % lanes:
                        piece = pltpu.roll(piece, (e - place % lanes) * yb % LANES, 1)
                    value = piece if value is None else jnp.where(slot_of == e, piece, value)
                field[sub * count + p, :, pl.ds(t * LANES, LANES)] = value


def gather_kernel(ratio, shots, *refs):
    parts, (y_high, y_low, out, buf, field, sems) = refs[:-6], refs[-6:]
    gather_planes(ratio, shots, parts, buf, field, sems)
    filter_second(field, out, y_high[...], y_low[...])


def filter_second(field, out, high_t, low_t):
    total, zb, ny = field.shape
    step = max(1, 256 // zb)
    while total % step:
        step -= 1
    for i in range(0, total, step):
        high, low = split(field[i : i + step].reshape(step * zb, ny))
        result = dot_t(high, high_t) + dot_t(low, high_t) + dot_t(high, low_t)
        out[i : i + step] = result.reshape(step, zb, ny)


def gather(parts, tables, ratio, shots):
    pieces = len(parts)
    count, zb, _ = parts[0].shape
    ny = tables[0].shape[0]
    total = ratio * count * (LANES * shots // ny)
    return pl.pallas_call(
        functools.partial(gather_kernel, ratio, shots),
        out_shape=held(total, zb, ny),
        in_specs=[VMEM] * (pieces + 2),
        out_specs=VMEM,
        scratch_shapes=[
            pltpu.VMEM((ratio, shots, count, zb, LANES), F32),
            pltpu.VMEM((total, zb, ny), F32),
            pltpu.SemaphoreType.DMA((pieces,)),
        ],
        compiler_params=cheap(16),
        cost_estimate=LONG,
        name="gather",
    )(*parts, *tables)


def scan_kernel(planes, rows, ratio, shots, scan, mains, *refs):
    refs, (buf, field, edges, ends, sems) = refs[:-5], refs[-5:]
    parts, (y_high, y_low, out), sends = refs[: -shots - 2], refs[-shots - 2 : -shots + 1], refs[-shots + 1 :]
    gather_halves(ratio, shots, parts, buf, edges, sems)
    filter_second(edges, edges, y_high[...], y_low[...])
    shot = lax.axis_index("shot")
    total, zb, ny = field.shape
    per_slab = len(planes)
    for sub in range(ratio):
        for i, x in enumerate(planes):
            field[sub * rows + x] = mains[sub * per_slab + i]
        even = lax.rem(shot * ratio + sub, 2) == 0
        for s, base in enumerate((jnp.where(even, rows - REACH, 0), jnp.where(even, 0, rows - REACH))):
            for q in range(REACH):
                field[sub * rows + base + q] = edges[sub * 2 * REACH + s * REACH + q]
    first_x = shot * total

    def up(x, carry):
        carry = field[x] + scan[1, first_x + x] * carry
        out[x] = carry
        return carry

    ends[0] = lax.fori_loop(0, total, up, jnp.zeros((zb, ny), F32))

    def down(i, carry):
        x = total - 1 - i
        out[x] = (out[x] + carry) * scan[0, first_x + x]
        return scan[2, first_x + x - 1] * (field[x] + carry)

    carry = lax.fori_loop(0, total - 1, down, jnp.zeros((zb, ny), F32))
    out[0] = (out[0] + carry) * scan[0, first_x]
    ends[1] = field[0] + carry
    for j, send in enumerate(sends, 1):
        send[...] = jnp.where((shot ^ j) > shot, ends[0], ends[1])


def scan_first(scan, mains, parts, tables, planes, rows, shots):
    per_slab = len(planes)
    ratio = mains.shape[0] // per_slab
    _, zb, ny = mains.shape
    end = held(zb, ny)
    total = rows * ratio
    pieces, count = len(parts), parts[0].shape[0]
    return pl.pallas_call(
        functools.partial(scan_kernel, planes, rows, ratio, shots),
        out_shape=(held(total, zb, ny),) + (end,) * (shots - 1),
        in_specs=[SMEM] + [VMEM] * (pieces + 3),
        out_specs=(VMEM,) * shots,
        scratch_shapes=[
            pltpu.VMEM((ratio, shots, count, zb, ny // 2), F32),
            pltpu.VMEM((total, zb, ny), F32),
            pltpu.VMEM((2 * REACH * ratio, zb, ny), F32),
            pltpu.VMEM((2, zb, ny), F32),
            pltpu.SemaphoreType.DMA((pieces,)),
        ],
        compiler_params=cheap(16),
        cost_estimate=COST,
        name="scan",
    )(scan, mains, *parts, *tables)


def join_kernel(shots, scan, carry, part, *refs):
    ends, out = refs[: shots - 1], refs[shots]
    total, zb, ny = part.shape
    shot = lax.axis_index("shot")
    first_x = shot * total
    below = jnp.zeros((zb, ny), F32)
    above = jnp.zeros((zb, ny), F32)
    for j, end in enumerate(ends, 1):
        other = shot ^ j
        term = carry[shot, other] * end[...]
        below += jnp.where(other < shot, term, 0.0)
        above += jnp.where(other > shot, term, 0.0)
    for x in range(total):
        out[x] = part[x] + scan[3, first_x + x] * below + scan[4, first_x + x] * above


def join(scan, carry, part, ends, after):
    total, zb, ny = part.shape
    shots = len(ends) + 1
    return pl.pallas_call(
        functools.partial(join_kernel, shots),
        out_shape=jax.ShapeDtypeStruct((total, zb, ny), F32),
        in_specs=[SMEM] * 2 + [VMEM] * shots + [ANY],
        out_specs=VMEM,
        compiler_params=cheap(16),
        cost_estimate=COST,
        name="join",
    )(scan, carry, part, *ends, *in_hbm((after,)))


def neighbours(count, start):
    low = range(start, count - 1, 2)
    return [(i, i + 1) for i in low] + [(i + 1, i) for i in low]


def swap(values):
    count = lax.axis_size("mp")
    return keep_held(lax.ppermute(v, "mp", neighbours(count, start)) for start, v in enumerate(values))


def flip(value, bit):
    count = lax.axis_size("shot")
    got = lax.ppermute(value, "shot", [(i, i ^ bit) for i in range(count)])
    return keep_held((got,))[0]


def share(terms, step):
    return [terms[0]] + [flip(term, step * i) for i, term in enumerate(terms[1:], 1)]


def spread(pieces, ratio):
    mp, shots = lax.axis_size("mp"), lax.axis_size("shot")
    out = []
    for k, piece in enumerate(pieces):
        pairs = []
        for m in range(mp):
            for s in range(shots):
                target = (s * ratio + m % ratio + k) % mp
                pairs.append((m * shots + s, target * shots + m // ratio))
        out.append(lax.ppermute(piece, ("mp", "shot"), pairs))
    return keep_held(out)


def per_device(
    courant, forward_old, forward_now, adjoint_late, adjoint_now,
    src_cell, src_sign, wavelet, rec_cell, rec_data,
):
    mp_count, shots = lax.axis_size("mp"), lax.axis_size("shot")
    rows, ny, nz = courant.shape
    ratio = mp_count // shots
    full_x = rows * mp_count
    band_y, band_z = band(ny), band(nz)
    bands = (jnp.asarray(band_y, BF16), jnp.asarray(np.concatenate([band_z, band_z]), BF16))
    strength = float(SMOOTH_YZ * SMOOTH_YZ)
    strength_x = float(SMOOTH_X * SMOOTH_X)
    scan, carry = scan_tables(full_x, strength_x, rows * ratio)
    kappa = 1.0
    for length, e in ((full_x, strength_x), (ny, strength), (nz, strength)):
        resp = response(length, e)
        kappa /= math.sqrt(np.mean(resp * resp))
    z_tables = split_table(filter_matrix(nz, strength))
    y_tables = split_table(kappa * filter_matrix(ny, strength))

    f_old, f_now, a_late, a_now = forward_old[0], forward_now[0], adjoint_late[0], adjoint_now[0]
    halos = swap(pick(f_now, a_now))
    c, accel, nxt, mid, a_base, src, *inner = step_one(
        src_cell, src_sign, wavelet, rec_cell, rec_data, courant, f_old, f_now, a_late, a_now, bands, shots
    )
    accel, nxt, mid, a_base, edge0, edge1 = correct(c, accel, nxt, mid, a_base, halos)
    halos = swap((edge0, edge1))
    inner = share(inner, 1)
    edge, by_f, by_a, *outer = step_two((c, accel, nxt, mid, a_base, src), bands, (), shots)
    inner, outer = add_up(inner, outer)
    outer = share(outer, 1)
    near, keep = finish(edge, by_f, by_a, halos, shots)
    raw_shape = (rows, ny // shots, nz)
    layout = [[(2 * REACH, rows - 4 * REACH)], [(REACH, REACH), (rows - 2 * REACH, REACH)]]
    terms = [[(term, 0) for term in chunk] for chunk in ((inner,), outer)]
    raw, *mains = depth(layout, terms, z_tables, raw_shape, mp_count)
    mains = gather(spread(mains, ratio), y_tables, ratio, shots)
    last, edges = depth_edge(keep, flip(near, 1), z_tables, mp_count)
    raw = raw_edge(share(last, 2), raw)
    edges = spread(edges, ratio)
    planes = [low + i for chunk in layout for low, count in chunk for i in range(count)]
    part, *ends = scan_first(jnp.asarray(scan), mains, edges, y_tables, planes, rows, shots)
    ends = [flip(end, j) for j, end in enumerate(ends, 1)]
    smooth = join(jnp.asarray(scan), jnp.asarray(carry), part, ends, raw)
    smooth = jnp.transpose(smooth, (0, 2, 1))
    return raw, smooth


def solution(mesh):
    return jax.shard_map(
        per_device,
        mesh=mesh,
        in_specs=(
            P(("parts", "mp"), None, None),
            P(("parts", "shot"), "mp", None, None),
            P(("parts", "shot"), "mp", None, None),
            P(("parts", "shot"), "mp", None, None),
            P(("parts", "shot"), "mp", None, None),
            P(("parts", "shot"), None),
            P(("parts", "shot"), None),
            P(("parts", "shot"), None, None),
            P("parts"),
            P(("parts", "shot"), None, None),
        ),
        out_specs=(P(("parts", "mp"), "shot", None), P(("parts", "shot"), None, "mp")),
        check_vma=False,
    )
```

```python
import functools
import math

import jax
import jax.numpy as jnp
import ml_dtypes
import numpy as np
from jax import lax
from jax.experimental import pallas as pl
from jax.experimental.pallas import tpu as pltpu
from jax.sharding import PartitionSpec as P

SMOOTH_X = 32
SMOOTH_YZ = 4

COEFS = (8.0 / 5.0, -1.0 / 5.0, 8.0 / 315.0, -1.0 / 560.0)
CENTER = -205.0 / 72.0
REACH = len(COEFS)
SCALE = 5040.0
WHOLE = tuple(float(round(SCALE * a)) for a in COEFS)

LANES = 128
BF16 = jnp.bfloat16
F32 = jnp.float32
ANY = pl.BlockSpec(memory_space=pl.ANY)
VMEM = pl.BlockSpec(memory_space=pltpu.VMEM)
SMEM = pl.BlockSpec(memory_space=pltpu.SMEM)


def band(length):
    table = np.zeros((length, length), np.float32)
    for k, weight in enumerate(WHOLE, 1):
        near = np.arange(length - k)
        table[near, near + k] = weight
        table[near + k, near] = weight
    return table


def response(length, strength):
    counter = np.arange(1, length + 1, dtype=np.float64)
    half_sine = np.sin(np.pi * counter / (2 * (length + 1)))
    return 1.0 / (1.0 + strength * 4.0 * half_sine * half_sine)


def filter_matrix(length, strength):
    counter = np.arange(1, length + 1, dtype=np.float64)
    table = np.sin(np.pi * counter[:, None] * counter[None, :] / (length + 1))
    return 2.0 / (length + 1) * (table * response(length, strength)[None, :]) @ table


def scan_tables(length, strength, block):
    rate = math.acosh(1.0 + 0.5 / strength)
    index = np.arange(1, length + 1, dtype=np.float64)
    rise = np.sinh(rate * index)
    fall = np.sinh(rate * (length + 1 - index))
    whole = strength * math.sinh(rate) * math.sinh(rate * (length + 1))
    diag = rise * fall / whole
    left = np.concatenate([[0.0], rise[:-1] / rise[1:]])
    right = np.concatenate([fall[1:] / fall[:-1], [0.0]])
    first = (np.arange(length) // block) * block
    last = first + block - 1
    from_left = np.where(first > 0, rise[np.maximum(first - 1, 0)], 0.0) / rise
    from_right = np.where(last + 1 < length, fall[np.minimum(last + 1, length - 1)], 0.0) / fall
    rows = np.stack([diag, left, right, diag * from_left, diag * from_right])
    blocks = length // block
    carry = np.zeros((blocks, blocks))
    for here in range(blocks):
        for there in range(blocks):
            if there < here:
                carry[here, there] = rise[there * block + block - 1] / rise[here * block - 1]
            elif there > here:
                carry[here, there] = fall[there * block] / fall[here * block + block]
    return rows.astype(np.float32), carry.astype(np.float32)


def split_table(table):
    high = table.astype(np.float32).astype(ml_dtypes.bfloat16)
    low = (table - high.astype(np.float64)).astype(np.float32).astype(ml_dtypes.bfloat16)
    return jnp.asarray(high), jnp.asarray(low)


def split(value):
    high = value.astype(BF16)
    low = (value - high.astype(F32)).astype(BF16)
    return high, low


def dot(a, b):
    return jnp.dot(a, b, preferred_element_type=F32)


def dot_t(a, b):
    return lax.dot_general(a, b, (((1,), (1,)), ((), ())), preferred_element_type=F32)


def laplace_plane(field, p, band_y, band_z):
    here = field[p]
    width = here.shape[1]
    both = jnp.concatenate(split(here), axis=1)
    along_y = dot(band_y[...], both)
    along_z = dot(both, band_z[...])
    total = (3.0 * SCALE * CENTER) * here
    for k, weight in enumerate(WHOLE, 1):
        total += weight * (field[p + k] + field[p - k])
    return total + (along_y[:, :width] + along_y[:, width:]) + along_z


def divmod_fixed(value, size):
    if size & (size - 1) == 0:
        return lax.shift_right_logical(value, size.bit_length() - 1), value & (size - 1)
    return lax.div(value, size), lax.rem(value, size)


class Copies:
    def __init__(self, sems):
        self.sems, self.used = sems, 0

    def start(self, source, target):
        copy = pltpu.make_async_copy(source, target, self.sems.at[self.used])
        self.used += 1
        copy.start()
        return copy


def wait_all(copies):
    for copy in copies:
        copy.wait()


def chunk_bounds(rows):
    step = max(2 * REACH, -(-rows // 3))
    return [(low, min(low + step, rows)) for low in range(0, rows, step)]


def put_blocks(copies, buf, planes, shot, outs):
    return [copies.start(buf.at[planes, shot ^ j], out) for j, out in enumerate(outs)]


def step_one_kernel(
    src_cell, src_sign, wavelet, rec_tile, data_tile,
    courant, f_old, f_now, a_late, a_now, band_y, band_z,
    c_buf, acc_buf, f_next, a_mid, a_base, s_second,
    *refs,
):
    terms_out = refs[:-15]
    (
        f_pad, a_pad, s_first, r_first, r_second, gt_buf,
        place_buf, value_buf, count_buf, places, values, counts, list_sems, term_sems, sems,
    ) = refs[-15:]
    rows, ny, nz = courant.shape
    copies = Copies(sems)
    bounds = chunk_bounds(rows)

    def chunks(source, target, offset=0):
        return [
            copies.start(source.at[pl.ds(low, high - low)], target.at[pl.ds(low + offset, high - low)])
            for low, high in bounds
        ]

    loads = [chunks(f_now, f_pad, REACH), chunks(courant, c_buf), chunks(f_old, f_next, REACH)]
    late_loads = [chunks(a_now, a_pad, REACH), chunks(a_late, a_mid, REACH)]
    edge = jnp.zeros((REACH, ny, nz), F32)
    for pad in (f_pad, a_pad, f_next, a_mid):
        pad[:REACH] = edge
        pad[REACH + rows :] = edge

    group = ny // 8

    def clear(p, _):
        blank = jnp.zeros((group, 8, nz), F32)
        for ref in (s_first, r_first, s_second, r_second):
            ref[pl.ds(p * group, group)] = blank
        return 0

    lax.fori_loop(0, rows, clear, 0)

    size = rows * ny * nz
    start = lax.axis_index("mp") * size
    flat = lax.broadcasted_iota(jnp.int32, (8, nz), 0) * nz + lax.broadcasted_iota(jnp.int32, (8, nz), 1)

    def put(refs, local, values):
        tile, within = divmod_fixed(local, 8 * nz)
        spot = flat == within
        for ref, value in zip(refs, values, strict=True):
            ref[tile] = ref[tile] + jnp.where(spot, value, 0.0)

    nsrc = src_cell.shape[1]

    def one_source(i, _):
        local = src_cell[0, i] - start
        mine = (local >= 0) & (local < size)
        local = jnp.where(mine, local, 0)
        sign = jnp.where(mine, (2 * src_sign[0, i] - 1).astype(F32), 0.0)
        put((s_first, s_second), local, (sign * wavelet[0, 0, i], sign * wavelet[0, 1, i]))
        return 0

    lax.fori_loop(0, nsrc, one_source, 0, unroll=8 if nsrc % 8 == 0 else 1)


    tiles = rec_tile.shape[0]
    local = rec_tile[...] - start
    inside = (local >= 0) & (local < size)
    marks = jnp.where(inside, 1.0, 0.0).astype(BF16)
    row, col = (lax.broadcasted_iota(jnp.int32, (LANES, LANES), d) for d in (0, 1))
    before = jnp.where(inside, dot(marks, jnp.where(row < col, 1.0, 0.0).astype(BF16)).astype(jnp.int32), -1)
    thirds = []
    for value in (jnp.where(inside, local, 0).astype(F32), data_tile[0], data_tile[1]):
        for _ in range(3):
            part = value.astype(BF16)
            value = value - part.astype(F32)
            thirds.append(part)
    for t in range(tiles):
        moves = jnp.where(row == before[t : t + 1], 1.0, 0.0).astype(BF16)
        stacked = jnp.concatenate([part[t : t + 1] for part in thirds] + [thirds[0][:7]], axis=0)
        moved = dot_t(stacked, moves)
        place_buf[t : t + 1] = (moved[0:1] + moved[1:2] + moved[2:3]).astype(jnp.int32)
        value_buf[0, t : t + 1] = moved[3:4] + moved[4:5] + moved[5:6]
        value_buf[1, t : t + 1] = moved[6:7] + moved[7:8] + moved[8:9]
    count_buf[...] = dot(marks, jnp.ones((LANES, LANES), BF16)).astype(jnp.int32)
    fetches = [
        pltpu.make_async_copy(source, target, list_sems.at[i])
        for i, (source, target) in enumerate(((place_buf, places), (value_buf, values), (count_buf, counts)))
    ]
    for fetch in fetches:
        fetch.start()
    wait_all(fetches)

    def receivers(t, _):
        def some(g, _):
            items = []
            for e in range(8):
                i = g * 8 + e
                items.append((places[t, i], values[0, t, i], values[1, t, i]))
            for place, first, second in items:
                put((r_first, r_second), place, (first, second))
            return 0

        return lax.fori_loop(0, lax.div(counts[t, 0] + 7, 8), some, 0)

    lax.fori_loop(0, tiles, receivers, 0)

    def forward(p, _):
        courant_here = c_buf[p] * (1.0 / SCALE)
        c_buf[p] = courant_here
        spike = s_first[pl.ds(p * group, group)].reshape(ny, nz)
        accel = courant_here * laplace_plane(f_pad, p + REACH, band_y, band_z) + spike
        acc_buf[p] = accel
        f_next[p + REACH] = (2.0 * f_pad[p + REACH] - f_next[p + REACH]) + accel
        return 0

    for group_loads in loads:
        wait_all(group_loads)
    lax.fori_loop(0, rows, forward, 0, unroll=2)

    def adjoint(p, _):
        spike = r_first[pl.ds(p * group, group)].reshape(ny, nz)
        change = c_buf[p] * laplace_plane(a_pad, p + REACH, band_y, band_z) + spike
        mid = (2.0 * a_pad[p + REACH] - a_mid[p + REACH]) + change
        a_mid[p + REACH] = mid
        later = r_second[pl.ds(p * group, group)].reshape(ny, nz)
        a_base[p] = (2.0 * mid - a_pad[p + REACH]) + later
        return 0

    for group_loads in late_loads:
        wait_all(group_loads)
    lax.fori_loop(0, rows, adjoint, 0, unroll=2)

    blocks = gt_buf.shape[1]

    def inner(i, _):
        p = i + 2 * REACH
        c = c_buf[p]
        here = pl.ds(p * group, group)
        accel = c * laplace_plane(f_next, p + REACH, band_y, band_z) + s_second[here].reshape(ny, nz)
        first = a_base[p] + c * laplace_plane(a_mid, p + REACH, band_y, band_z)
        gt_buf[i] = (first * acc_buf[p] + a_mid[p + REACH] * accel).reshape(blocks, ny // blocks, nz)
        return 0

    lax.fori_loop(0, rows - 4 * REACH, inner, 0, unroll=2)
    wait_all(put_blocks(Copies(term_sems), gt_buf, slice(None), lax.axis_index("shot"), terms_out))


def cheap(megabytes):
    return pltpu.CompilerParams(vmem_limit_bytes=megabytes * 2**20)


COST = pl.CostEstimate(flops=1000, bytes_accessed=1000, transcendentals=0)
LONG = pl.CostEstimate(flops=10**12, bytes_accessed=1000, transcendentals=0)


def held(*shape):
    return pltpu.VMEM(shape, F32)


def in_hbm(arrays):
    return [pltpu.with_memory_space_constraint(array, pltpu.HBM) for array in arrays]


def keep_held(arrays):
    return [pltpu.with_memory_space_constraint(array, pltpu.VMEM) for array in arrays]


def step_one(src_cell, src_sign, wavelet, rec_cell, rec_data, courant, f_old, f_now, a_late, a_now, bands, shots):
    rows, ny, nz = courant.shape
    term = held(rows - 4 * REACH, ny // shots, nz)
    whole, padded, sparse = (rows, ny, nz), (rows + 2 * REACH, ny, nz), (rows * ny // 8, 8, nz)
    tiles = rec_cell.shape[0] // LANES
    return pl.pallas_call(
        step_one_kernel,
        out_shape=tuple(held(*shape) for shape in (whole, whole, padded, padded, whole, sparse)) + (term,) * shots,
        in_specs=[SMEM] * 3 + [VMEM] * 2 + [ANY] * 5 + [VMEM] * 2,
        out_specs=(VMEM,) * (6 + shots),
        scratch_shapes=[
            held(*padded), held(*padded), held(*sparse), held(*sparse), held(*sparse),
            held(rows - 4 * REACH, shots, ny // shots, nz),
            pltpu.VMEM((tiles, LANES), jnp.int32),
            pltpu.VMEM((2, tiles, LANES), F32),
            pltpu.VMEM((tiles, LANES), jnp.int32),
            pltpu.SMEM((tiles, LANES), jnp.int32),
            pltpu.SMEM((2, tiles, LANES), F32),
            pltpu.SMEM((tiles, LANES), jnp.int32),
            pltpu.SemaphoreType.DMA((3,)),
            pltpu.SemaphoreType.DMA((shots,)),
            pltpu.SemaphoreType.DMA((5 * len(chunk_bounds(rows)),)),
        ],
        compiler_params=cheap(24),
        cost_estimate=LONG,
        name="step_one",
    )(
        src_cell, src_sign, wavelet, rec_cell.reshape(-1, LANES), rec_data.reshape(2, -1, LANES),
        *in_hbm((courant, f_old, f_now, a_late, a_now)), *bands,
    )


def sides(rows):
    even = lax.rem(lax.axis_index("mp"), 2) == 0
    high = rows - REACH
    return (jnp.where(even, high, 0), even), (jnp.where(even, 0, high), jnp.logical_not(even))


STRIP = 32


def halo_sums(halo, upper):
    planes = [halo(jnp.where(upper, h, REACH - 1 - h)) for h in range(REACH)]
    return [sum(WHOLE[h + REACH - q - 1] * planes[h] for h in range(q + 1)) for q in range(REACH)]


def strips(count, body):
    def step(i, _):
        body(pl.ds(pl.multiple_of(i * STRIP, STRIP), STRIP))
        return 0

    lax.fori_loop(0, count // STRIP, step, 0)


def pick_kernel(f_now, a_now, *refs):
    outs, sems = refs[:2], refs[2]
    copies = Copies(sems)
    wait_all([
        copies.start(field.at[pl.ds(base, REACH)], outs[s].at[i])
        for s, (base, _) in enumerate(sides(f_now.shape[0]))
        for i, field in enumerate((f_now, a_now))
    ])


def pick(f_now, a_now):
    _, ny, nz = f_now.shape
    both = held(2, REACH, ny, nz)
    return pl.pallas_call(
        pick_kernel,
        out_shape=(both, both),
        in_specs=[ANY] * 2,
        out_specs=(VMEM,) * 2,
        scratch_shapes=[pltpu.SemaphoreType.DMA((4,))],
        compiler_params=cheap(8),
        cost_estimate=COST,
        name="pick",
    )(*in_hbm((f_now, a_now)))


def correct_kernel(
    c_buf, acc_in, next_in, mid_in, base_in, halo0, halo1, acc_buf, f_next, a_mid, a_base, edge0, edge1,
    halo_buf, edge_buf, sems,
):
    rows, ny, _ = c_buf.shape
    copies = Copies(sems)
    step = max(STRIP, ny // 4)
    parts = [slice(low, low + step) for low in range(0, ny, step)]
    loads = [
        [copies.start(halo.at[:, :, part], halo_buf.at[s, :, :, part]) for s, halo in enumerate((halo0, halo1))]
        for part in parts
    ]

    def strip(i, _):
        part = pl.ds(pl.multiple_of(i * STRIP, STRIP), STRIP)
        for s, (base, upper) in enumerate(sides(rows)):
            forward = halo_sums(lambda h, s=s: halo_buf[s, 0, h, part], upper)
            adjoint = halo_sums(lambda h, s=s: halo_buf[s, 1, h, part], upper)
            for q in range(REACH):
                place = jnp.where(upper, q, REACH - 1 - q)
                here = base + place
                c = c_buf[here, part]
                change = c * forward[q]
                acc_buf[here, part] = acc_in[here, part] + change
                value = next_in[here + REACH, part] + change
                f_next[here + REACH, part] = value
                edge_buf[s, 0, place, part] = value
                change = c * adjoint[q]
                value = mid_in[here + REACH, part] + change
                a_mid[here + REACH, part] = value
                edge_buf[s, 1, place, part] = value
                a_base[here, part] = base_in[here, part] + 2.0 * change
        return 0

    stores = []
    for part, group in zip(parts, loads, strict=True):
        wait_all(group)
        lax.fori_loop(part.start // STRIP, part.stop // STRIP, strip, 0)
        for s, edge in enumerate((edge0, edge1)):
            stores.append(copies.start(edge_buf.at[s, :, :, part], edge.at[:, :, part]))
    wait_all(stores)


def correct(c, accel, nxt, mid, a_base, halos):
    rows, ny, nz = c.shape
    both = held(2, REACH, ny, nz)
    return pl.pallas_call(
        correct_kernel,
        out_shape=tuple(held(*array.shape) for array in (accel, nxt, mid, a_base)) + (both, both),
        in_specs=[VMEM] * 5 + [ANY] * 2,
        out_specs=(VMEM,) * 4 + (ANY,) * 2,
        scratch_shapes=[
            held(2, 2, REACH, ny, nz), held(2, 2, REACH, ny, nz),
            pltpu.SemaphoreType.DMA((4 * len(range(0, ny, max(STRIP, ny // 4))),)),
        ],
        input_output_aliases={1: 0, 2: 1, 3: 2, 4: 3},
        compiler_params=cheap(8),
        cost_estimate=COST,
        name="correct",
    )(*keep_held((c, accel, nxt, mid, a_base)), *halos)


def step_two_kernel(waits, c_buf, acc_buf, f_next, a_mid, a_base, s_buf, band_y, band_z, *refs):
    edge_out, by_f, by_a, *terms_out, gt_buf, sems = refs[waits:]
    rows, ny, nz = c_buf.shape
    copies = Copies(sems)
    group = ny // 8
    blocks = gt_buf.shape[1]

    def plane(p, _):
        c = c_buf[p]
        here = pl.ds(p * group, group)
        mid = a_mid[p + REACH]
        accel = c * laplace_plane(f_next, p + REACH, band_y, band_z) + s_buf[here].reshape(ny, nz)
        first = a_base[p] + c * laplace_plane(a_mid, p + REACH, band_y, band_z)
        gt_buf[p] = (first * acc_buf[p] + mid * accel).reshape(blocks, ny // blocks, nz)
        return 0

    def inner(i, _):
        return plane(jnp.where(i < REACH, i + REACH, i + rows - 3 * REACH), 0)

    lax.fori_loop(0, 2 * REACH, inner, 0, unroll=2)
    stores = []
    for i, low in enumerate((REACH, rows - 2 * REACH)):
        outs = [out.at[pl.ds(i * REACH, REACH)] for out in terms_out]
        stores += put_blocks(copies, gt_buf, pl.ds(low, REACH), lax.axis_index("shot"), outs)

    bases = [base for base, _ in sides(rows)]

    def outer(i, _):
        s, q = lax.div(i, REACH), lax.rem(i, REACH)
        p = jnp.where(s == 0, bases[0], bases[1]) + q
        plane(p, 0)
        c = c_buf[p]
        by_f[s, q] = c * a_mid[p + REACH]
        by_a[s, q] = c * acc_buf[p]
        edge_out[s, q] = gt_buf[p].reshape(ny, nz)
        return 0

    lax.fori_loop(0, 2 * REACH, outer, 0, unroll=2)
    wait_all(stores)


def step_two(arrays, bands, after, shots):
    rows, ny, nz = arrays[0].shape
    edge = held(2, REACH, ny, nz)
    term = held(2 * REACH, ny // shots, nz)
    return pl.pallas_call(
        functools.partial(step_two_kernel, len(after)),
        out_shape=(edge, edge, edge) + (term,) * shots,
        in_specs=[VMEM] * (8 + len(after)),
        out_specs=(VMEM,) * (3 + shots),
        scratch_shapes=[held(rows, shots, ny // shots, nz), pltpu.SemaphoreType.DMA((2 * shots,))],
        compiler_params=cheap(12),
        cost_estimate=LONG,
        name="step_two",
    )(*keep_held(arrays), *bands, *after)


def add_up_kernel(shots, *refs):
    terms, out = refs[:shots], refs[2 * shots]
    total = terms[0][...]
    for term in terms[1:]:
        total += term[...]
    out[...] = total


def add_up(terms, passed):
    shots = len(terms)
    outs = pl.pallas_call(
        functools.partial(add_up_kernel, shots),
        out_shape=tuple(held(*array.shape) for array in (terms[0], *passed)),
        in_specs=[VMEM] * shots + [ANY] * shots,
        out_specs=(VMEM,) + (ANY,) * shots,
        input_output_aliases={shots + i: 1 + i for i in range(shots)},
        compiler_params=cheap(8),
        cost_estimate=COST,
        name="add_up",
    )(*keep_held((*terms, *passed)))
    return outs[0], outs[1:]


def finish_kernel(edge, by_f, by_a, halo0, halo1, near_out, keep_out, halo_buf, near_buf, sems):
    _, blocks, yb, _ = near_out.shape
    copies = Copies(sems)
    bit = lax.rem(lax.axis_index("shot"), 2)
    width = math.gcd(yb, STRIP)
    jobs = []
    for out, mine in ((near_buf, 1 - bit), (keep_out, bit)):
        for j in range(blocks):
            low = pl.multiple_of((2 * j + mine) * yb, yb)
            here = pl.ds(low, yb)
            loads = [
                copies.start(halo.at[:, :, here], halo_buf.at[s, :, :, here]) for s, halo in enumerate((halo0, halo1))
            ]
            jobs.append((out, j, low, loads))
    stores = []
    for out, j, low, loads in jobs:
        wait_all(loads)

        def strip(i, _, out=out, j=j, low=low):
            inside = pl.ds(pl.multiple_of(i * width, width), width)
            part = pl.ds(pl.multiple_of(low + i * width, width), width)
            for s, (_, upper) in enumerate(sides(2 * REACH)):
                forward = halo_sums(lambda h, s=s: halo_buf[s, 0, h, part], upper)
                adjoint = halo_sums(lambda h, s=s: halo_buf[s, 1, h, part], upper)
                for q in range(REACH):
                    place = jnp.where(upper, q, REACH - 1 - q)
                    total = edge[s, place, part] + by_f[s, place, part] * forward[q]
                    out[s * REACH + place, j, inside] = total + by_a[s, place, part] * adjoint[q]
            return 0

        lax.fori_loop(0, yb // width, strip, 0)
        if out is near_buf:
            stores.append(copies.start(near_buf.at[:, j], near_out.at[:, j]))
    wait_all(stores)


def finish(edge, by_f, by_a, halos, shots):
    _, reach, ny, nz = edge.shape
    half = held(2 * reach, shots // 2, ny // shots, nz)
    return pl.pallas_call(
        finish_kernel,
        out_shape=(half, half),
        in_specs=[VMEM] * 3 + [ANY] * 2,
        out_specs=(ANY, VMEM),
        scratch_shapes=[
            held(2, 2, reach, ny, nz),
            held(*half.shape),
            pltpu.SemaphoreType.DMA((shots * 2 + shots // 2,)),
        ],
        compiler_params=cheap(16),
        cost_estimate=LONG,
        name="finish",
    )(edge, by_f, by_a, *halos)


def depth_kernel(layout, parts, pieces, *refs):
    used = sum(len(offsets) for offsets in parts)
    terms, refs = refs[:used], refs[used:]
    z_high, z_low = refs[:2]
    raw_out, outs, (raw_buf, spectrum, sems) = refs[-pieces - 4], refs[-pieces - 3 : -3], refs[-3:]
    planes, yb, nz = raw_buf.shape
    shots = lax.axis_size("shot")
    copies = Copies(sems)
    low, at = 0, 0
    for chunk, offsets in zip(layout, parts, strict=True):
        size = sum(count for _, count in chunk)
        total = None
        for offset in offsets:
            term = terms[at][offset : offset + size]
            total = term if total is None else total + term
            at += 1
        raw_buf[low : low + size] = total / shots
        low += size
    stores, done = [], 0
    rows = raw_out.shape[0]
    for chunk in layout:
        for where, count in chunk:
            base = sides(rows)[where][0] if isinstance(where, bool) else where
            stores.append(copies.start(raw_buf.at[pl.ds(done, count)], raw_out.at[pl.ds(base, count)]))
            done += count
    lanes = LANES // yb
    count = planes // lanes
    zb = nz // pieces

    def turn(p, _):
        rows_here = jnp.concatenate([raw_buf[h * count + p] for h in range(lanes)], axis=0)
        high, low_part = split(rows_here)
        table = z_high[...]
        spectrum[p] = (dot_t(table, high) + dot_t(table, low_part) + dot_t(z_low[...], high)).reshape(pieces, zb, LANES)
        return 0

    lax.fori_loop(0, count, turn, 0, unroll=2)
    offset = piece_offset()
    for k, out in enumerate(outs):
        out[...] = spectrum[:, lax.rem(offset + k, pieces)]
    wait_all(stores)


def depth(layout, terms, tables, raw_shape, pieces, after=(), previous=None):
    planes = sum(count for chunk in layout for _, count in chunk)
    _, yb, nz = raw_shape
    lanes = LANES // yb
    count = planes // lanes
    piece = held(count, nz // pieces, LANES)
    extra = (*after, *(() if previous is None else (previous,)))
    flat = [term for chunk in terms for term, _ in chunk]
    offsets = [[offset for _, offset in chunk] for chunk in terms]
    last = len(flat) + 2 + len(extra) - 1
    return pl.pallas_call(
        functools.partial(depth_kernel, layout, offsets, pieces),
        out_shape=(jax.ShapeDtypeStruct(raw_shape, F32),) + (piece,) * pieces,
        in_specs=[VMEM] * (len(flat) + 2) + [ANY] * len(extra),
        out_specs=(ANY,) + (VMEM,) * pieces,
        scratch_shapes=[
            pltpu.VMEM((planes, yb, nz), F32),
            pltpu.VMEM((count, pieces, nz // pieces, LANES), F32),
            pltpu.SemaphoreType.DMA((sum(len(chunk) for chunk in layout),)),
        ],
        input_output_aliases={} if previous is None else {last: 0},
        compiler_params=cheap(16),
        cost_estimate=LONG,
        name="depth",
    )(*flat, *tables, *extra)


def piece_offset():
    ratio = lax.axis_size("mp") // lax.axis_size("shot")
    return lax.axis_index("shot") * ratio + lax.rem(lax.axis_index("mp"), ratio)


def depth_edge_kernel(pieces, keep, near, z_high, z_low, own, *refs):
    far, outs, (total, spectrum) = refs[: -pieces - 2], refs[-pieces - 2 : -2], refs[-2:]
    planes, blocks, yb, nz = keep.shape
    total[...] = (keep[...] + near[...]) / lax.axis_size("shot")
    for i, term in enumerate((own, *far)):
        term[...] = total[:, lax.div(lax.axis_index("shot") ^ (2 * i), 2)]

    def turn(p, _):
        high, low = split(total[p].reshape(blocks * yb, nz))
        table = z_high[...]
        both = dot_t(table, high) + dot_t(table, low) + dot_t(z_low[...], high)
        spectrum[p] = both.reshape(pieces, nz // pieces, blocks * yb)
        return 0

    lax.fori_loop(0, planes, turn, 0, unroll=2)
    for k, out in enumerate(outs):
        out[...] = spectrum[:, lax.rem(piece_offset() + k, pieces)]


def depth_edge(keep, near, tables, pieces):
    planes, blocks, yb, nz = keep.shape
    term = held(planes, yb, nz)
    piece = held(planes, nz // pieces, blocks * yb)
    outs = pl.pallas_call(
        functools.partial(depth_edge_kernel, pieces),
        out_shape=(term,) * blocks + (piece,) * pieces,
        in_specs=[VMEM] * 4,
        out_specs=(VMEM,) * (blocks + pieces),
        scratch_shapes=[
            pltpu.VMEM(keep.shape, F32),
            pltpu.VMEM((planes, pieces, nz // pieces, blocks * yb), F32),
        ],
        compiler_params=cheap(12),
        cost_estimate=LONG,
        name="depth_edge",
    )(keep, near, *tables)
    return outs[:blocks], outs[blocks:]


def raw_edge_kernel(*refs):
    terms, (raw_out, buf, sems) = refs[:-4], refs[-3:]
    total = terms[0][...]
    for term in terms[1:]:
        total += term[...]
    buf[...] = total
    copies = Copies(sems)
    wait_all([
        copies.start(buf.at[pl.ds(s * REACH, REACH)], raw_out.at[pl.ds(base, REACH)])
        for s, (base, _) in enumerate(sides(raw_out.shape[0]))
    ])


def raw_edge(terms, raw):
    return pl.pallas_call(
        raw_edge_kernel,
        out_shape=jax.ShapeDtypeStruct(raw.shape, F32),
        in_specs=[VMEM] * len(terms) + [ANY],
        out_specs=ANY,
        scratch_shapes=[pltpu.VMEM(terms[0].shape, F32), pltpu.SemaphoreType.DMA((2,))],
        input_output_aliases={len(terms): 0},
        compiler_params=cheap(8),
        cost_estimate=COST,
        name="raw_edge",
    )(*terms, raw)


def gather_planes(ratio, shots, parts, buf, field, sems):
    pieces = len(parts)
    mp = lax.axis_index("mp")
    copies = Copies(sems)
    loads = []
    for k, part in enumerate(parts):
        q = lax.rem(mp - k + pieces, pieces)
        loads.append(copies.start(part, buf.at[lax.rem(q, ratio), lax.div(q, ratio)]))
    wait_all(loads)
    count = buf.shape[2]
    _, zb, ny = field.shape
    yb = ny // shots
    lanes = LANES // yb
    slot_of = lax.broadcasted_iota(jnp.int32, (zb, LANES), 1) // yb
    for sub in range(ratio):
        for p in range(count):
            for h in range(lanes):
                x = sub * count * lanes + h * count + p
                for t in range(shots // lanes):
                    value = None
                    for e in range(lanes):
                        piece = buf[sub, t * lanes + e, p]
                        if e != h:
                            piece = pltpu.roll(piece, (e - h) * yb % LANES, 1)
                        value = piece if value is None else jnp.where(slot_of == e, piece, value)
                    field[x, :, pl.ds(t * LANES, LANES)] = value


def gather_halves(ratio, shots, parts, buf, field, sems):
    pieces = len(parts)
    copies = Copies(sems)
    loads = []
    for k, part in enumerate(parts):
        q = lax.rem(lax.axis_index("mp") - k + pieces, pieces)
        loads.append(copies.start(part, buf.at[lax.rem(q, ratio), lax.div(q, ratio)]))
    wait_all(loads)
    _, _, count, zb, half = buf.shape
    ny = field.shape[2]
    yb = ny // shots
    lanes = LANES // yb
    slot_of = lax.broadcasted_iota(jnp.int32, (zb, LANES), 1) // yb
    for sub in range(ratio):
        for p in range(count):
            cores = [sum(buf[sub, s, p] for s in range(core, shots, 2)) for core in (0, 1)]
            for t in range(ny // LANES):
                value = None
                for e in range(lanes):
                    core, place = (t * lanes + e) % 2, (t * lanes + e) // 2
                    low = place // lanes * LANES
                    piece = cores[core][:, low : low + LANES]
                    if e != place % lanes:
                        piece = pltpu.roll(piece, (e - place % lanes) * yb % LANES, 1)
                    value = piece if value is None else jnp.where(slot_of == e, piece, value)
                field[sub * count + p, :, pl.ds(t * LANES, LANES)] = value


def gather_kernel(ratio, shots, *refs):
    parts, (y_high, y_low, out, buf, field, sems) = refs[:-6], refs[-6:]
    gather_planes(ratio, shots, parts, buf, field, sems)
    filter_second(field, out, y_high[...], y_low[...])


def filter_second(field, out, high_t, low_t):
    total, zb, ny = field.shape
    step = max(1, 256 // zb)
    while total % step:
        step -= 1
    for i in range(0, total, step):
        high, low = split(field[i : i + step].reshape(step * zb, ny))
        result = dot_t(high, high_t) + dot_t(low, high_t) + dot_t(high, low_t)
        out[i : i + step] = result.reshape(step, zb, ny)


def gather(parts, tables, ratio, shots):
    pieces = len(parts)
    count, zb, _ = parts[0].shape
    ny = tables[0].shape[0]
    total = ratio * count * (LANES * shots // ny)
    return pl.pallas_call(
        functools.partial(gather_kernel, ratio, shots),
        out_shape=held(total, zb, ny),
        in_specs=[VMEM] * (pieces + 2),
        out_specs=VMEM,
        scratch_shapes=[
            pltpu.VMEM((ratio, shots, count, zb, LANES), F32),
            pltpu.VMEM((total, zb, ny), F32),
            pltpu.SemaphoreType.DMA((pieces,)),
        ],
        compiler_params=cheap(16),
        cost_estimate=LONG,
        name="gather",
    )(*parts, *tables)


def scan_kernel(planes, rows, ratio, shots, scan, mains, *refs):
    refs, (buf, field, edges, ends, sems) = refs[:-5], refs[-5:]
    parts, (y_high, y_low, out), sends = refs[: -shots - 2], refs[-shots - 2 : -shots + 1], refs[-shots + 1 :]
    gather_halves(ratio, shots, parts, buf, edges, sems)
    filter_second(edges, edges, y_high[...], y_low[...])
    shot = lax.axis_index("shot")
    total, zb, ny = field.shape
    per_slab = len(planes)
    for sub in range(ratio):
        for i, x in enumerate(planes):
            field[sub * rows + x] = mains[sub * per_slab + i]
        even = lax.rem(shot * ratio + sub, 2) == 0
        for s, base in enumerate((jnp.where(even, rows - REACH, 0), jnp.where(even, 0, rows - REACH))):
            for q in range(REACH):
                field[sub * rows + base + q] = edges[sub * 2 * REACH + s * REACH + q]
    first_x = shot * total

    def up(x, carry):
        carry = field[x] + scan[1, first_x + x] * carry
        out[x] = carry
        return carry

    ends[0] = lax.fori_loop(0, total, up, jnp.zeros((zb, ny), F32))

    def down(i, carry):
        x = total - 1 - i
        out[x] = (out[x] + carry) * scan[0, first_x + x]
        return scan[2, first_x + x - 1] * (field[x] + carry)

    carry = lax.fori_loop(0, total - 1, down, jnp.zeros((zb, ny), F32))
    out[0] = (out[0] + carry) * scan[0, first_x]
    ends[1] = field[0] + carry
    for j, send in enumerate(sends, 1):
        send[...] = jnp.where((shot ^ j) > shot, ends[0], ends[1])


def scan_first(scan, mains, parts, tables, planes, rows, shots):
    per_slab = len(planes)
    ratio = mains.shape[0] // per_slab
    _, zb, ny = mains.shape
    end = held(zb, ny)
    total = rows * ratio
    pieces, count = len(parts), parts[0].shape[0]
    return pl.pallas_call(
        functools.partial(scan_kernel, planes, rows, ratio, shots),
        out_shape=(held(total, zb, ny),) + (end,) * (shots - 1),
        in_specs=[SMEM] + [VMEM] * (pieces + 3),
        out_specs=(VMEM,) * shots,
        scratch_shapes=[
            pltpu.VMEM((ratio, shots, count, zb, ny // 2), F32),
            pltpu.VMEM((total, zb, ny), F32),
            pltpu.VMEM((2 * REACH * ratio, zb, ny), F32),
            pltpu.VMEM((2, zb, ny), F32),
            pltpu.SemaphoreType.DMA((pieces,)),
        ],
        compiler_params=cheap(16),
        cost_estimate=COST,
        name="scan",
    )(scan, mains, *parts, *tables)


def join_kernel(shots, scan, carry, part, *refs):
    ends, out = refs[: shots - 1], refs[shots]
    total, zb, ny = part.shape
    shot = lax.axis_index("shot")
    first_x = shot * total
    below = jnp.zeros((zb, ny), F32)
    above = jnp.zeros((zb, ny), F32)
    for j, end in enumerate(ends, 1):
        other = shot ^ j
        term = carry[shot, other] * end[...]
        below += jnp.where(other < shot, term, 0.0)
        above += jnp.where(other > shot, term, 0.0)
    for x in range(total):
        out[x] = part[x] + scan[3, first_x + x] * below + scan[4, first_x + x] * above


def join(scan, carry, part, ends, after):
    total, zb, ny = part.shape
    shots = len(ends) + 1
    return pl.pallas_call(
        functools.partial(join_kernel, shots),
        out_shape=jax.ShapeDtypeStruct((total, zb, ny), F32),
        in_specs=[SMEM] * 2 + [VMEM] * shots + [ANY],
        out_specs=VMEM,
        compiler_params=cheap(16),
        cost_estimate=COST,
        name="join",
    )(scan, carry, part, *ends, *in_hbm((after,)))


def neighbours(count, start):
    low = range(start, count - 1, 2)
    return [(i, i + 1) for i in low] + [(i + 1, i) for i in low]


def swap(values):
    count = lax.axis_size("mp")
    return keep_held(lax.ppermute(v, "mp", neighbours(count, start)) for start, v in enumerate(values))


def flip(value, bit):
    count = lax.axis_size("shot")
    got = lax.ppermute(value, "shot", [(i, i ^ bit) for i in range(count)])
    return keep_held((got,))[0]


def share(terms, step):
    return [terms[0]] + [flip(term, step * i) for i, term in enumerate(terms[1:], 1)]


def spread(pieces, ratio):
    mp, shots = lax.axis_size("mp"), lax.axis_size("shot")
    out = []
    for k, piece in enumerate(pieces):
        pairs = []
        for m in range(mp):
            for s in range(shots):
                target = (s * ratio + m % ratio + k) % mp
                pairs.append((m * shots + s, target * shots + m // ratio))
        out.append(lax.ppermute(piece, ("mp", "shot"), pairs))
    return keep_held(out)


def per_device(
    courant, forward_old, forward_now, adjoint_late, adjoint_now,
    src_cell, src_sign, wavelet, rec_cell, rec_data,
):
    mp_count, shots = lax.axis_size("mp"), lax.axis_size("shot")
    rows, ny, nz = courant.shape
    ratio = mp_count // shots
    full_x = rows * mp_count
    band_y, band_z = band(ny), band(nz)
    bands = (jnp.asarray(band_y, BF16), jnp.asarray(np.concatenate([band_z, band_z]), BF16))
    strength = float(SMOOTH_YZ * SMOOTH_YZ)
    strength_x = float(SMOOTH_X * SMOOTH_X)
    scan, carry = scan_tables(full_x, strength_x, rows * ratio)
    kappa = 1.0
    for length, e in ((full_x, strength_x), (ny, strength), (nz, strength)):
        resp = response(length, e)
        kappa /= math.sqrt(np.mean(resp * resp))
    z_tables = split_table(filter_matrix(nz, strength))
    y_tables = split_table(kappa * filter_matrix(ny, strength))

    f_old, f_now, a_late, a_now = forward_old[0], forward_now[0], adjoint_late[0], adjoint_now[0]
    halos = swap(pick(f_now, a_now))
    c, accel, nxt, mid, a_base, src, *inner = step_one(
        src_cell, src_sign, wavelet, rec_cell, rec_data, courant, f_old, f_now, a_late, a_now, bands, shots
    )
    accel, nxt, mid, a_base, edge0, edge1 = correct(c, accel, nxt, mid, a_base, halos)
    halos = swap((edge0, edge1))
    inner = share(inner, 1)
    edge, by_f, by_a, *outer = step_two((c, accel, nxt, mid, a_base, src), bands, (), shots)
    inner, outer = add_up(inner, outer)
    outer = share(outer, 1)
    near, keep = finish(edge, by_f, by_a, halos, shots)
    raw_shape = (rows, ny // shots, nz)
    layout = [[(2 * REACH, rows - 4 * REACH)], [(REACH, REACH), (rows - 2 * REACH, REACH)]]
    terms = [[(term, 0) for term in chunk] for chunk in ((inner,), outer)]
    raw, *mains = depth(layout, terms, z_tables, raw_shape, mp_count)
    mains = gather(spread(mains, ratio), y_tables, ratio, shots)
    last, edges = depth_edge(keep, flip(near, 1), z_tables, mp_count)
    raw = raw_edge(share(last, 2), raw)
    edges = spread(edges, ratio)
    planes = [low + i for chunk in layout for low, count in chunk for i in range(count)]
    part, *ends = scan_first(jnp.asarray(scan), mains, edges, y_tables, planes, rows, shots)
    ends = [flip(end, j) for j, end in enumerate(ends, 1)]
    smooth = join(jnp.asarray(scan), jnp.asarray(carry), part, ends, raw)
    smooth = jnp.transpose(smooth, (0, 2, 1))
    return raw, smooth


def solution(mesh):
    return jax.shard_map(
        per_device,
        mesh=mesh,
        in_specs=(
            P(("parts", "mp"), None, None),
            P(("parts", "shot"), "mp", None, None),
            P(("parts", "shot"), "mp", None, None),
            P(("parts", "shot"), "mp", None, None),
            P(("parts", "shot"), "mp", None, None),
            P(("parts", "shot"), None),
            P(("parts", "shot"), None),
            P(("parts", "shot"), None, None),
            P("parts"),
            P(("parts", "shot"), None, None),
        ),
        out_specs=(P(("parts", "mp"), "shot", None), P(("parts", "shot"), None, "mp")),
        check_vma=False,
    )
```

```python
import functools
import math

import jax
import jax.numpy as jnp
import ml_dtypes
import numpy as np
from jax import lax
from jax.experimental import pallas as pl
from jax.experimental.pallas import tpu as pltpu
from jax.sharding import PartitionSpec as P

SMOOTH_X = 32
SMOOTH_YZ = 4

COEFS = (8.0 / 5.0, -1.0 / 5.0, 8.0 / 315.0, -1.0 / 560.0)
CENTER = -205.0 / 72.0
REACH = len(COEFS)
SCALE = 5040.0
WHOLE = tuple(float(round(SCALE * a)) for a in COEFS)

LANES = 128
BF16 = jnp.bfloat16
F32 = jnp.float32
ANY = pl.BlockSpec(memory_space=pl.ANY)
VMEM = pl.BlockSpec(memory_space=pltpu.VMEM)
SMEM = pl.BlockSpec(memory_space=pltpu.SMEM)


def band(length):
    table = np.zeros((length, length), np.float32)
    for k, weight in enumerate(WHOLE, 1):
        near = np.arange(length - k)
        table[near, near + k] = weight
        table[near + k, near] = weight
    return table


def response(length, strength):
    counter = np.arange(1, length + 1, dtype=np.float64)
    half_sine = np.sin(np.pi * counter / (2 * (length + 1)))
    return 1.0 / (1.0 + strength * 4.0 * half_sine * half_sine)


def filter_matrix(length, strength):
    counter = np.arange(1, length + 1, dtype=np.float64)
    table = np.sin(np.pi * counter[:, None] * counter[None, :] / (length + 1))
    return 2.0 / (length + 1) * (table * response(length, strength)[None, :]) @ table


def scan_tables(length, strength, block):
    rate = math.acosh(1.0 + 0.5 / strength)
    index = np.arange(1, length + 1, dtype=np.float64)
    rise = np.sinh(rate * index)
    fall = np.sinh(rate * (length + 1 - index))
    whole = strength * math.sinh(rate) * math.sinh(rate * (length + 1))
    diag = rise * fall / whole
    left = np.concatenate([[0.0], rise[:-1] / rise[1:]])
    right = np.concatenate([fall[1:] / fall[:-1], [0.0]])
    first = (np.arange(length) // block) * block
    last = first + block - 1
    from_left = np.where(first > 0, rise[np.maximum(first - 1, 0)], 0.0) / rise
    from_right = np.where(last + 1 < length, fall[np.minimum(last + 1, length - 1)], 0.0) / fall
    rows = np.stack([diag, left, right, diag * from_left, diag * from_right])
    blocks = length // block
    carry = np.zeros((blocks, blocks))
    for here in range(blocks):
        for there in range(blocks):
            if there < here:
                carry[here, there] = rise[there * block + block - 1] / rise[here * block - 1]
            elif there > here:
                carry[here, there] = fall[there * block] / fall[here * block + block]
    return rows.astype(np.float32), carry.astype(np.float32)


def split_table(table):
    high = table.astype(np.float32).astype(ml_dtypes.bfloat16)
    low = (table - high.astype(np.float64)).astype(np.float32).astype(ml_dtypes.bfloat16)
    return jnp.asarray(high), jnp.asarray(low)


def split(value):
    high = value.astype(BF16)
    low = (value - high.astype(F32)).astype(BF16)
    return high, low


def dot(a, b):
    return jnp.dot(a, b, preferred_element_type=F32)


def dot_t(a, b):
    return lax.dot_general(a, b, (((1,), (1,)), ((), ())), preferred_element_type=F32)


def laplace_plane(field, p, band_y, band_z):
    here = field[p]
    width = here.shape[1]
    both = jnp.concatenate(split(here), axis=1)
    along_y = dot(band_y[...], both)
    along_z = dot(both, band_z[...])
    total = (3.0 * SCALE * CENTER) * here
    for k, weight in enumerate(WHOLE, 1):
        total += weight * (field[p + k] + field[p - k])
    return total + (along_y[:, :width] + along_y[:, width:]) + along_z


def divmod_fixed(value, size):
    if size & (size - 1) == 0:
        return lax.shift_right_logical(value, size.bit_length() - 1), value & (size - 1)
    return lax.div(value, size), lax.rem(value, size)


class Copies:
    def __init__(self, sems):
        self.sems, self.used = sems, 0

    def start(self, source, target):
        copy = pltpu.make_async_copy(source, target, self.sems.at[self.used])
        self.used += 1
        copy.start()
        return copy


def wait_all(copies):
    for copy in copies:
        copy.wait()


def chunk_bounds(rows):
    step = max(2 * REACH, -(-rows // 3))
    return [(low, min(low + step, rows)) for low in range(0, rows, step)]


def put_blocks(copies, buf, planes, shot, outs):
    return [copies.start(buf.at[planes, shot ^ j], out) for j, out in enumerate(outs)]


def step_one_kernel(
    src_cell, src_sign, wavelet, rec_tile, data_tile,
    courant, f_old, f_now, a_late, a_now, band_y, band_z,
    c_buf, acc_buf, f_next, a_mid, a_base, s_second,
    *refs,
):
    terms_out = refs[:-15]
    (
        f_pad, a_pad, s_first, r_first, r_second, gt_buf,
        place_buf, value_buf, count_buf, places, values, counts, list_sems, term_sems, sems,
    ) = refs[-15:]
    rows, ny, nz = courant.shape
    copies = Copies(sems)
    bounds = chunk_bounds(rows)

    def chunks(source, target, offset=0):
        return [
            copies.start(source.at[pl.ds(low, high - low)], target.at[pl.ds(low + offset, high - low)])
            for low, high in bounds
        ]

    loads = [chunks(f_now, f_pad, REACH), chunks(courant, c_buf), chunks(f_old, f_next, REACH)]
    late_loads = [chunks(a_now, a_pad, REACH), chunks(a_late, a_mid, REACH)]
    edge = jnp.zeros((REACH, ny, nz), F32)
    for pad in (f_pad, a_pad, f_next, a_mid):
        pad[:REACH] = edge
        pad[REACH + rows :] = edge

    group = ny // 8

    def clear(p, _):
        blank = jnp.zeros((group, 8, nz), F32)
        for ref in (s_first, r_first, s_second, r_second):
            ref[pl.ds(p * group, group)] = blank
        return 0

    lax.fori_loop(0, rows, clear, 0)

    size = rows * ny * nz
    start = lax.axis_index("mp") * size
    flat = lax.broadcasted_iota(jnp.int32, (8, nz), 0) * nz + lax.broadcasted_iota(jnp.int32, (8, nz), 1)

    def put(refs, local, values):
        tile, within = divmod_fixed(local, 8 * nz)
        spot = flat == within
        for ref, value in zip(refs, values, strict=True):
            ref[tile] = ref[tile] + jnp.where(spot, value, 0.0)

    nsrc = src_cell.shape[1]

    def one_source(i, _):
        local = src_cell[0, i] - start
        mine = (local >= 0) & (local < size)
        local = jnp.where(mine, local, 0)
        sign = jnp.where(mine, (2 * src_sign[0, i] - 1).astype(F32), 0.0)
        put((s_first, s_second), local, (sign * wavelet[0, 0, i], sign * wavelet[0, 1, i]))
        return 0

    lax.fori_loop(0, nsrc, one_source, 0, unroll=8 if nsrc % 8 == 0 else 1)


    tiles = rec_tile.shape[0]
    local = rec_tile[...] - start
    inside = (local >= 0) & (local < size)
    marks = jnp.where(inside, 1.0, 0.0).astype(BF16)
    row, col = (lax.broadcasted_iota(jnp.int32, (LANES, LANES), d) for d in (0, 1))
    before = jnp.where(inside, dot(marks, jnp.where(row < col, 1.0, 0.0).astype(BF16)).astype(jnp.int32), -1)
    thirds = []
    for value in (jnp.where(inside, local, 0).astype(F32), data_tile[0], data_tile[1]):
        for _ in range(3):
            part = value.astype(BF16)
            value = value - part.astype(F32)
            thirds.append(part)
    for t in range(tiles):
        moves = jnp.where(row == before[t : t + 1], 1.0, 0.0).astype(BF16)
        stacked = jnp.concatenate([part[t : t + 1] for part in thirds] + [thirds[0][:7]], axis=0)
        moved = dot_t(stacked, moves)
        place_buf[t : t + 1] = (moved[0:1] + moved[1:2] + moved[2:3]).astype(jnp.int32)
        value_buf[0, t : t + 1] = moved[3:4] + moved[4:5] + moved[5:6]
        value_buf[1, t : t + 1] = moved[6:7] + moved[7:8] + moved[8:9]
    count_buf[...] = dot(marks, jnp.ones((LANES, LANES), BF16)).astype(jnp.int32)
    fetches = [
        pltpu.make_async_copy(source, target, list_sems.at[i])
        for i, (source, target) in enumerate(((place_buf, places), (value_buf, values), (count_buf, counts)))
    ]
    for fetch in fetches:
        fetch.start()
    wait_all(fetches)

    def receivers(t, _):
        def some(g, _):
            items = []
            for e in range(8):
                i = g * 8 + e
                items.append((places[t, i], values[0, t, i], values[1, t, i]))
            for place, first, second in items:
                put((r_first, r_second), place, (first, second))
            return 0

        return lax.fori_loop(0, lax.div(counts[t, 0] + 7, 8), some, 0)

    lax.fori_loop(0, tiles, receivers, 0)

    def forward(p, _):
        courant_here = c_buf[p] * (1.0 / SCALE)
        c_buf[p] = courant_here
        spike = s_first[pl.ds(p * group, group)].reshape(ny, nz)
        accel = courant_here * laplace_plane(f_pad, p + REACH, band_y, band_z) + spike
        acc_buf[p] = accel
        f_next[p + REACH] = (2.0 * f_pad[p + REACH] - f_next[p + REACH]) + accel
        return 0

    for group_loads in loads:
        wait_all(group_loads)
    lax.fori_loop(0, rows, forward, 0, unroll=2)

    def adjoint(p, _):
        spike = r_first[pl.ds(p * group, group)].reshape(ny, nz)
        change = c_buf[p] * laplace_plane(a_pad, p + REACH, band_y, band_z) + spike
        mid = (2.0 * a_pad[p + REACH] - a_mid[p + REACH]) + change
        a_mid[p + REACH] = mid
        later = r_second[pl.ds(p * group, group)].reshape(ny, nz)
        a_base[p] = (2.0 * mid - a_pad[p + REACH]) + later
        return 0

    for group_loads in late_loads:
        wait_all(group_loads)
    lax.fori_loop(0, rows, adjoint, 0, unroll=2)

    blocks = gt_buf.shape[1]

    def inner(i, _):
        p = i + 2 * REACH
        c = c_buf[p]
        here = pl.ds(p * group, group)
        accel = c * laplace_plane(f_next, p + REACH, band_y, band_z) + s_second[here].reshape(ny, nz)
        first = a_base[p] + c * laplace_plane(a_mid, p + REACH, band_y, band_z)
        gt_buf[i] = (first * acc_buf[p] + a_mid[p + REACH] * accel).reshape(blocks, ny // blocks, nz)
        return 0

    lax.fori_loop(0, rows - 4 * REACH, inner, 0, unroll=2)
    wait_all(put_blocks(Copies(term_sems), gt_buf, slice(None), lax.axis_index("shot"), terms_out))


def cheap(megabytes):
    return pltpu.CompilerParams(vmem_limit_bytes=megabytes * 2**20)


COST = pl.CostEstimate(flops=1000, bytes_accessed=1000, transcendentals=0)
LONG = pl.CostEstimate(flops=10**12, bytes_accessed=1000, transcendentals=0)


def held(*shape):
    return pltpu.VMEM(shape, F32)


def in_hbm(arrays):
    return [pltpu.with_memory_space_constraint(array, pltpu.HBM) for array in arrays]


def keep_held(arrays):
    return [pltpu.with_memory_space_constraint(array, pltpu.VMEM) for array in arrays]


def step_one(src_cell, src_sign, wavelet, rec_cell, rec_data, courant, f_old, f_now, a_late, a_now, bands, shots):
    rows, ny, nz = courant.shape
    term = held(rows - 4 * REACH, ny // shots, nz)
    whole, padded, sparse = (rows, ny, nz), (rows + 2 * REACH, ny, nz), (rows * ny // 8, 8, nz)
    tiles = rec_cell.shape[0] // LANES
    return pl.pallas_call(
        step_one_kernel,
        out_shape=tuple(held(*shape) for shape in (whole, whole, padded, padded, whole, sparse)) + (term,) * shots,
        in_specs=[SMEM] * 3 + [VMEM] * 2 + [ANY] * 5 + [VMEM] * 2,
        out_specs=(VMEM,) * (6 + shots),
        scratch_shapes=[
            held(*padded), held(*padded), held(*sparse), held(*sparse), held(*sparse),
            held(rows - 4 * REACH, shots, ny // shots, nz),
            pltpu.VMEM((tiles, LANES), jnp.int32),
            pltpu.VMEM((2, tiles, LANES), F32),
            pltpu.VMEM((tiles, LANES), jnp.int32),
            pltpu.SMEM((tiles, LANES), jnp.int32),
            pltpu.SMEM((2, tiles, LANES), F32),
            pltpu.SMEM((tiles, LANES), jnp.int32),
            pltpu.SemaphoreType.DMA((3,)),
            pltpu.SemaphoreType.DMA((shots,)),
            pltpu.SemaphoreType.DMA((5 * len(chunk_bounds(rows)),)),
        ],
        compiler_params=cheap(24),
        cost_estimate=LONG,
        name="step_one",
    )(
        src_cell, src_sign, wavelet, rec_cell.reshape(-1, LANES), rec_data.reshape(2, -1, LANES),
        *in_hbm((courant, f_old, f_now, a_late, a_now)), *bands,
    )


def sides(rows):
    even = lax.rem(lax.axis_index("mp"), 2) == 0
    high = rows - REACH
    return (jnp.where(even, high, 0), even), (jnp.where(even, 0, high), jnp.logical_not(even))


STRIP = 32


def halo_sums(halo, upper):
    planes = [halo(jnp.where(upper, h, REACH - 1 - h)) for h in range(REACH)]
    return [sum(WHOLE[h + REACH - q - 1] * planes[h] for h in range(q + 1)) for q in range(REACH)]


def strips(count, body):
    def step(i, _):
        body(pl.ds(pl.multiple_of(i * STRIP, STRIP), STRIP))
        return 0

    lax.fori_loop(0, count // STRIP, step, 0)


def pick_kernel(f_now, a_now, out0, out1, buf, sems):
    copies = Copies(sems)
    loads = [
        (copies.start(field.at[pl.ds(base, REACH)], buf.at[s, i]), s, i)
        for s, (base, _) in enumerate(sides(f_now.shape[0]))
        for i, field in enumerate((f_now, a_now))
    ]
    stores = []
    for load, s, i in loads:
        load.wait()
        stores.append(copies.start(buf.at[s, i], (out0, out1)[s].at[i]))
    wait_all(stores)


def pick(f_now, a_now):
    _, ny, nz = f_now.shape
    both = held(2, REACH, ny, nz)
    return pl.pallas_call(
        pick_kernel,
        out_shape=(both, both),
        in_specs=[ANY] * 2,
        out_specs=(ANY,) * 2,
        scratch_shapes=[held(2, 2, REACH, ny, nz), pltpu.SemaphoreType.DMA((8,))],
        compiler_params=cheap(8),
        cost_estimate=COST,
        name="pick",
    )(*in_hbm((f_now, a_now)))


def correct_kernel(
    c_buf, acc_in, next_in, mid_in, base_in, halo0, halo1, acc_buf, f_next, a_mid, a_base, edge0, edge1,
    halo_buf, edge_buf, sems,
):
    rows, ny, _ = c_buf.shape
    copies = Copies(sems)
    step = max(STRIP, ny // 4)
    parts = [slice(low, low + step) for low in range(0, ny, step)]
    loads = [
        [copies.start(halo.at[:, :, part], halo_buf.at[s, :, :, part]) for s, halo in enumerate((halo0, halo1))]
        for part in parts
    ]

    def strip(i, _):
        part = pl.ds(pl.multiple_of(i * STRIP, STRIP), STRIP)
        for s, (base, upper) in enumerate(sides(rows)):
            forward = halo_sums(lambda h, s=s: halo_buf[s, 0, h, part], upper)
            adjoint = halo_sums(lambda h, s=s: halo_buf[s, 1, h, part], upper)
            for q in range(REACH):
                place = jnp.where(upper, q, REACH - 1 - q)
                here = base + place
                c = c_buf[here, part]
                change = c * forward[q]
                acc_buf[here, part] = acc_in[here, part] + change
                value = next_in[here + REACH, part] + change
                f_next[here + REACH, part] = value
                edge_buf[s, 0, place, part] = value
                change = c * adjoint[q]
                value = mid_in[here + REACH, part] + change
                a_mid[here + REACH, part] = value
                edge_buf[s, 1, place, part] = value
                a_base[here, part] = base_in[here, part] + 2.0 * change
        return 0

    stores = []
    for part, group in zip(parts, loads, strict=True):
        wait_all(group)
        lax.fori_loop(part.start // STRIP, part.stop // STRIP, strip, 0)
        for s, edge in enumerate((edge0, edge1)):
            stores.append(copies.start(edge_buf.at[s, :, :, part], edge.at[:, :, part]))
    wait_all(stores)


def correct(c, accel, nxt, mid, a_base, halos):
    rows, ny, nz = c.shape
    both = held(2, REACH, ny, nz)
    return pl.pallas_call(
        correct_kernel,
        out_shape=tuple(held(*array.shape) for array in (accel, nxt, mid, a_base)) + (both, both),
        in_specs=[VMEM] * 5 + [ANY] * 2,
        out_specs=(VMEM,) * 4 + (ANY,) * 2,
        scratch_shapes=[
            held(2, 2, REACH, ny, nz), held(2, 2, REACH, ny, nz),
            pltpu.SemaphoreType.DMA((4 * len(range(0, ny, max(STRIP, ny // 4))),)),
        ],
        input_output_aliases={1: 0, 2: 1, 3: 2, 4: 3},
        compiler_params=cheap(8),
        cost_estimate=COST,
        name="correct",
    )(*keep_held((c, accel, nxt, mid, a_base)), *halos)


def step_two_kernel(waits, c_buf, acc_buf, f_next, a_mid, a_base, s_buf, band_y, band_z, *refs):
    edge_out, by_f, by_a, *terms_out, gt_buf, sems = refs[waits:]
    rows, ny, nz = c_buf.shape
    copies = Copies(sems)
    group = ny // 8
    blocks = gt_buf.shape[1]

    def plane(p, _):
        c = c_buf[p]
        here = pl.ds(p * group, group)
        mid = a_mid[p + REACH]
        accel = c * laplace_plane(f_next, p + REACH, band_y, band_z) + s_buf[here].reshape(ny, nz)
        first = a_base[p] + c * laplace_plane(a_mid, p + REACH, band_y, band_z)
        gt_buf[p] = (first * acc_buf[p] + mid * accel).reshape(blocks, ny // blocks, nz)
        return 0

    def inner(i, _):
        return plane(jnp.where(i < REACH, i + REACH, i + rows - 3 * REACH), 0)

    lax.fori_loop(0, 2 * REACH, inner, 0, unroll=2)
    stores = []
    for i, low in enumerate((REACH, rows - 2 * REACH)):
        outs = [out.at[pl.ds(i * REACH, REACH)] for out in terms_out]
        stores += put_blocks(copies, gt_buf, pl.ds(low, REACH), lax.axis_index("shot"), outs)

    bases = [base for base, _ in sides(rows)]

    def outer(i, _):
        s, q = lax.div(i, REACH), lax.rem(i, REACH)
        p = jnp.where(s == 0, bases[0], bases[1]) + q
        plane(p, 0)
        c = c_buf[p]
        by_f[s, q] = c * a_mid[p + REACH]
        by_a[s, q] = c * acc_buf[p]
        edge_out[s, q] = gt_buf[p].reshape(ny, nz)
        return 0

    lax.fori_loop(0, 2 * REACH, outer, 0, unroll=2)
    wait_all(stores)


def step_two(arrays, bands, after, shots):
    rows, ny, nz = arrays[0].shape
    edge = held(2, REACH, ny, nz)
    term = held(2 * REACH, ny // shots, nz)
    return pl.pallas_call(
        functools.partial(step_two_kernel, len(after)),
        out_shape=(edge, edge, edge) + (term,) * shots,
        in_specs=[VMEM] * (8 + len(after)),
        out_specs=(VMEM,) * (3 + shots),
        scratch_shapes=[held(rows, shots, ny // shots, nz), pltpu.SemaphoreType.DMA((2 * shots,))],
        compiler_params=cheap(12),
        cost_estimate=LONG,
        name="step_two",
    )(*keep_held(arrays), *bands, *after)


def add_up_kernel(shots, *refs):
    terms, out = refs[:shots], refs[2 * shots]
    total = terms[0][...]
    for term in terms[1:]:
        total += term[...]
    out[...] = total


def add_up(terms, passed):
    shots = len(terms)
    outs = pl.pallas_call(
        functools.partial(add_up_kernel, shots),
        out_shape=tuple(held(*array.shape) for array in (terms[0], *passed)),
        in_specs=[VMEM] * shots + [ANY] * shots,
        out_specs=(VMEM,) + (ANY,) * shots,
        input_output_aliases={shots + i: 1 + i for i in range(shots)},
        compiler_params=cheap(8),
        cost_estimate=COST,
        name="add_up",
    )(*keep_held((*terms, *passed)))
    return outs[0], outs[1:]


def finish_kernel(edge, by_f, by_a, halo0, halo1, near_out, keep_out, halo_buf, near_buf, sems):
    _, blocks, yb, _ = near_out.shape
    copies = Copies(sems)
    bit = lax.rem(lax.axis_index("shot"), 2)
    width = math.gcd(yb, STRIP)
    jobs = []
    for out, mine in ((near_buf, 1 - bit), (keep_out, bit)):
        for j in range(blocks):
            low = pl.multiple_of((2 * j + mine) * yb, yb)
            here = pl.ds(low, yb)
            loads = [
                copies.start(halo.at[:, :, here], halo_buf.at[s, :, :, here]) for s, halo in enumerate((halo0, halo1))
            ]
            jobs.append((out, j, low, loads))
    stores = []
    for out, j, low, loads in jobs:
        wait_all(loads)

        def strip(i, _, out=out, j=j, low=low):
            inside = pl.ds(pl.multiple_of(i * width, width), width)
            part = pl.ds(pl.multiple_of(low + i * width, width), width)
            for s, (_, upper) in enumerate(sides(2 * REACH)):
                forward = halo_sums(lambda h, s=s: halo_buf[s, 0, h, part], upper)
                adjoint = halo_sums(lambda h, s=s: halo_buf[s, 1, h, part], upper)
                for q in range(REACH):
                    place = jnp.where(upper, q, REACH - 1 - q)
                    total = edge[s, place, part] + by_f[s, place, part] * forward[q]
                    out[s * REACH + place, j, inside] = total + by_a[s, place, part] * adjoint[q]
            return 0

        lax.fori_loop(0, yb // width, strip, 0)
        if out is near_buf:
            stores.append(copies.start(near_buf.at[:, j], near_out.at[:, j]))
    wait_all(stores)


def finish(edge, by_f, by_a, halos, shots):
    _, reach, ny, nz = edge.shape
    half = held(2 * reach, shots // 2, ny // shots, nz)
    return pl.pallas_call(
        finish_kernel,
        out_shape=(half, half),
        in_specs=[VMEM] * 3 + [ANY] * 2,
        out_specs=(ANY, VMEM),
        scratch_shapes=[
            held(2, 2, reach, ny, nz),
            held(*half.shape),
            pltpu.SemaphoreType.DMA((shots * 2 + shots // 2,)),
        ],
        compiler_params=cheap(16),
        cost_estimate=LONG,
        name="finish",
    )(edge, by_f, by_a, *halos)


def depth_kernel(layout, parts, pieces, *refs):
    used = sum(len(offsets) for offsets in parts)
    terms, refs = refs[:used], refs[used:]
    z_high, z_low = refs[:2]
    raw_out, outs, (raw_buf, spectrum, sems) = refs[-pieces - 4], refs[-pieces - 3 : -3], refs[-3:]
    planes, yb, nz = raw_buf.shape
    shots = lax.axis_size("shot")
    copies = Copies(sems)
    low, at = 0, 0
    for chunk, offsets in zip(layout, parts, strict=True):
        size = sum(count for _, count in chunk)
        total = None
        for offset in offsets:
            term = terms[at][offset : offset + size]
            total = term if total is None else total + term
            at += 1
        raw_buf[low : low + size] = total / shots
        low += size
    stores, done = [], 0
    rows = raw_out.shape[0]
    for chunk in layout:
        for where, count in chunk:
            base = sides(rows)[where][0] if isinstance(where, bool) else where
            stores.append(copies.start(raw_buf.at[pl.ds(done, count)], raw_out.at[pl.ds(base, count)]))
            done += count
    lanes = LANES // yb
    count = planes // lanes
    zb = nz // pieces

    def turn(p, _):
        rows_here = jnp.concatenate([raw_buf[h * count + p] for h in range(lanes)], axis=0)
        high, low_part = split(rows_here)
        table = z_high[...]
        spectrum[p] = (dot_t(table, high) + dot_t(table, low_part) + dot_t(z_low[...], high)).reshape(pieces, zb, LANES)
        return 0

    lax.fori_loop(0, count, turn, 0, unroll=2)
    offset = piece_offset()
    for k, out in enumerate(outs):
        out[...] = spectrum[:, lax.rem(offset + k, pieces)]
    wait_all(stores)


def depth(layout, terms, tables, raw_shape, pieces, after=(), previous=None):
    planes = sum(count for chunk in layout for _, count in chunk)
    _, yb, nz = raw_shape
    lanes = LANES // yb
    count = planes // lanes
    piece = held(count, nz // pieces, LANES)
    extra = (*after, *(() if previous is None else (previous,)))
    flat = [term for chunk in terms for term, _ in chunk]
    offsets = [[offset for _, offset in chunk] for chunk in terms]
    last = len(flat) + 2 + len(extra) - 1
    return pl.pallas_call(
        functools.partial(depth_kernel, layout, offsets, pieces),
        out_shape=(jax.ShapeDtypeStruct(raw_shape, F32),) + (piece,) * pieces,
        in_specs=[VMEM] * (len(flat) + 2) + [ANY] * len(extra),
        out_specs=(ANY,) + (VMEM,) * pieces,
        scratch_shapes=[
            pltpu.VMEM((planes, yb, nz), F32),
            pltpu.VMEM((count, pieces, nz // pieces, LANES), F32),
            pltpu.SemaphoreType.DMA((sum(len(chunk) for chunk in layout),)),
        ],
        input_output_aliases={} if previous is None else {last: 0},
        compiler_params=cheap(16),
        cost_estimate=LONG,
        name="depth",
    )(*flat, *tables, *extra)


def piece_offset():
    ratio = lax.axis_size("mp") // lax.axis_size("shot")
    return lax.axis_index("shot") * ratio + lax.rem(lax.axis_index("mp"), ratio)


def depth_edge_kernel(pieces, keep, near, z_high, z_low, own, *refs):
    far, outs, (total, spectrum) = refs[: -pieces - 2], refs[-pieces - 2 : -2], refs[-2:]
    planes, blocks, yb, nz = keep.shape
    total[...] = (keep[...] + near[...]) / lax.axis_size("shot")
    for i, term in enumerate((own, *far)):
        term[...] = total[:, lax.div(lax.axis_index("shot") ^ (2 * i), 2)]

    def turn(p, _):
        high, low = split(total[p].reshape(blocks * yb, nz))
        table = z_high[...]
        both = dot_t(table, high) + dot_t(table, low) + dot_t(z_low[...], high)
        spectrum[p] = both.reshape(pieces, nz // pieces, blocks * yb)
        return 0

    lax.fori_loop(0, planes, turn, 0, unroll=2)
    for k, out in enumerate(outs):
        out[...] = spectrum[:, lax.rem(piece_offset() + k, pieces)]


def depth_edge(keep, near, tables, pieces):
    planes, blocks, yb, nz = keep.shape
    term = held(planes, yb, nz)
    piece = held(planes, nz // pieces, blocks * yb)
    outs = pl.pallas_call(
        functools.partial(depth_edge_kernel, pieces),
        out_shape=(term,) * blocks + (piece,) * pieces,
        in_specs=[VMEM] * 4,
        out_specs=(VMEM,) * (blocks + pieces),
        scratch_shapes=[
            pltpu.VMEM(keep.shape, F32),
            pltpu.VMEM((planes, pieces, nz // pieces, blocks * yb), F32),
        ],
        compiler_params=cheap(12),
        cost_estimate=LONG,
        name="depth_edge",
    )(keep, near, *tables)
    return outs[:blocks], outs[blocks:]


def raw_edge_kernel(*refs):
    terms, (raw_out, buf, sems) = refs[:-4], refs[-3:]
    total = terms[0][...]
    for term in terms[1:]:
        total += term[...]
    buf[...] = total
    copies = Copies(sems)
    wait_all([
        copies.start(buf.at[pl.ds(s * REACH, REACH)], raw_out.at[pl.ds(base, REACH)])
        for s, (base, _) in enumerate(sides(raw_out.shape[0]))
    ])


def raw_edge(terms, raw):
    return pl.pallas_call(
        raw_edge_kernel,
        out_shape=jax.ShapeDtypeStruct(raw.shape, F32),
        in_specs=[VMEM] * len(terms) + [ANY],
        out_specs=ANY,
        scratch_shapes=[pltpu.VMEM(terms[0].shape, F32), pltpu.SemaphoreType.DMA((2,))],
        input_output_aliases={len(terms): 0},
        compiler_params=cheap(8),
        cost_estimate=COST,
        name="raw_edge",
    )(*terms, raw)


def gather_planes(ratio, shots, parts, buf, field, sems):
    pieces = len(parts)
    mp = lax.axis_index("mp")
    copies = Copies(sems)
    loads = []
    for k, part in enumerate(parts):
        q = lax.rem(mp - k + pieces, pieces)
        loads.append(copies.start(part, buf.at[lax.rem(q, ratio), lax.div(q, ratio)]))
    wait_all(loads)
    count = buf.shape[2]
    _, zb, ny = field.shape
    yb = ny // shots
    lanes = LANES // yb
    slot_of = lax.broadcasted_iota(jnp.int32, (zb, LANES), 1) // yb
    for sub in range(ratio):
        for p in range(count):
            for h in range(lanes):
                x = sub * count * lanes + h * count + p
                for t in range(shots // lanes):
                    value = None
                    for e in range(lanes):
                        piece = buf[sub, t * lanes + e, p]
                        if e != h:
                            piece = pltpu.roll(piece, (e - h) * yb % LANES, 1)
                        value = piece if value is None else jnp.where(slot_of == e, piece, value)
                    field[x, :, pl.ds(t * LANES, LANES)] = value


def gather_halves(ratio, shots, parts, buf, field, sems):
    pieces = len(parts)
    copies = Copies(sems)
    loads = []
    for k, part in enumerate(parts):
        q = lax.rem(lax.axis_index("mp") - k + pieces, pieces)
        loads.append(copies.start(part, buf.at[lax.rem(q, ratio), lax.div(q, ratio)]))
    wait_all(loads)
    _, _, count, zb, half = buf.shape
    ny = field.shape[2]
    yb = ny // shots
    lanes = LANES // yb
    slot_of = lax.broadcasted_iota(jnp.int32, (zb, LANES), 1) // yb
    for sub in range(ratio):
        for p in range(count):
            cores = [sum(buf[sub, s, p] for s in range(core, shots, 2)) for core in (0, 1)]
            for t in range(ny // LANES):
                value = None
                for e in range(lanes):
                    core, place = (t * lanes + e) % 2, (t * lanes + e) // 2
                    low = place // lanes * LANES
                    piece = cores[core][:, low : low + LANES]
                    if e != place % lanes:
                        piece = pltpu.roll(piece, (e - place % lanes) * yb % LANES, 1)
                    value = piece if value is None else jnp.where(slot_of == e, piece, value)
                field[sub * count + p, :, pl.ds(t * LANES, LANES)] = value


def gather_kernel(ratio, shots, *refs):
    parts, (y_high, y_low, out, buf, field, sems) = refs[:-6], refs[-6:]
    gather_planes(ratio, shots, parts, buf, field, sems)
    filter_second(field, out, y_high[...], y_low[...])


def filter_second(field, out, high_t, low_t):
    total, zb, ny = field.shape
    step = max(1, 256 // zb)
    while total % step:
        step -= 1
    for i in range(0, total, step):
        high, low = split(field[i : i + step].reshape(step * zb, ny))
        result = dot_t(high, high_t) + dot_t(low, high_t) + dot_t(high, low_t)
        out[i : i + step] = result.reshape(step, zb, ny)


def gather(parts, tables, ratio, shots):
    pieces = len(parts)
    count, zb, _ = parts[0].shape
    ny = tables[0].shape[0]
    total = ratio * count * (LANES * shots // ny)
    return pl.pallas_call(
        functools.partial(gather_kernel, ratio, shots),
        out_shape=held(total, zb, ny),
        in_specs=[VMEM] * (pieces + 2),
        out_specs=VMEM,
        scratch_shapes=[
            pltpu.VMEM((ratio, shots, count, zb, LANES), F32),
            pltpu.VMEM((total, zb, ny), F32),
            pltpu.SemaphoreType.DMA((pieces,)),
        ],
        compiler_params=cheap(16),
        cost_estimate=LONG,
        name="gather",
    )(*parts, *tables)


def scan_kernel(planes, rows, ratio, shots, scan, mains, *refs):
    refs, (buf, field, edges, ends, sems) = refs[:-5], refs[-5:]
    parts, (y_high, y_low, out), sends = refs[: -shots - 2], refs[-shots - 2 : -shots + 1], refs[-shots + 1 :]
    gather_halves(ratio, shots, parts, buf, edges, sems)
    filter_second(edges, edges, y_high[...], y_low[...])
    shot = lax.axis_index("shot")
    total, zb, ny = field.shape
    per_slab = len(planes)
    for sub in range(ratio):
        for i, x in enumerate(planes):
            field[sub * rows + x] = mains[sub * per_slab + i]
        even = lax.rem(shot * ratio + sub, 2) == 0
        for s, base in enumerate((jnp.where(even, rows - REACH, 0), jnp.where(even, 0, rows - REACH))):
            for q in range(REACH):
                field[sub * rows + base + q] = edges[sub * 2 * REACH + s * REACH + q]
    first_x = shot * total

    def up(x, carry):
        carry = field[x] + scan[1, first_x + x] * carry
        out[x] = carry
        return carry

    ends[0] = lax.fori_loop(0, total, up, jnp.zeros((zb, ny), F32))

    def down(i, carry):
        x = total - 1 - i
        out[x] = (out[x] + carry) * scan[0, first_x + x]
        return scan[2, first_x + x - 1] * (field[x] + carry)

    carry = lax.fori_loop(0, total - 1, down, jnp.zeros((zb, ny), F32))
    out[0] = (out[0] + carry) * scan[0, first_x]
    ends[1] = field[0] + carry
    for j, send in enumerate(sends, 1):
        send[...] = jnp.where((shot ^ j) > shot, ends[0], ends[1])


def scan_first(scan, mains, parts, tables, planes, rows, shots):
    per_slab = len(planes)
    ratio = mains.shape[0] // per_slab
    _, zb, ny = mains.shape
    end = held(zb, ny)
    total = rows * ratio
    pieces, count = len(parts), parts[0].shape[0]
    return pl.pallas_call(
        functools.partial(scan_kernel, planes, rows, ratio, shots),
        out_shape=(held(total, zb, ny),) + (end,) * (shots - 1),
        in_specs=[SMEM] + [VMEM] * (pieces + 3),
        out_specs=(VMEM,) * shots,
        scratch_shapes=[
            pltpu.VMEM((ratio, shots, count, zb, ny // 2), F32),
            pltpu.VMEM((total, zb, ny), F32),
            pltpu.VMEM((2 * REACH * ratio, zb, ny), F32),
            pltpu.VMEM((2, zb, ny), F32),
            pltpu.SemaphoreType.DMA((pieces,)),
        ],
        compiler_params=cheap(16),
        cost_estimate=COST,
        name="scan",
    )(scan, mains, *parts, *tables)


def join_kernel(shots, scan, carry, part, *refs):
    ends, out = refs[: shots - 1], refs[shots]
    total, zb, ny = part.shape
    shot = lax.axis_index("shot")
    first_x = shot * total
    below = jnp.zeros((zb, ny), F32)
    above = jnp.zeros((zb, ny), F32)
    for j, end in enumerate(ends, 1):
        other = shot ^ j
        term = carry[shot, other] * end[...]
        below += jnp.where(other < shot, term, 0.0)
        above += jnp.where(other > shot, term, 0.0)
    for x in range(total):
        out[x] = part[x] + scan[3, first_x + x] * below + scan[4, first_x + x] * above


def join(scan, carry, part, ends, after):
    total, zb, ny = part.shape
    shots = len(ends) + 1
    return pl.pallas_call(
        functools.partial(join_kernel, shots),
        out_shape=jax.ShapeDtypeStruct((total, zb, ny), F32),
        in_specs=[SMEM] * 2 + [VMEM] * shots + [ANY],
        out_specs=VMEM,
        compiler_params=cheap(16),
        cost_estimate=COST,
        name="join",
    )(scan, carry, part, *ends, *in_hbm((after,)))


def neighbours(count, start):
    low = range(start, count - 1, 2)
    return [(i, i + 1) for i in low] + [(i + 1, i) for i in low]


def swap(values):
    count = lax.axis_size("mp")
    return keep_held(lax.ppermute(v, "mp", neighbours(count, start)) for start, v in enumerate(values))


def flip(value, bit):
    count = lax.axis_size("shot")
    got = lax.ppermute(value, "shot", [(i, i ^ bit) for i in range(count)])
    return keep_held((got,))[0]


def share(terms, step):
    return [terms[0]] + [flip(term, step * i) for i, term in enumerate(terms[1:], 1)]


def spread(pieces, ratio):
    mp, shots = lax.axis_size("mp"), lax.axis_size("shot")
    out = []
    for k, piece in enumerate(pieces):
        pairs = []
        for m in range(mp):
            for s in range(shots):
                target = (s * ratio + m % ratio + k) % mp
                pairs.append((m * shots + s, target * shots + m // ratio))
        out.append(lax.ppermute(piece, ("mp", "shot"), pairs))
    return keep_held(out)


def per_device(
    courant, forward_old, forward_now, adjoint_late, adjoint_now,
    src_cell, src_sign, wavelet, rec_cell, rec_data,
):
    mp_count, shots = lax.axis_size("mp"), lax.axis_size("shot")
    rows, ny, nz = courant.shape
    ratio = mp_count // shots
    full_x = rows * mp_count
    band_y, band_z = band(ny), band(nz)
    bands = (jnp.asarray(band_y, BF16), jnp.asarray(np.concatenate([band_z, band_z]), BF16))
    strength = float(SMOOTH_YZ * SMOOTH_YZ)
    strength_x = float(SMOOTH_X * SMOOTH_X)
    scan, carry = scan_tables(full_x, strength_x, rows * ratio)
    kappa = 1.0
    for length, e in ((full_x, strength_x), (ny, strength), (nz, strength)):
        resp = response(length, e)
        kappa /= math.sqrt(np.mean(resp * resp))
    z_tables = split_table(filter_matrix(nz, strength))
    y_tables = split_table(kappa * filter_matrix(ny, strength))

    f_old, f_now, a_late, a_now = forward_old[0], forward_now[0], adjoint_late[0], adjoint_now[0]
    halos = swap(pick(f_now, a_now))
    c, accel, nxt, mid, a_base, src, *inner = step_one(
        src_cell, src_sign, wavelet, rec_cell, rec_data, courant, f_old, f_now, a_late, a_now, bands, shots
    )
    accel, nxt, mid, a_base, edge0, edge1 = correct(c, accel, nxt, mid, a_base, halos)
    halos = swap((edge0, edge1))
    inner = share(inner, 1)
    edge, by_f, by_a, *outer = step_two((c, accel, nxt, mid, a_base, src), bands, (), shots)
    inner, outer = add_up(inner, outer)
    outer = share(outer, 1)
    near, keep = finish(edge, by_f, by_a, halos, shots)
    raw_shape = (rows, ny // shots, nz)
    layout = [[(2 * REACH, rows - 4 * REACH)], [(REACH, REACH), (rows - 2 * REACH, REACH)]]
    terms = [[(term, 0) for term in chunk] for chunk in ((inner,), outer)]
    raw, *mains = depth(layout, terms, z_tables, raw_shape, mp_count)
    mains = gather(spread(mains, ratio), y_tables, ratio, shots)
    last, edges = depth_edge(keep, flip(near, 1), z_tables, mp_count)
    raw = raw_edge(share(last, 2), raw)
    edges = spread(edges, ratio)
    planes = [low + i for chunk in layout for low, count in chunk for i in range(count)]
    part, *ends = scan_first(jnp.asarray(scan), mains, edges, y_tables, planes, rows, shots)
    ends = [flip(end, j) for j, end in enumerate(ends, 1)]
    smooth = join(jnp.asarray(scan), jnp.asarray(carry), part, ends, raw)
    smooth = jnp.transpose(smooth, (0, 2, 1))
    return raw, smooth


def solution(mesh):
    return jax.shard_map(
        per_device,
        mesh=mesh,
        in_specs=(
            P(("parts", "mp"), None, None),
            P(("parts", "shot"), "mp", None, None),
            P(("parts", "shot"), "mp", None, None),
            P(("parts", "shot"), "mp", None, None),
            P(("parts", "shot"), "mp", None, None),
            P(("parts", "shot"), None),
            P(("parts", "shot"), None),
            P(("parts", "shot"), None, None),
            P("parts"),
            P(("parts", "shot"), None, None),
        ),
        out_specs=(P(("parts", "mp"), "shot", None), P(("parts", "shot"), None, "mp")),
        check_vma=False,
    )
```
